32 devices in a mesh: dp: 8 (over z, y), head: 4 (over x, core).
Axes of the slice: x: 2, y: 2, z: 4, core: 2. Of those that a mesh axis runs over, the one named last changes fastest.
Arguments:
- tokens: bfloat16 [8192, 768], P(('dp', 'head'))
- w_qkv: bfloat16 [768, 2304], replicated
- w_out: bfloat16 [768, 768], replicated, may hold values from -0.21875 to 0.21875
- w_up: bfloat16 [768, 3072], replicated, may hold values from -0.21875 to 0.21875
- w_down: bfloat16 [3072, 768], replicated, may hold values from -0.109375 to 0.109375
- norm_gains: float32 [2, 768], replicated, may hold values from 0.5 to 1.5
- norm_shifts: float32 [2, 768], replicated, may hold values from -1.8 to 1.8
- conv_kernels: bfloat16 [12, 33], replicated, may hold values from -1 to 1
- seq_lengths: int32 [8], P('dp'), may hold values from 256 to 1024, as said below
- seg_bounds: int32 [8, 65], P('dp'), may hold values from 0 to 1024, as said below
- out_grad: bfloat16 [8192, 768], P(('dp', 'head')), may hold values from -6 to 6
Outputs:
- output: bfloat16 [8192, 768], P(('dp', 'head'))
- input_grad: bfloat16 [8192, 768], P(('dp', 'head'))
- grad_qkv: float32 [768, 2304], P('dp', 'head')
- grad_out: float32 [768, 768], P('dp', 'head')
- grad_up: float32 [768, 3072], P('dp', 'head')
- grad_down: float32 [3072, 768], P('dp', 'head')
- grad_gains: float32 [2, 768], replicated
- grad_shifts: float32 [2, 768], replicated
- grad_kernels: float32 [12, 33], replicated
The draws below stay inside these ranges and needn't reach their ends.
Inputs may be any that keep to these rules, and one draw needn't show every extreme that they name: `seq_lengths`: some sequence has 1024 tokens and some has 256. `seg_bounds`: each row starts at 0, ends at the sequence's length and rises, every segment holding at least 2 positions.
All inputs are finite; a program needn't handle non-finite values.
Results may differ from the reference program's by a relative error of at most 0.01.
Values may be sent and summed in bfloat16 or wider, within the bound.
A program may use at most 192 MiB of HBM per device.

```python
import jax
import jax.numpy as jnp
from jax import lax

D = 768
HEADS = 12
HD = 64
FF = 3072
LANDMARKS = 64
KERNEL = 33
NEWTON = 6
SLOT = 1024
SEQ_GRP = 1
SEQUENCES = 8
TOKENS = 8192
N_DP = 8


def layout_draw(key):
    base_key = jax.random.fold_in(key, 41)
    length_key, jitter_key = jax.random.split(base_key)
    seq_index = jnp.arange(SEQUENCES, dtype=jnp.int32)
    lengths = jax.random.randint(length_key, (SEQUENCES,), SLOT // 4, SLOT + 1, dtype=jnp.int32)
    lengths = jnp.where(seq_index == 0, SLOT, jnp.where(seq_index == 1, SLOT // 4, lengths))
    spread_cells = SLOT // (16 * LANDMARKS)
    mark_index = jnp.arange(LANDMARKS + 1, dtype=jnp.int32)
    nominal = mark_index[None, :] * lengths[:, None] // LANDMARKS
    jitter = jax.random.randint(jitter_key, (SEQUENCES, LANDMARKS + 1), -spread_cells, spread_cells + 1, dtype=jnp.int32)
    interior = (mark_index > 0) & (mark_index < LANDMARKS)
    bounds = nominal + jnp.where(interior[None, :], jitter, 0)
    return (lengths.astype(jnp.int32), bounds.astype(jnp.int32))


def draw_seq_lengths(key, part):
    return layout_draw(key)[0]


def draw_seg_bounds(key, part):
    return layout_draw(key)[1]


def draw_tokens(key, part):
    noise_key, block_key = jax.random.split(jax.random.fold_in(key, 3))
    noise = jax.random.normal(noise_key, (TOKENS, D), jnp.float32)
    blocks = jax.random.normal(block_key, (TOKENS // 32, D), jnp.float32)
    return (0.6 * noise + 0.8 * jnp.repeat(blocks, 32, axis=0)).astype(jnp.bfloat16)


def draw_w_qkv(key, part):
    first_key, second_key, third_key = jax.random.split(jax.random.fold_in(key, 5), 3)
    scaling = D ** (-0.5)
    shared = jax.random.normal(first_key, (D, HEADS * HD), jnp.float32)
    own_part = jax.random.normal(second_key, (D, HEADS * HD), jnp.float32)
    value_part = jax.random.normal(third_key, (D, HEADS * HD), jnp.float32)
    query_cols = shared * scaling
    key_cols = (0.8 * shared + 0.6 * own_part) * scaling
    value_cols = value_part * scaling
    return jnp.concatenate([query_cols, key_cols, value_cols], axis=1).astype(jnp.bfloat16)


def level_of(key, shape, shards, least, high):
    def one(axis_at, blocks):
        draws = jax.random.uniform(jax.random.fold_in(jax.random.fold_in(key, 6), axis_at), (blocks,), jnp.float32, least / len(shards), high / len(shards))
        return jnp.repeat(jnp.exp(draws), shape[axis_at] // blocks).reshape((-1,) + (1,) * (len(shape) - axis_at - 1))

    level = one(*shards[0])
    for cut in shards[1:]:
        level = level * one(*cut)
    return level


def scatter_about(stream_key, extent, width, bound, cuts=(), held_as=jnp.bfloat16):
    level = level_of(stream_key, extent, cuts, -0.22, 0.18) if cuts else 1.0
    array = jax.random.normal(stream_key, extent, jnp.float32) * width * level
    return jnp.minimum(jnp.maximum(array, -bound), bound).astype(held_as)


def setup_inputs(seed: int = 0) -> dict:
    arg_keys = jax.random.split(jax.random.key(seed), 12)
    return {
        "tokens": draw_tokens(jax.random.fold_in(arg_keys[11], 71), 0),
        "w_qkv": draw_w_qkv(jax.random.fold_in(arg_keys[11], 71), 0),
        "w_out": scatter_about(arg_keys[2], (D, D), D ** -0.5, 0.21875),
        "w_up": scatter_about(arg_keys[3], (D, FF), D ** -0.5, 0.21875),
        "w_down": scatter_about(arg_keys[4], (FF, D), FF ** -0.5, 0.109375),
        "norm_gains": jnp.clip(1.0 + 0.1 * jax.random.normal(arg_keys[5], (2, D), jnp.float32), 0.5, 1.5),
        "norm_shifts": scatter_about(arg_keys[6], (2, D), 0.3, 1.8, (), jnp.float32),
        "conv_kernels": scatter_about(arg_keys[7], (HEADS, KERNEL), KERNEL ** -0.5, 1.0),
        "seq_lengths": draw_seq_lengths(jax.random.fold_in(arg_keys[11], 71), 0),
        "seg_bounds": draw_seg_bounds(jax.random.fold_in(arg_keys[11], 71), 0),
        "out_grad": scatter_about(arg_keys[10], (TOKENS, D), 1.0, 6.0, ((0, 32),)),
    }


highest = lax.Precision.HIGHEST
epsilon = 1e-05

@jax.custom_vjp
def low(v):
    return lax.optimization_barrier(v.astype(jnp.bfloat16)).astype(jnp.float32)

@jax.custom_vjp
def low_back(v):
    return v

def low_keep(v):
    return (low(v), None)

def low_pass(kept, grad):
    return (grad,)

def back_keep(v):
    return (v, None)

def back_low(kept, grad):
    return (low(grad),)
low.defvjp(low_keep, low_pass)
low_back.defvjp(back_keep, back_low)

def layer_norm(values, gain, shift):
    center = lax.optimization_barrier(jnp.mean(values, axis=-1, keepdims=True))
    centred = values - center
    spread_sq = lax.optimization_barrier(jnp.mean(centred * centred, axis=-1, keepdims=True))
    return centred * lax.rsqrt(spread_sq + epsilon) * gain + shift

def exact_gelu(values):
    return jax.nn.gelu(values, approximate=False)

def shifted_conv(values, kernel):
    slot_len = values.shape[0]
    taps = kernel.shape[0]
    half_width = taps // 2
    padded = jnp.pad(values, ((half_width, half_width), (0, 0)))
    total = jnp.zeros_like(values)
    for offset in range(taps):
        total = total + kernel[offset] * padded[offset:offset + slot_len]
    return total

def nystrom_head(queries, keys, values, kernel, length, bounds):
    slot_len = queries.shape[0]
    mark_count = bounds.shape[0] - 1
    head_dim = queries.shape[1]
    places = jnp.arange(slot_len, dtype=jnp.int32)
    valid = places < length
    weight_mask = valid.astype(jnp.float32)[:, None]
    scaling = head_dim ** (-0.25)
    queries = queries * weight_mask * scaling
    keys = keys * weight_mask * scaling
    values = values * weight_mask
    member = ((places[None, :] >= bounds[:-1, None]) & (places[None, :] < bounds[1:, None])).astype(jnp.float32)
    counts = (bounds[1:] - bounds[:-1]).astype(jnp.float32)[:, None]
    query_marks = jnp.dot(member, queries, precision=highest) / counts
    key_marks = jnp.dot(member, keys, precision=highest) / counts
    first = jax.nn.softmax(jnp.dot(queries, key_marks.T, precision=highest), axis=-1)
    middle = jax.nn.softmax(jnp.dot(query_marks, key_marks.T, precision=highest), axis=-1)
    third_scores = jnp.dot(query_marks, keys.T, precision=highest)
    third = jax.nn.softmax(jnp.where(valid[None, :], third_scores, -1000000000.0), axis=-1)
    inverse = middle.T / (jnp.max(lax.optimization_barrier(jnp.sum(middle, axis=0))) * jnp.max(lax.optimization_barrier(jnp.sum(middle, axis=1))))
    identity = jnp.eye(mark_count, dtype=jnp.float32)
    for _ in range(NEWTON):
        product = jnp.dot(middle, inverse, precision=highest)
        inner = 7.0 * identity - product
        inner = 15.0 * identity - jnp.dot(product, inner, precision=highest)
        inner = 13.0 * identity - jnp.dot(product, inner, precision=highest)
        inverse = 0.25 * jnp.dot(inverse, inner, precision=highest)
    summary = jnp.dot(third, values, precision=highest)
    mixed = jnp.dot(first, jnp.dot(inverse, summary, precision=highest), precision=highest)
    return (mixed + shifted_conv(values, kernel)) * weight_mask

def attend(packed, kernels, lengths, bounds):
    seq_count = lengths.shape[0]
    head_count = kernels.shape[0]
    head_dim = packed.shape[-1] // (3 * head_count)
    grouped = packed.reshape(seq_count, -1, 3, head_count, head_dim)
    over_heads = jax.vmap(nystrom_head, in_axes=(1, 1, 1, 0, None, None), out_axes=1)
    over_seqs = jax.vmap(over_heads, in_axes=(0, 0, 0, None, 0, 0))
    result = over_seqs(grouped[:, :, 0], grouped[:, :, 1], grouped[:, :, 2], kernels, lengths, bounds)
    return result.reshape(seq_count * grouped.shape[1], head_count * head_dim)

def layer(inputs, lengths, bounds, w_qkv, w_out, w_up, w_down, gains, shifts, kernels):
    projected = low(low_back(jnp.dot(inputs, w_qkv, precision=highest)))
    attended = low(low_back(attend(projected, kernels, lengths, bounds)))
    branch = low_back(jnp.dot(attended, w_out, precision=highest))
    first_norm = layer_norm(inputs + branch, gains[0], shifts[0])
    hidden = low_back(jnp.dot(low(first_norm), w_up, precision=highest))
    activated = low(exact_gelu(hidden))
    second = low_back(jnp.dot(activated, w_down, precision=highest))
    return layer_norm(first_norm + second, gains[1], shifts[1])

def reference(tokens, w_qkv, w_out, w_up, w_down, norm_gains, norm_shifts, conv_kernels, seq_lengths, seg_bounds, out_grad):
    group_rows = SEQ_GRP * SLOT

    def forward(inputs, wq, wo, wu, wd, gains, shifts, kernels):

        def one_group(pieces):
            return layer(pieces[0], pieces[1], pieces[2], wq, wo, wu, wd, gains, shifts, kernels)
        grouped = (inputs.reshape(N_DP, group_rows, D), seq_lengths.reshape(N_DP, SEQ_GRP), seg_bounds.reshape(N_DP, SEQ_GRP, LANDMARKS + 1))
        return lax.map(jax.checkpoint(one_group), grouped).reshape(N_DP * group_rows, D)
    floats = (tokens.astype(jnp.float32), w_qkv.astype(jnp.float32), w_out.astype(jnp.float32), w_up.astype(jnp.float32), w_down.astype(jnp.float32), norm_gains.astype(jnp.float32), norm_shifts.astype(jnp.float32), conv_kernels.astype(jnp.float32))
    output, pullback = jax.vjp(forward, *floats)
    places = jnp.arange(SLOT, dtype=jnp.int32)
    live = (places[None, :] < seq_lengths[:, None]).astype(jnp.float32).reshape(-1, 1)
    grads = pullback(out_grad.astype(jnp.float32) * live)
    return (output.astype(jnp.bfloat16), grads[0].astype(jnp.bfloat16), grads[1], grads[2], grads[3], grads[4], grads[5], grads[6], grads[7])
```

```python
import functools
import jax
import jax.numpy as jnp
from jax import lax
from jax.sharding import PartitionSpec as P
from jax.experimental import pallas as pl
from jax.experimental.pallas import tpu as pltpu

MESH = pl.DeviceIdType.MESH
NEWTON = 6
F32 = jnp.float32
BF16 = jnp.bfloat16
HIGHEST = lax.Precision.HIGHEST
VMEM = pltpu.VMEM


def mm(a, b, ca, cb, precision=None):
    return lax.dot_general(
        a, b, (((ca,), (cb,)), ((), ())), precision=precision, preferred_element_type=F32
    )


def halves(value):
    high = value.astype(BF16)
    low = (value - high.astype(F32)).astype(BF16)
    return high, low


def left(value):
    high, low = halves(value)
    return jnp.concatenate([high, high, low], axis=1)


def right(value):
    high, low = halves(value)
    return jnp.concatenate([high, low, high], axis=0)


def fine(a, b):
    return mm(left(a), right(b), 1, 0)


def eye(size):
    rows = lax.broadcasted_iota(jnp.int32, (size, size), 0)
    cols = lax.broadcasted_iota(jnp.int32, (size, size), 1)
    return (rows == cols).astype(F32)


def toeplitz(base):
    rows = jnp.broadcast_to(base, (128, base.shape[1]))
    return pltpu.roll(rows, 0, 1, stride=1, stride_axis=0).astype(BF16)


def windows(mat):
    zero = jnp.zeros((mat.shape[0], 128), mat.dtype)
    wide = jnp.concatenate([zero, mat, zero], axis=1)
    count = mat.shape[1] // 128
    return jnp.concatenate([wide[:, 128 * b : 128 * b + 384] for b in range(count)], axis=0)


def unwindow(stacked, rows):
    count = stacked.shape[0] // rows
    return jnp.concatenate([stacked[rows * b : rows * (b + 1)] for b in range(count)], axis=1)


def members(bnd_ref, slot):
    place = lax.broadcasted_iota(jnp.int32, (bnd_ref.shape[0], slot), 1)
    inside = (place >= bnd_ref[:, 0:1]) & (place < bnd_ref[:, 1:2])
    return inside.astype(F32).astype(BF16)


def copy_to(src, dst, sems, index, device):
    return pltpu.make_async_remote_copy(
        src_ref=src,
        dst_ref=dst,
        send_sem=sems.at[0, index],
        recv_sem=sems.at[1, index],
        device_id=device,
        device_id_type=MESH,
    )


def greet(devices):
    barrier = pltpu.get_barrier_semaphore()
    for device in devices:
        pl.semaphore_signal(barrier, inc=1, device_id=device, device_id_type=MESH)
    pl.semaphore_wait(barrier, len(devices))


def forward_kernel(
    tok_ref, wq_hbm, kb_ref, bnd_ref, cnt_ref, len_ref,
    heads_ref, all_ref, packed_ref, a1_ref, a3_ref, n1_ref, n2_ref, marks_ref,
    wfull, wt, att, wsem, sems,
):
    dp = lax.axis_index("dp")
    me = lax.axis_index("head")
    quarters = lax.axis_size("head")
    rows, width = tok_ref.shape
    slot = rows * quarters
    head_width = att.shape[0]
    count = bnd_ref.shape[0]
    dim = 64
    nh = head_width // dim
    fetch = pltpu.make_async_copy(wq_hbm, wfull, wsem)
    fetch.start()
    peers = [(dp, me ^ k) for k in range(1, quarters)]
    greet(peers)
    half = rows // 2
    near = copy_to(tok_ref, all_ref.at[me], sems, 0, (dp, me ^ 1))
    near.start()
    far = []
    for piece in range(2):
        part = pl.ds(piece * half, half)
        sent = copy_to(tok_ref.at[part], all_ref.at[me, part], sems, 1 + piece, (dp, me ^ 2))
        sent.start()
        far.append(sent)
    all_ref[me] = tok_ref[...]
    fetch.wait()
    odd = lax.rem(me, 2)
    for part in range(3):
        start = pl.multiple_of(part * width + 384 * lax.div(me, 2) + 128 * odd, 128)
        window = wfull[:, pl.ds(start, 256)]
        wt[part] = window.T
    w_own = [wt[part, pl.ds(pl.multiple_of(64 * odd, 64), head_width), :] for part in range(3)]
    w_own = jnp.concatenate(w_own, axis=0)

    def project(block):
        lanes = pl.ds(pl.multiple_of(rows * block, rows), rows)
        packed_ref[:, lanes] = mm(w_own, all_ref[block], 1, 1).astype(BF16)

    project(me)
    near.wait()
    project(me ^ 1)
    onward = []
    for piece in range(2):
        part = pl.ds(piece * half, half)
        far[piece].wait()
        sent = copy_to(
            all_ref.at[me ^ 2, part], all_ref.at[me ^ 2, part], sems, 3 + piece, (dp, me ^ 1)
        )
        sent.start()
        onward.append(sent)
    project(me ^ 2)
    for sent in onward:
        sent.wait()
    project(me ^ 3)

    scale = dim ** (-0.25)
    member = members(bnd_ref, slot)
    means = mm(packed_ref[: 2 * head_width], member, 1, 1) * (scale / cnt_ref[...])
    length = len_ref[...]
    live = lax.broadcasted_iota(jnp.int32, (1, slot), 1) < length
    unit = eye(count)
    state = []
    for head in range(nh):
        q_marks_t = means[dim * head : dim * (head + 1)]
        k_marks_t = means[head_width + dim * head : head_width + dim * (head + 1)]
        q_marks = q_marks_t.T
        k_marks = k_marks_t.T
        marks_ref[head, 0] = q_marks
        marks_ref[head, 1] = k_marks
        scores = fine(q_marks, k_marks_t)
        powers = jnp.exp(scores - jnp.max(scores, axis=1, keepdims=True))
        middle = powers / jnp.sum(powers, axis=1, keepdims=True)
        marks_ref[head, 2] = middle
        cols = jnp.max(jnp.sum(middle, axis=0, keepdims=True), axis=1, keepdims=True)
        sums = jnp.max(jnp.sum(middle, axis=1, keepdims=True), axis=0, keepdims=True)
        inverse = middle.T / (cols * sums)
        product = fine(middle, inverse)
        state.append((inverse, product))

    def newton(step, carry):
        out = []
        for head in range(nh):
            inverse, product = carry[head]
            spread = left(product)
            second = mm(spread, right(product), 1, 0)
            third = mm(spread, right(second), 1, 0)
            n1_ref[head, step] = jnp.concatenate([product, second], axis=1)
            n2_ref[head, step] = jnp.concatenate([third, inverse], axis=1)
            blend = 0.25 * (13.0 * unit - 15.0 * product + 7.0 * second - third)
            both = mm(jnp.concatenate([left(inverse), spread], axis=0), right(blend), 1, 0)
            out.append((both[:count], both[count:]))
        return tuple(out)

    state = lax.fori_loop(0, NEWTON, newton, tuple(state))
    for head in range(nh):
        at = dim * head
        queries = packed_ref[at : at + dim]
        keys = packed_ref[head_width + at : head_width + at + dim]
        values = packed_ref[2 * head_width + at : 2 * head_width + at + dim]
        values = jnp.where(live, values.astype(F32), 0.0).astype(BF16)
        k_high, k_low = halves(marks_ref[head, 1] * scale)
        scores = mm(
            jnp.concatenate([k_high, k_low], axis=1),
            jnp.concatenate([queries, queries], axis=0), 1, 0,
        )
        powers = jnp.exp(scores - jnp.max(scores, axis=0, keepdims=True))
        first = powers * (1.0 / jnp.sum(powers, axis=0, keepdims=True))
        a1_ref[head] = first
        q_high, q_low = halves(marks_ref[head, 0] * scale)
        scores = mm(
            jnp.concatenate([q_high, q_low], axis=1),
            jnp.concatenate([keys, keys], axis=0), 1, 0,
        )
        scores = jnp.where(live, scores, -1e9)
        powers = jnp.exp(scores - jnp.max(scores, axis=1, keepdims=True))
        third = powers * (1.0 / jnp.sum(powers, axis=1, keepdims=True))
        a3_ref[head] = third
        t_high, t_low = halves(third)
        summary = mm(jnp.concatenate([t_high, t_low], axis=0), values, 1, 1)
        summary = summary[:count] + summary[count:]
        weights = fine(state[head][0], summary)
        marks_ref[head, 3] = summary
        marks_ref[head, 4] = weights
        marks_ref[head, 5] = state[head][0]
        w_high, w_low = halves(weights.T)
        f_high, f_low = halves(first)
        mixed = mm(
            jnp.concatenate([w_high, w_high, w_low], axis=1),
            jnp.concatenate([f_high, f_low, f_high], axis=0), 1, 0,
        )
        band = toeplitz(kb_ref[head, 0:1])
        conv = unwindow(mm(windows(values), band, 1, 1), dim)
        att[at : at + dim] = jnp.where(live, mixed + conv, 0.0).astype(BF16)
    done = []
    for k in range(1, quarters):
        lanes = pl.ds(pl.multiple_of(rows * (me ^ k), rows), rows)
        sent = copy_to(att.at[:, lanes], heads_ref.at[me], sems, 4 + k, (dp, me ^ k))
        sent.start()
        done.append(sent)
    heads_ref[me] = att[:, pl.ds(pl.multiple_of(rows * me, rows), rows)]
    for sent in done:
        sent.wait()


def forward_call(tokens, w_qkv, kernel_rows, bounds_two, counts, length, quarters):
    rows, width = tokens.shape
    nh = kernel_rows.shape[0]
    head_width = nh * 64
    slot = rows * quarters
    count = bounds_two.shape[0]
    whole = pl.BlockSpec(memory_space=VMEM)
    return pl.pallas_call(
        forward_kernel,
        out_shape=(
            jax.ShapeDtypeStruct((quarters, head_width, rows), BF16),
            jax.ShapeDtypeStruct((quarters, rows, width), BF16),
            jax.ShapeDtypeStruct((3 * head_width, slot), BF16),
            jax.ShapeDtypeStruct((nh, count, slot), F32),
            jax.ShapeDtypeStruct((nh, count, slot), F32),
            jax.ShapeDtypeStruct((nh, NEWTON, count, 2 * count), F32),
            jax.ShapeDtypeStruct((nh, NEWTON, count, 2 * count), F32),
            jax.ShapeDtypeStruct((nh, 6, count, 64), F32),
        ),
        in_specs=[whole, pl.BlockSpec(memory_space=pl.ANY), whole, whole, whole, whole],
        out_specs=[whole] * 8,
        scratch_shapes=[
            VMEM(w_qkv.shape, BF16),
            VMEM((3, 256, width), BF16),
            VMEM((head_width, slot), BF16),
            pltpu.SemaphoreType.DMA,
            pltpu.SemaphoreType.DMA((2, 8)),
        ],
        compiler_params=pltpu.CompilerParams(
            collective_id=0, has_side_effects=True, vmem_limit_bytes=48 * 2**20
        ),
    )(tokens, w_qkv, kernel_rows, bounds_two, counts, length)


def small_inputs(conv_kernels, seq_lengths, seg_bounds, quarter, local):
    taps = conv_kernels.shape[1]
    mine = lax.dynamic_slice_in_dim(conv_kernels.astype(F32), quarter * local, local, 0)
    both = jnp.stack([mine, mine[:, ::-1]], axis=1)
    kernel_rows = jnp.pad(both, ((0, 0), (0, 0), (112, 384 - 112 - taps)))
    low, high = seg_bounds[0, :-1], seg_bounds[0, 1:]
    bounds_two = jnp.stack([low, high], axis=1)
    counts = (high - low).astype(F32)[None, :]
    return kernel_rows, bounds_two, counts, seq_lengths.reshape(1, 1)


def gelu_pair(hidden):
    tail = jnp.exp(-0.5 * hidden * hidden)
    t = 1.0 / (1.0 + 0.23164190 * jnp.abs(hidden))
    poly = 1.330274429
    for term in (-1.821255978, 1.781477937, -0.356563782, 0.319381530):
        poly = poly * t + term
    density = 0.3989422804014327 * tail
    below = density * poly * t
    normal = jnp.where(hidden >= 0.0, 1.0 - below, below)
    return hidden * normal, normal + hidden * density


def norm_forward(values):
    center = jnp.mean(values, axis=-1, keepdims=True)
    centred = values - center
    spread = jnp.mean(centred * centred, axis=-1, keepdims=True)
    root = lax.rsqrt(spread + 1e-5)
    return centred * root, root


def norm_backward(grad, gain, normed, root):
    scaled = grad * gain
    center = jnp.mean(scaled, axis=-1, keepdims=True)
    along = jnp.mean(scaled * normed, axis=-1, keepdims=True)
    return root * (scaled - center - normed * along)


class Spread:
    def __init__(self, acc, got, bits, sems, base):
        self.acc, self.got, self.bits, self.sems, self.base = acc, got, bits, sems, base
        self.blocks = acc.shape[0]
        self.stage = 0
        self.offset = 0
        self.at = 0
        self.flight = None
        self.sent = []

    def start(self):
        bit, device = self.bits[self.stage]
        size = self.blocks >> (self.stage + 1)
        self.keep = self.offset + bit * size
        other = self.offset + (1 - bit) * size
        self.flight = copy_to(
            self.acc.at[pl.ds(other, size)], self.got.at[pl.ds(self.at, size)],
            self.sems, self.base + self.stage, device,
        )
        self.flight.start()
        self.size = size

    def take(self):
        self.flight.wait_recv()
        self.sent.append(self.flight)
        mine, new = pl.ds(self.keep, self.size), pl.ds(self.at, self.size)
        self.at += self.size
        self.offset = self.keep
        self.stage += 1
        if self.stage == len(self.bits):
            return self.acc[mine].astype(F32) + self.got[new].astype(F32)
        self.acc[mine] = self.acc[mine] + self.got[new]
        return None

    def step(self):
        self.take()
        self.start()

    def finish(self):
        total = self.take()
        for sent in self.sent:
            sent.wait_send()
        return total[0]


def position(order, values):
    spot = 0
    for name in order:
        spot = 2 * spot + values[name]
    return spot


DOWN_ORDERS = (("x", "y", "l", "h"), ("y", "x", "l", "h"), ("l", "x", "y", "h"))
UP_ORDERS = (("y", "x", "l", "h"), ("l", "y", "x", "h"), ("x", "y", "l", "h"))
OUT_ORDER = ("l", "x", "y", "h")
QKV_ORDERS = (("y", "l", "h"), ("l", "y", "h"), ("y", "l", "h"))


def backward_kernel(
    tok_ref, grad_ref, gain_ref, shift_ref, heads_ref, all_ref, packed_ref, a1_ref, a3_ref,
    n1_ref, n2_ref, marks_ref, kb_ref, bnd_ref, cnt_ref, len_ref,
    wout_hbm, wup_hbm, wdown_hbm, wqkv_hbm,
    out_ref, in_ref, gqkv_ref, gout_ref, gup_ref, gdown_ref, small_ref,
    w_out, w_up, w_down, w_qkv, wsem, sems,
    heads_x, low_t, low_x, act, gst, gst_x, slope, gh, gh_x, gb, gb_x, gatt, g_in, gproj, gp_in,
    first_ref, norm1_ref, gr1_ref, sum_s, sum_r, fin,
    acc_down, got_down, acc_up, got_up, acc_out, got_out, acc_qkv, got_qkv,
):
    dp = lax.axis_index("dp")
    me = lax.axis_index("head")
    quarters = 4
    rows, width = tok_ref.shape
    slot = rows * quarters
    hidden_width = w_up.shape[1]
    block = hidden_width // quarters
    head_width = width // quarters
    dim = 64
    nh = head_width // dim
    count = bnd_ref.shape[0]
    band_rows = width // 8
    down_cols = hidden_width // 8
    core = lax.rem(me, 2)
    mate = (dp, me ^ 1)
    bits = {
        "x": (lax.div(me, 2), (dp, me ^ 2)),
        "y": (lax.rem(dp, 2), (dp ^ 1, me)),
        "l": (lax.rem(lax.div(dp, 2), 2), (dp ^ 2, me)),
        "h": (lax.div(dp, 4), (dp ^ 4, me)),
    }
    fetches = []
    for i, (src, dst) in enumerate(
        ((wout_hbm, w_out), (wup_hbm, w_up), (wdown_hbm, w_down), (wqkv_hbm, w_qkv))
    ):
        fetch = pltpu.make_async_copy(src, dst, wsem.at[i])
        fetch.start()
        fetches.append(fetch)
    greet([(dp, me ^ k) for k in (1, 2, 3)] + [(dp ^ k, me) for k in (1, 2, 4)])
    counter = iter(range(200))

    def send(src, dst, device):
        copy = copy_to(src, dst, sems, next(counter), device)
        copy.start()
        return copy

    def reserve(n):
        base = next(counter)
        for _ in range(n - 1):
            next(counter)
        return base

    def spread(acc, got, order):
        return Spread(acc, got, [bits[name] for name in order], sems, reserve(len(order)))

    heads_sent = send(heads_ref, heads_x, mate)
    length = len_ref[...]
    fetches[0].wait()
    branch = mm(heads_ref[...], w_out[...], 0, 0)
    normed, root_one = norm_forward(tok_ref[...].astype(F32) + branch)
    norm1_ref[...] = normed
    first = normed * gain_ref[0:1] + shift_ref[0:1]
    first_ref[...] = first
    low = first.astype(BF16)
    low_t[...] = low.T
    low_sent = send(low_t, low_x, mate)
    fetches[1].wait()
    fetches[2].wait()
    second = None
    act_sent = []
    for i in range(quarters):
        cols = slice(block * i, block * (i + 1))
        active, slope_part = gelu_pair(mm(low, w_up[:, cols], 1, 0))
        active = active.astype(BF16)
        act[:rows, cols] = active
        act_sent.append(send(act.at[:rows, cols], act.at[rows:, cols], mate))
        slope[:, cols] = slope_part
        part = mm(active, w_down[cols, :], 1, 0)
        second = part if second is None else second + part
    normed_two, root_two = norm_forward(first_ref[...] + second)
    out_ref[...] = (normed_two * gain_ref[1:2] + shift_ref[1:2]).astype(BF16)
    place = me * rows + lax.broadcasted_iota(jnp.int32, (rows, 1), 0)
    cotangent = jnp.where(place < length, grad_ref[...].astype(F32), 0.0)
    sum_s[0] = jnp.zeros(sum_s.shape[1:], F32)
    sum_s[0, 1:2] = jnp.sum(cotangent * normed_two, axis=0, keepdims=True)
    sum_s[0, 3:4] = jnp.sum(cotangent, axis=0, keepdims=True)
    g_two = norm_backward(cotangent, gain_ref[1:2], normed_two, root_two)
    gr1_ref[...] = g_two
    g_low = g_two.astype(BF16)
    gst[...] = g_low.T
    gst_sent = send(gst, gst_x, mate)
    for copy in act_sent:
        copy.wait()
    gst_sent.wait()
    lead = jnp.concatenate(
        [
            jnp.concatenate(
                [
                    ref[pl.ds(pl.multiple_of(head_width * (2 * x + core), 64), head_width), :]
                    for ref in (gst, gst_x)
                ],
                axis=1,
            )
            for x in range(2)
        ],
        axis=0,
    )
    for pair in range(4):
        total = mm(lead, act[:, 2 * down_cols * pair : 2 * down_cols * (pair + 1)], 1, 0)
        total = total.astype(BF16)
        for x in range(2):
            for inner in range(2):
                values = {"x": x, "y": inner, "l": pair % 2, "h": pair // 2}
                for q in range(3):
                    top = head_width * x + 64 * q
                    acc_down[q, position(DOWN_ORDERS[q], values)] = total[
                        top : top + 64, down_cols * inner : down_cols * (inner + 1)
                    ]
    downs = [spread(acc_down.at[q], got_down.at[q], DOWN_ORDERS[q]) for q in range(3)]
    for chunk in downs:
        chunk.start()
    g_first = gr1_ref[...]
    gh_sent = []
    for i in range(quarters):
        cols = slice(block * i, block * (i + 1))
        part = (slope[:, cols] * mm(g_low, w_down[cols, :], 1, 1)).astype(BF16)
        gh[:, cols] = part
        g_first = g_first + mm(part, w_up[:, cols], 1, 1)
        if i % 2:
            lanes = pl.ds(pl.multiple_of(block * (i - core), 128), block)
            gh_sent.append(send(gh.at[:, lanes], gh_x.at[i // 2], mate))
    normed = norm1_ref[...]
    sum_s[0, 0:1] = jnp.sum(g_first * normed, axis=0, keepdims=True)
    sum_s[0, 2:3] = jnp.sum(g_first, axis=0, keepdims=True)
    g_one = norm_backward(g_first, gain_ref[0:1], normed, root_one)
    gr1_ref[...] = g_one
    g_branch = g_one.astype(BF16)
    gb[...] = g_branch
    gb_sent = send(gb, gb_x, mate)
    gatt[...] = mm(w_out[...], g_branch, 1, 1).astype(BF16)
    g_sent = []
    mine = pl.ds(pl.multiple_of(rows * me, rows), rows)
    for k in range(1, quarters):
        src = gatt.at[pl.ds(pl.multiple_of(head_width * (me ^ k), 64), head_width)]
        g_sent.append(send(src, g_in.at[:, mine], (dp, me ^ k)))
    g_in[:, mine] = gatt[pl.ds(pl.multiple_of(head_width * me, 64), head_width)]
    heads_sent.wait()
    low_sent.wait()
    for copy in gh_sent:
        copy.wait()
    gb_sent.wait()
    lead = jnp.concatenate([low_t[...], low_x[...]], axis=1)
    for x in range(2):
        for q in range(3):
            lanes = pl.ds(pl.multiple_of(block * (2 * x + core) + 256 * q, 128), 256)
            side = jnp.concatenate([gh[:, lanes], gh_x[x, :, 256 * q : 256 * (q + 1)]], axis=0)
            total = mm(lead, side, 1, 0).astype(BF16)
            for d in range(8):
                values = {"x": x, "y": d % 2, "l": d // 2 % 2, "h": d // 4}
                acc_up[q, position(UP_ORDERS[q], values)] = total[
                    band_rows * d : band_rows * (d + 1)
                ]
    ups = [spread(acc_up.at[q], got_up.at[q], UP_ORDERS[q]) for q in range(3)]
    for chunk in ups:
        chunk.start()
    lead = jnp.concatenate([heads_ref[...], heads_x[...]], axis=1)
    both = jnp.concatenate([gb[...], gb_x[...]], axis=0)
    for x in range(2):
        left_cols = both[:, 2 * head_width * x : 2 * head_width * x + head_width]
        right_cols = both[:, 2 * head_width * x + head_width : 2 * head_width * (x + 1)]
        total = mm(lead, jnp.where(core == 0, left_cols, right_cols), 1, 0).astype(BF16)
        for d in range(8):
            values = {"x": x, "y": d % 2, "l": d // 2 % 2, "h": d // 4}
            acc_out[position(OUT_ORDER, values)] = total[band_rows * d : band_rows * (d + 1)]
    outs = spread(acc_out, got_out, OUT_ORDER)
    outs.start()
    tokens_t = all_ref[...].T
    for copy in g_sent:
        copy.wait()
    scale = dim ** (-0.25)
    live = lax.broadcasted_iota(jnp.int32, (1, slot), 1) < length
    member = members(bnd_ref, slot)
    unit = eye(count)
    flip_rows = lax.broadcasted_iota(jnp.int32, (128, 128), 0)
    flip_cols = lax.broadcasted_iota(jnp.int32, (128, 128), 1)
    flip = (flip_rows + flip_cols == 127).astype(F32).astype(BF16)
    starts = []
    kept = []
    for head in range(nh):
        at = dim * head
        grad = jnp.where(live, g_in[at : at + dim].astype(F32), 0.0).astype(BF16)
        values = packed_ref[2 * head_width + at : 2 * head_width + at + dim]
        values = jnp.where(live, values.astype(F32), 0.0).astype(BF16)
        first = a1_ref[head]
        third = a3_ref[head]
        summary, inverse = marks_ref[head, 3], marks_ref[head, 5]
        f_high, f_low = halves(first)
        g_weights = mm(jnp.concatenate([f_high, f_low], axis=0), grad, 1, 1)
        g_weights = g_weights[:count] + g_weights[count:]
        starts.append((fine(g_weights, summary.T), jnp.zeros((count, count), F32)))
        g_summary = fine(inverse.T, g_weights)
        gt_high, gt_low = halves(g_summary.T)
        t_high, t_low = halves(third)
        g_values = mm(
            jnp.concatenate([gt_high, gt_high, gt_low], axis=1),
            jnp.concatenate([t_high, t_low, t_high], axis=0), 1, 0,
        )
        g_wide = windows(grad)
        g_values = g_values + unwindow(mm(g_wide, toeplitz(kb_ref[head, 1:2]), 1, 1), dim)
        gproj[2 * head_width + at : 2 * head_width + at + dim] = jnp.where(
            live, g_values, 0.0
        ).astype(BF16)
        turned = mm(g_wide[:, 128:256], flip, 1, 0).astype(BF16)
        gram = mm(turned, windows(values), 0, 0)
        gram = pltpu.roll(gram, 384 - 127, 1, stride=1, stride_axis=0)
        taps = pltpu.roll(jnp.sum(gram, axis=0, keepdims=True), 384 - 112, 1)
        lane = lax.broadcasted_iota(jnp.int32, taps.shape, 1)
        sum_s[0, pl.ds(4 + nh * me + head, 1), 0:384] = jnp.where(lane < 33, taps, 0.0)
        kept.append((grad, values, g_summary))
    p_sent = []

    def share(part):
        for k in range(1, quarters):
            lanes = pl.ds(pl.multiple_of(rows * (me ^ k), rows), rows)
            src = gproj.at[head_width * part : head_width * (part + 1), lanes]
            dst = gp_in.at[
                pl.ds(pl.multiple_of(width * part + head_width * me, 64), head_width)
            ]
            p_sent.append(send(src, dst, (dp, me ^ k)))
        gp_in[pl.ds(pl.multiple_of(width * part + head_width * me, 64), head_width)] = gproj[
            head_width * part : head_width * (part + 1), mine
        ]

    projs = [spread(acc_qkv.at[j], got_qkv.at[j], QKV_ORDERS[j]) for j in range(3)]

    def qkv_gradient(part):
        total = mm(tokens_t, gproj[head_width * part : head_width * (part + 1)], 1, 1)
        total = total.astype(BF16)
        for d in range(8):
            values = {"y": d % 2, "l": d // 2 % 2, "h": d // 4}
            acc_qkv[part, position(QKV_ORDERS[part], values)] = total[
                band_rows * d : band_rows * (d + 1)
            ]
        projs[part].start()

    share(2)
    qkv_gradient(2)
    sums = []
    for k, name in enumerate(("c", "x", "y", "l", "h")):
        sums.append((mate if name == "c" else bits[name][1]))
    sum_base = reserve(5)

    def sum_start(k):
        copy = copy_to(sum_s.at[k], sum_r.at[k], sems, sum_base + k, sums[k])
        copy.start()
        return copy

    def sum_step(k, copy):
        copy.wait()
        total = sum_s[k] + sum_r[k]
        if k == 4:
            small_ref[...] = total
            return None
        sum_s[k + 1] = total
        return sum_start(k + 1)

    pending = sum_start(0)
    for chunk in downs:
        chunk.step()

    def newton(index, carry):
        step = NEWTON - 1 - index
        out = []
        for head in range(nh):
            outer, hold = carry[head]
            pair_one, pair_two = n1_ref[head, step], n2_ref[head, step]
            product, second = pair_one[:, :count], pair_one[:, count:]
            third, inverse = pair_two[:, :count], pair_two[:, count:]
            blend = 0.25 * (13.0 * unit - 15.0 * product + 7.0 * second - third)
            left_p, left_s = left(product), left(second)
            inner = fine(inverse.T, outer)
            by_hold = mm(jnp.concatenate([left_p, left_s, left(third)], axis=0), right(hold), 1, 0)
            by_inner = mm(jnp.concatenate([left_p, left_s], axis=0), right(inner), 1, 0)
            zero_th = inner + by_hold[:count]
            once = by_inner[:count] + by_hold[count : 2 * count]
            twice = by_inner[count:] + by_hold[2 * count :]
            both = mm(jnp.concatenate([left(outer), left(hold)], axis=0), right(blend), 1, 0)
            rest = fine(zero_th, 7.0 * product - second - 15.0 * unit)
            rest = rest + fine(once, 7.0 * unit - product) - twice
            out.append((both[:count], both[count:] + 0.25 * rest))
        return tuple(out)

    ends = lax.fori_loop(0, NEWTON, newton, tuple(starts))
    pending = sum_step(0, pending)
    for chunk in downs:
        chunk.step()
    for chunk in ups:
        chunk.step()
    outs.step()
    for head in range(nh):
        at = dim * head
        grad, values, g_summary = kept[head]
        q_marks, k_marks, middle = marks_ref[head, 0], marks_ref[head, 1], marks_ref[head, 2]
        weights = marks_ref[head, 4]
        queries = packed_ref[at : at + dim]
        keys = packed_ref[head_width + at : head_width + at + dim]
        first = a1_ref[head]
        third = a3_ref[head]
        w_high, w_low = halves(weights)
        g_first_a = mm(
            jnp.concatenate([w_high, w_low], axis=1), jnp.concatenate([grad, grad], axis=0), 1, 0
        )
        g_one_s = first * (g_first_a - jnp.sum(g_first_a * first, axis=0, keepdims=True))
        s_high, s_low = halves(g_summary)
        g_third = mm(
            jnp.concatenate([s_high, s_low], axis=1),
            jnp.concatenate([values, values], axis=0), 1, 0,
        )
        g_three_s = third * (g_third - jnp.sum(g_third * third, axis=1, keepdims=True))
        one_high, one_low = halves(g_one_s)
        three_high, three_low = halves(g_three_s)
        g_k_marks = mm(jnp.concatenate([one_high, one_low], axis=0), queries, 1, 1)
        g_k_marks = (g_k_marks[:count] + g_k_marks[count:]) * scale
        g_q_marks = mm(jnp.concatenate([three_high, three_low], axis=0), keys, 1, 1)
        g_q_marks = (g_q_marks[:count] + g_q_marks[count:]) * scale
        outer, hold = ends[head]
        inverse = n2_ref[head, 0][:, count:]
        col_sums = jnp.sum(middle, axis=0, keepdims=True)
        row_sums = jnp.sum(middle, axis=1, keepdims=True)
        col_top = jnp.max(col_sums, axis=1, keepdims=True)
        row_top = jnp.max(row_sums, axis=0, keepdims=True)
        g_start = outer + fine(middle.T, hold)
        g_norm = -jnp.sum(
            jnp.sum(g_start * inverse, axis=1, keepdims=True), axis=0, keepdims=True
        ) / (col_top * row_top)
        col_hit = (col_sums == col_top).astype(F32)
        row_hit = (row_sums == row_top).astype(F32)
        col_hit = col_hit / jnp.sum(col_hit, axis=1, keepdims=True)
        row_hit = row_hit / jnp.sum(row_hit, axis=0, keepdims=True)
        g_middle = fine(hold, inverse.T) + g_start.T / (col_top * row_top)
        g_middle = g_middle + g_norm * (row_top * col_hit + col_top * row_hit)
        g_two_s = middle * (g_middle - jnp.sum(g_middle * middle, axis=1, keepdims=True))
        g_q_marks = g_q_marks + fine(g_two_s, k_marks)
        g_k_marks = g_k_marks + fine(g_two_s.T, q_marks)
        share_of = 1.0 / cnt_ref[...]
        for base, marks, g_marks, high in (
            (at, k_marks, g_q_marks, one_high),
            (head_width + at, q_marks, g_k_marks, three_high),
        ):
            m_high, m_low = halves(marks.T)
            l_high, l_low = halves(g_marks.T * share_of)
            total = mm(
                jnp.concatenate([m_high, m_low, l_high, l_low], axis=1),
                jnp.concatenate([high, high, member, member], axis=0), 1, 0,
            )
            gproj[base : base + dim] = (total * scale).astype(BF16)
    share(0)
    share(1)
    qkv_gradient(0)
    qkv_gradient(1)
    pending = sum_step(1, pending)
    for chunk in ups:
        chunk.step()
    outs.step()
    for chunk in downs:
        chunk.step()
    projs[2].step()
    fetches[3].wait()
    for copy in p_sent:
        copy.wait()
    in_ref[...] = (gr1_ref[...] + mm(gp_in[...], w_qkv[...], 0, 1)).astype(BF16)
    pending = sum_step(2, pending)
    projs[0].step()
    projs[1].step()
    for chunk in ups:
        chunk.step()
    outs.step()
    for q in range(3):
        gdown_ref[64 * q : 64 * (q + 1)] = downs[q].finish()
    pending = sum_step(3, pending)
    projs[2].step()
    projs[0].step()
    projs[1].step()
    for q in range(3):
        gup_ref[:, 256 * q : 256 * (q + 1)] = ups[q].finish()
    gout_ref[...] = outs.finish()
    sum_step(4, pending)
    last = reserve(3)
    for part in (2, 0, 1):
        total = projs[part].finish()
        spot = quarters * part + me
        dest, where = lax.div(spot, 3), lax.rem(spot, 3)

        @pl.when(dest == me)
        def _():
            gqkv_ref[where] = total

        @pl.when(dest != me)
        def _():
            fin[part] = total
            pltpu.make_async_remote_copy(
                src_ref=fin.at[part], dst_ref=gqkv_ref.at[where],
                send_sem=sems.at[0, last + part], recv_sem=sems.at[1, last + where],
                device_id=(dp, dest), device_id_type=MESH,
            ).start()

    for index in range(3):
        spot = quarters * index + me
        source = lax.rem(3 * me + index, quarters)

        @pl.when(lax.div(spot, 3) != me)
        def _():
            copy_to(fin.at[index], gqkv_ref.at[0], sems, last + index, mate).wait_send()

        @pl.when(source != me)
        def _():
            copy_to(fin.at[0], gqkv_ref.at[index], sems, last + index, mate).wait_recv()


def backward_call(tokens, out_grad, gains, shifts, forward, small, w_out, w_up, w_down, w_qkv):
    heads, everyone, packed, a1, a3, n1, n2, marks = forward
    kernel_rows, bounds_two, counts, length = small
    rows, width = tokens.shape
    ff = w_up.shape[1]
    nh = kernel_rows.shape[0]
    head_width = nh * 64
    band_rows, down_cols = width // 8, ff // 8
    whole = pl.BlockSpec(memory_space=VMEM)
    anywhere = pl.BlockSpec(memory_space=pl.ANY)
    shape = jax.ShapeDtypeStruct
    return pl.pallas_call(
        backward_kernel,
        out_shape=(
            shape((rows, width), BF16),
            shape((rows, width), BF16),
            shape((3, band_rows, head_width), F32),
            shape((band_rows, head_width), F32),
            shape((band_rows, ff // 4), F32),
            shape((head_width, down_cols), F32),
            shape((16, width), F32),
        ),
        in_specs=[whole] * 16 + [anywhere] * 4,
        out_specs=[whole] * 7,
        scratch_shapes=[
            VMEM(w_out.shape, BF16), VMEM(w_up.shape, BF16), VMEM(w_down.shape, BF16),
            VMEM(w_qkv.shape, BF16), pltpu.SemaphoreType.DMA((4,)),
            pltpu.SemaphoreType.DMA((2, 96)),
            VMEM((width, rows), BF16),
            VMEM((width, rows), BF16), VMEM((width, rows), BF16),
            VMEM((2 * rows, ff), BF16),
            VMEM((width, rows), BF16), VMEM((width, rows), BF16),
            VMEM((rows, ff), F32),
            VMEM((rows, ff), BF16), VMEM((2, rows, ff // 4), BF16),
            VMEM((rows, width), BF16), VMEM((rows, width), BF16),
            VMEM((width, rows), BF16),
            VMEM((head_width, 4 * rows), BF16),
            VMEM((3 * head_width, 4 * rows), BF16),
            VMEM((3 * width, rows), BF16),
            VMEM((rows, width), F32), VMEM((rows, width), F32), VMEM((rows, width), F32),
            VMEM((5, 16, width), F32), VMEM((5, 16, width), F32),
            VMEM((3, band_rows, head_width), F32),
            VMEM((3, 16, 64, down_cols), BF16), VMEM((3, 15, 64, down_cols), BF16),
            VMEM((3, 16, band_rows, 256), BF16), VMEM((3, 15, band_rows, 256), BF16),
            VMEM((16, band_rows, head_width), BF16), VMEM((15, band_rows, head_width), BF16),
            VMEM((3, 8, band_rows, head_width), BF16), VMEM((3, 7, band_rows, head_width), BF16),
        ],
        compiler_params=pltpu.CompilerParams(
            collective_id=1, has_side_effects=True, vmem_limit_bytes=62 * 2**20
        ),
    )(
        tokens, out_grad, gains, shifts, heads.reshape(width, rows),
        everyone.reshape(4 * rows, width), packed, a1, a3, n1, n2, marks,
        kernel_rows, bounds_two, counts, length, w_out, w_up, w_down, w_qkv,
    )


def per_device_fast(
    tokens, w_qkv, w_out, w_up, w_down, norm_gains, norm_shifts, conv_kernels, seq_lengths,
    seg_bounds, out_grad,
):
    quarters = lax.axis_size("head")
    heads, taps = conv_kernels.shape
    small = small_inputs(conv_kernels, seq_lengths, seg_bounds, lax.axis_index("head"), heads // quarters)
    forward = forward_call(tokens, w_qkv, *small, quarters)
    out, in_grad, g_qkv, g_out, g_up, g_down, sums = backward_call(
        tokens, out_grad, norm_gains, norm_shifts, forward, small, w_out, w_up, w_down, w_qkv
    )
    g_qkv = g_qkv.transpose(1, 0, 2).reshape(g_qkv.shape[1], -1)
    return (
        out, in_grad, g_qkv, g_out, g_up, g_down.T, sums[0:2], sums[2:4],
        sums[4 : 4 + heads, :taps],
    )


highest = lax.Precision.HIGHEST
epsilon = 1e-05


def layer_norm(values, gain, shift):
    center = jnp.mean(values, axis=-1, keepdims=True)
    centred = values - center
    spread_sq = jnp.mean(centred * centred, axis=-1, keepdims=True)
    return centred * lax.rsqrt(spread_sq + epsilon) * gain + shift


def exact_gelu(values):
    return jax.nn.gelu(values, approximate=False)


def shifted_conv(values, kernel):
    slot_len = values.shape[0]
    taps = kernel.shape[0]
    half_width = taps // 2
    padded = jnp.pad(values, ((half_width, half_width), (0, 0)))
    total = jnp.zeros_like(values)
    for offset in range(taps):
        total = total + kernel[offset] * padded[offset : offset + slot_len]
    return total


def nystrom_head(queries, keys, values, kernel, length, bounds):
    slot_len = queries.shape[0]
    mark_count = bounds.shape[0] - 1
    head_dim = queries.shape[1]
    places = jnp.arange(slot_len, dtype=jnp.int32)
    valid = places < length
    weight_mask = valid.astype(jnp.float32)[:, None]
    scaling = head_dim ** (-0.25)
    queries = queries * weight_mask * scaling
    keys = keys * weight_mask * scaling
    values = values * weight_mask
    member = ((places[None, :] >= bounds[:-1, None]) & (places[None, :] < bounds[1:, None])).astype(
        jnp.float32
    )
    counts = (bounds[1:] - bounds[:-1]).astype(jnp.float32)[:, None]
    query_marks = jnp.dot(member, queries, precision=highest) / counts
    key_marks = jnp.dot(member, keys, precision=highest) / counts
    first = jax.nn.softmax(jnp.dot(queries, key_marks.T, precision=highest), axis=-1)
    middle = jax.nn.softmax(jnp.dot(query_marks, key_marks.T, precision=highest), axis=-1)
    third_scores = jnp.dot(query_marks, keys.T, precision=highest)
    third = jax.nn.softmax(jnp.where(valid[None, :], third_scores, -1000000000.0), axis=-1)
    inverse = middle.T / (jnp.max(jnp.sum(middle, axis=0)) * jnp.max(jnp.sum(middle, axis=1)))
    identity = jnp.eye(mark_count, dtype=jnp.float32)
    for _ in range(NEWTON):
        product = jnp.dot(middle, inverse, precision=highest)
        inner = 7.0 * identity - product
        inner = 15.0 * identity - jnp.dot(product, inner, precision=highest)
        inner = 13.0 * identity - jnp.dot(product, inner, precision=highest)
        inverse = 0.25 * jnp.dot(inverse, inner, precision=highest)
    summary = jnp.dot(third, values, precision=highest)
    mixed = jnp.dot(first, jnp.dot(inverse, summary, precision=highest), precision=highest)
    return (mixed + shifted_conv(values, kernel)) * weight_mask


def attend(packed, kernels, lengths, bounds):
    seq_count = lengths.shape[0]
    head_count = kernels.shape[0]
    head_dim = packed.shape[-1] // (3 * head_count)
    grouped = packed.reshape(seq_count, -1, 3, head_count, head_dim)
    over_heads = jax.vmap(nystrom_head, in_axes=(1, 1, 1, 0, None, None), out_axes=1)
    over_seqs = jax.vmap(over_heads, in_axes=(0, 0, 0, None, 0, 0))
    result = over_seqs(
        grouped[:, :, 0], grouped[:, :, 1], grouped[:, :, 2], kernels, lengths, bounds
    )
    return result.reshape(seq_count * grouped.shape[1], head_count * head_dim)


def row_contract(left, right):
    return lax.dot_general(
        left, right, (((0,), (0,)), ((), ())), preferred_element_type=jnp.float32
    )


def to_blocks(matrix, dp_count, quarters):
    total_rows, total_cols = matrix.shape
    shaped = matrix.reshape(dp_count, total_rows // dp_count, quarters, total_cols // quarters)
    return shaped.transpose(0, 2, 1, 3).reshape(total_rows * quarters, total_cols // quarters)


def per_device(
    tokens,
    w_qkv,
    w_out,
    w_up,
    w_down,
    norm_gains,
    norm_shifts,
    conv_kernels,
    seq_lengths,
    seg_bounds,
    out_grad,
):
    quarters = lax.axis_size("head")
    quarter = lax.axis_index("head")
    dp_count = lax.axis_size("dp")
    tok_rows, width = tokens.shape
    seq_count = seq_lengths.shape[0]
    group_rows = tok_rows * quarters
    slot_len = group_rows // seq_count
    head_count, kernel_len = conv_kernels.shape
    local_heads = head_count // quarters
    head_width = w_qkv.shape[1] // (3 * quarters)
    places = quarter * tok_rows + jnp.arange(tok_rows, dtype=jnp.int32)
    owners = places // slot_len
    within = places % slot_len
    limits = jnp.sum(
        jnp.where(
            owners[:, None] == jnp.arange(seq_count, dtype=jnp.int32)[None, :],
            seq_lengths[None, :],
            0,
        ),
        axis=1,
    )
    live = (within < limits).astype(jnp.float32)[:, None]
    local_kernels = lax.dynamic_slice_in_dim(
        conv_kernels.astype(jnp.float32), quarter * local_heads, local_heads, 0
    )
    projected = jnp.dot(tokens, w_qkv, preferred_element_type=jnp.float32).astype(jnp.bfloat16)
    packed = lax.all_to_all(
        projected.reshape(tok_rows, 3, quarters, head_width),
        "head",
        split_axis=2,
        concat_axis=0,
        tiled=True,
    )
    packed_rows = packed.reshape(group_rows, 3 * head_width)

    def attention_piece(packed_in, kernel_in):
        return attend(packed_in, kernel_in, seq_lengths, seg_bounds)

    attended, attention_back = jax.vjp(
        attention_piece, packed_rows.astype(jnp.float32), local_kernels
    )
    attended_low = attended.astype(jnp.bfloat16)
    heads_rows = lax.all_to_all(
        attended_low.reshape(group_rows, 1, head_width),
        "head",
        split_axis=0,
        concat_axis=1,
        tiled=True,
    ).reshape(tok_rows, width)
    branch = jnp.dot(heads_rows, w_out, preferred_element_type=jnp.float32)
    first_in = tokens.astype(jnp.float32) + branch
    first_norm, first_back = jax.vjp(layer_norm, first_in, norm_gains[0], norm_shifts[0])
    first_low = first_norm.astype(jnp.bfloat16)
    hidden = jnp.dot(first_low, w_up, preferred_element_type=jnp.float32)
    activated, gelu_back = jax.vjp(exact_gelu, hidden)
    act_low = activated.astype(jnp.bfloat16)
    second = jnp.dot(act_low, w_down, preferred_element_type=jnp.float32)
    output, second_back = jax.vjp(layer_norm, first_norm + second, norm_gains[1], norm_shifts[1])
    cotangent = out_grad.astype(jnp.float32) * live
    grad_second_in, grad_gain_two, grad_shift_two = second_back(cotangent)
    grad_second = grad_second_in.astype(jnp.bfloat16)
    grad_down = row_contract(act_low, grad_second)
    grad_act = jnp.dot(grad_second, w_down.T, preferred_element_type=jnp.float32)
    grad_hidden = gelu_back(grad_act)[0].astype(jnp.bfloat16)
    grad_up = row_contract(first_low, grad_hidden)
    grad_first = grad_second_in + jnp.dot(grad_hidden, w_up.T, preferred_element_type=jnp.float32)
    grad_first_in, grad_gain_one, grad_shift_one = first_back(grad_first)
    grad_branch = grad_first_in.astype(jnp.bfloat16)
    grad_wout = row_contract(heads_rows, grad_branch)
    grad_heads = jnp.dot(grad_branch, w_out.T, preferred_element_type=jnp.float32).astype(
        jnp.bfloat16
    )
    heads_grad = lax.all_to_all(
        grad_heads.reshape(tok_rows, quarters, head_width),
        "head",
        split_axis=1,
        concat_axis=0,
        tiled=True,
    ).reshape(group_rows, head_width)
    grad_packed, grad_local_kernels = attention_back(heads_grad.astype(jnp.float32))
    grad_packed_low = grad_packed.astype(jnp.bfloat16).reshape(group_rows, 3, 1, head_width)
    grad_projected = lax.all_to_all(
        grad_packed_low, "head", split_axis=0, concat_axis=2, tiled=True
    ).reshape(tok_rows, 3 * quarters * head_width)
    grad_wqkv = row_contract(tokens, grad_projected)
    input_grad = (
        grad_first_in + jnp.dot(grad_projected, w_qkv.T, preferred_element_type=jnp.float32)
    ).astype(jnp.bfloat16)
    kernel_full = lax.dynamic_update_slice_in_dim(
        jnp.zeros((head_count, kernel_len), jnp.float32),
        grad_local_kernels,
        quarter * local_heads,
        0,
    )
    small_sums = lax.psum(
        (
            jnp.stack([grad_gain_one, grad_gain_two]),
            jnp.stack([grad_shift_one, grad_shift_two]),
            kernel_full,
        ),
        ("dp", "head"),
    )
    blocked_qkv = to_blocks(grad_wqkv, dp_count, quarters)
    blocked_out = to_blocks(grad_wout, dp_count, quarters)
    blocked_up = to_blocks(grad_up, dp_count, quarters)
    blocked_down = to_blocks(grad_down, dp_count, quarters)
    weight_sums = (
        lax.psum_scatter(blocked_qkv, ("dp", "head"), scatter_dimension=0, tiled=True),
        lax.psum_scatter(blocked_out, ("dp", "head"), scatter_dimension=0, tiled=True),
        lax.psum_scatter(blocked_up, ("dp", "head"), scatter_dimension=0, tiled=True),
        lax.psum_scatter(blocked_down, ("dp", "head"), scatter_dimension=0, tiled=True),
    )
    return (
        output.astype(jnp.bfloat16),
        input_grad,
        weight_sums[0],
        weight_sums[1],
        weight_sums[2],
        weight_sums[3],
        small_sums[0],
        small_sums[1],
        small_sums[2],
    )


def solution(mesh):
    placed = (
        P(("dp", "head"), None),
        P(),
        P(),
        P(),
        P(),
        P(),
        P(),
        P(),
        P("dp"),
        P("dp", None),
        P(("dp", "head"), None),
    )
    aligned = mesh.shape["dp"] == 8 and mesh.shape["head"] == 4
    return jax.shard_map(
        per_device_fast if aligned else per_device,
        mesh=mesh,
        in_specs=placed,
        out_specs=(
            P(("dp", "head"), None),
            P(("dp", "head"), None),
            P("dp", "head"),
            P("dp", "head"),
            P("dp", "head"),
            P("dp", "head"),
            P(),
            P(),
            P(),
        ),
        check_vma=False,
    )
```

```python
import jax
import jax.numpy as jnp
from jax import lax
from jax.sharding import PartitionSpec as P
from jax.experimental import pallas as pl
from jax.experimental.pallas import tpu as pltpu

MESH = pl.DeviceIdType.MESH
NEWTON = 6
F32 = jnp.float32
BF16 = jnp.bfloat16
VMEM = pltpu.VMEM
HEADS_HERE = 3
DIM = 64
TAPS = 33


def mm(a, b, ca, cb):
    return lax.dot_general(a, b, (((ca,), (cb,)), ((), ())), preferred_element_type=F32)


def halves(value):
    high = value.astype(BF16)
    return high, (value - high.astype(F32)).astype(BF16)


def cat(parts, axis):
    return jnp.concatenate(parts, axis=axis)


class Packs:
    def __init__(self):
        lane = lax.broadcasted_iota(jnp.int32, (1, HEADS_HERE * DIM), 1)
        self.hit = [(lane // DIM == h).astype(F32) for h in range(HEADS_HERE)]
        self.low_hit = [h.astype(BF16) for h in self.hit]
        rows = lax.broadcasted_iota(jnp.int32, (DIM, HEADS_HERE * DIM), 0)
        cols = lax.broadcasted_iota(jnp.int32, (DIM, HEADS_HERE * DIM), 1)
        self.unit = (rows == cols % DIM).astype(F32)

    def block(self, low):
        return cat([low * h for h in self.low_hit], 0)

    def times(self, lhs, rhs, side=0):
        rows = lhs.shape[0]
        l_high, l_low = halves(lhs)
        r_high, r_low = halves(rhs)
        both = mm(cat([l_high, l_low], 0), self.block(r_high), 1, side)
        return both[:rows] + both[rows:] + mm(l_high, self.block(r_low), 1, side)

    def diagonal(self, full):
        total = full[:DIM] * self.hit[0]
        for h in range(1, HEADS_HERE):
            total = total + full[DIM * h : DIM * (h + 1)] * self.hit[h]
        return total

    def turn(self, value):
        tall = value.T
        return cat([tall[DIM * h : DIM * (h + 1)] for h in range(HEADS_HERE)], 1)

    def each(self, values):
        total = values[0] * self.hit[0]
        for h in range(1, HEADS_HERE):
            total = total + values[h] * self.hit[h]
        return total

    def row_max(self, value):
        return self.each(
            [
                jnp.max(jnp.where(h > 0, value, -jnp.inf), axis=1, keepdims=True)
                for h in self.hit
            ]
        )

    def row_sum(self, value):
        return self.each([jnp.sum(value * h, axis=1, keepdims=True) for h in self.hit])


def expand(block_low, lhs_side, wide):
    return mm(block_low, wide, lhs_side, 0)


def toeplitz(base):
    rows = jnp.broadcast_to(base, (128, base.shape[1]))
    return pltpu.roll(rows, 0, 1, stride=1, stride_axis=0).astype(BF16)


def windows(mat):
    zero = jnp.zeros((mat.shape[0], 128), mat.dtype)
    wide = cat([zero, mat, zero], 1)
    return cat([wide[:, 128 * b : 128 * b + 384] for b in range(mat.shape[1] // 128)], 0)


def unwindow(stacked, rows):
    return cat([stacked[rows * b : rows * (b + 1)] for b in range(stacked.shape[0] // rows)], 1)


def gelu_pair(hidden):
    tail = jnp.exp(-0.5 * hidden * hidden)
    t = 1.0 / (1.0 + 0.23164190 * jnp.abs(hidden))
    poly = 1.330274429
    for term in (-1.821255978, 1.781477937, -0.356563782, 0.319381530):
        poly = poly * t + term
    density = 0.3989422804014327 * tail
    below = density * poly * t
    normal = jnp.where(hidden >= 0.0, 1.0 - below, below)
    return hidden * normal, normal + hidden * density


def norm_forward(values):
    center = jnp.mean(values, axis=-1, keepdims=True)
    centred = values - center
    spread = jnp.mean(centred * centred, axis=-1, keepdims=True)
    root = lax.rsqrt(spread + 1e-5)
    return centred * root, root


def norm_backward(grad, gain, normed, root):
    scaled = grad * gain
    center = jnp.mean(scaled, axis=-1, keepdims=True)
    along = jnp.mean(scaled * normed, axis=-1, keepdims=True)
    return root * (scaled - center - normed * along)


def copy_to(src, dst, sems, index, device):
    return pltpu.make_async_remote_copy(
        src_ref=src,
        dst_ref=dst,
        send_sem=sems.at[0, index],
        recv_sem=sems.at[1, index],
        device_id=device,
        device_id_type=MESH,
    )


def greet(devices):
    barrier = pltpu.get_barrier_semaphore()
    for device in devices:
        pl.semaphore_signal(barrier, inc=1, device_id=device, device_id_type=MESH)
    pl.semaphore_wait(barrier, len(devices))


class Spread:
    def __init__(self, acc, got, bits, sems, base):
        self.acc, self.got, self.bits, self.sems, self.base = acc, got, bits, sems, base
        self.blocks = acc.shape[0]
        self.stage = 0
        self.offset = 0
        self.at = 0
        self.sent = []

    def start(self):
        bit, device = self.bits[self.stage]
        size = self.blocks >> (self.stage + 1)
        self.keep = self.offset + bit * size
        other = self.offset + (1 - bit) * size
        self.flight = copy_to(
            self.acc.at[pl.ds(other, size)], self.got.at[pl.ds(self.at, size)],
            self.sems, self.base + self.stage, device,
        )
        self.flight.start()
        self.size = size

    def take(self):
        self.flight.wait_recv()
        self.sent.append(self.flight)
        mine, new = pl.ds(self.keep, self.size), pl.ds(self.at, self.size)
        self.at += self.size
        self.offset = self.keep
        self.stage += 1
        if self.stage == len(self.bits):
            return self.acc[mine].astype(F32) + self.got[new].astype(F32)
        self.acc[mine] = self.acc[mine] + self.got[new]
        return None

    def step(self):
        self.take()
        self.start()

    def finish(self):
        total = self.take()
        for sent in self.sent:
            sent.wait_send()
        return total[0]


def position(order, values):
    spot = 0
    for name in order:
        spot = 2 * spot + values[name]
    return spot


DOWN_ORDERS = (("x", "y", "l", "h"), ("y", "l", "x", "h"), ("l", "y", "x", "h"))
UP_ORDERS = (("y", "l", "x", "h"), ("l", "y", "x", "h"), ("x", "l", "y", "h"))
OUT_ORDER = ("y", "l", "x", "h")
QKV_ORDERS = (("y", "l", "h"), ("l", "y", "h"), ("l", "y", "h"))


def main_kernel(
    tok_hbm, grad_hbm, wqkv_hbm, wout_hbm, wup_hbm, wdown_hbm,
    gain_ref, shift_ref, taps_ref, len_ref, bounds_ref,
    out_hbm, in_hbm, gqkv_hbm, gout_hbm, gup_hbm, gdown_hbm, ggain_hbm, gshift_hbm, gtaps_hbm,
    tok, grad_in, w_qkv, w_out, w_up, w_down, lsem, sems,
    everyone, wt, bases, packed, a1, a3, chain, marks, att, heads, heads_x,
    low_t, low_x, act, gst, gst_x, slope, gh, gh_x, gb, gb_x, gatt, g_in, gproj, gp_in,
    first_ref, norm1_ref, gr1_ref, sum_s, sum_r, fin, slots,
    acc_down, got_down, acc_up, got_up, acc_out, got_out, acc_qkv, got_qkv,
    out_v, in_v, gqkv_v, gout_v, gup_v, gdown_v, ggain_v, gshift_v, gtaps_v,
):
    dp = lax.axis_index("dp")
    me = lax.axis_index("head")
    quarters = 4
    rows, width = tok.shape
    slot = rows * quarters
    hidden_width = w_up.shape[1]
    block = hidden_width // quarters
    head_width = width // quarters
    count = DIM
    nh = HEADS_HERE
    band_rows = width // 8
    down_cols = hidden_width // 8
    core = lax.rem(me, 2)
    mate = (dp, me ^ 1)
    bits = {
        "x": (lax.div(me, 2), (dp, me ^ 2)),
        "y": (lax.rem(dp, 2), (dp ^ 1, me)),
        "l": (lax.rem(lax.div(dp, 2), 2), (dp ^ 2, me)),
        "h": (lax.div(dp, 4), (dp ^ 4, me)),
    }
    counter = iter(range(200))
    local = iter(range(40))

    def fetch(src, dst):
        copy = pltpu.make_async_copy(src, dst, lsem.at[next(local)])
        copy.start()
        return copy

    def send(src, dst, device):
        copy = copy_to(src, dst, sems, next(counter), device)
        copy.start()
        return copy

    def reserve(n):
        base = next(counter)
        for _ in range(n - 1):
            next(counter)
        return base

    def spread(acc, got, order):
        return Spread(acc, got, [bits[name] for name in order], sems, reserve(len(order)))

    own_fetch = fetch(tok_hbm, everyone.at[me])
    tok_fetch = fetch(tok_hbm, tok)
    wqkv_fetch = fetch(wqkv_hbm, w_qkv)
    wout_fetch = fetch(wout_hbm, w_out)
    wup_fetch = fetch(wup_hbm, w_up)
    wdown_fetch = fetch(wdown_hbm, w_down)
    grad_fetch = fetch(grad_hbm, grad_in)
    greet([(dp, me ^ k) for k in (1, 2, 3)] + [(dp ^ k, me) for k in (1, 2, 4)])
    half = rows // 2
    far = []
    for piece in range(2):
        part = pl.ds(piece * half, half)
        far.append(send(tok_hbm.at[part], everyone.at[me, part], (dp, me ^ 2)))
    near = send(tok_hbm, everyone.at[me], mate)
    wqkv_fetch.wait()
    odd = lax.rem(me, 2)
    for part in range(3):
        start = pl.multiple_of(part * width + 2 * head_width * lax.div(me, 2) + 128 * odd, 128)
        wt[part] = w_qkv[:, pl.ds(start, 256)].T
    w_own = cat(
        [wt[part, pl.ds(pl.multiple_of(64 * odd, 64), head_width), :] for part in range(3)], 0
    )
    packs = Packs()
    lane = lax.broadcasted_iota(jnp.int32, (TAPS, 384), 1)
    tap = lax.broadcasted_iota(jnp.int32, (TAPS, 384), 0)
    for turn, spots in enumerate((tap + 112, 144 - tap)):
        bases[turn] = mm(taps_ref[...], (lane == spots).astype(F32).astype(BF16), 1, 0)
    bands = [
        [toeplitz(bases[turn, pl.ds(nh * me + h, 1), :]) for h in range(nh)] for turn in range(2)
    ]
    edges = bounds_ref[...].astype(F32)
    low_edge = jnp.broadcast_to(edges[:, :count], (count, count)).T[:, 0:1]
    high_edge = jnp.broadcast_to(edges[:, 1 : count + 1], (count, count)).T[:, 0:1]
    place = lax.broadcasted_iota(jnp.int32, (count, slot), 1).astype(F32)
    member = ((place >= low_edge) & (place < high_edge)).astype(F32).astype(BF16)
    share_of = 1.0 / (high_edge - low_edge)
    length = len_ref[0]
    live = lax.broadcasted_iota(jnp.int32, (1, slot), 1) < length
    scale = DIM ** (-0.25)

    def project(which):
        lanes = pl.ds(pl.multiple_of(rows * which, rows), rows)
        packed[:, lanes] = mm(w_own, everyone[which], 1, 1).astype(BF16)

    own_fetch.wait()
    project(me)
    near.wait()
    project(me ^ 1)
    onward = []
    for piece in range(2):
        part = pl.ds(piece * half, half)
        far[piece].wait()
        onward.append(send(everyone.at[me ^ 2, part], everyone.at[me ^ 2, part], mate))
    project(me ^ 2)
    for copy in onward:
        copy.wait()
    project(me ^ 3)
    queries = packed[:head_width]
    keys = packed[head_width : 2 * head_width]
    q_marks = mm(member, queries, 1, 1) * (scale * share_of)
    k_marks = mm(member, keys, 1, 1) * (scale * share_of)
    marks[0] = q_marks
    marks[1] = k_marks
    scores = packs.times(q_marks, k_marks, 1)
    powers = jnp.exp(scores - packs.row_max(scores))
    middle = powers / packs.row_sum(powers)
    marks[2] = middle
    col_sums = jnp.sum(middle, axis=0, keepdims=True)
    col_top = packs.row_max(col_sums)
    row_top = jnp.max(packs.row_sum(middle), axis=0, keepdims=True)
    inverse_t = middle / (col_top * row_top)
    product = packs.times(inverse_t, middle, 1)
    for step in range(NEWTON):
        second = packs.times(product, product)
        pair = packs.times(cat([product, second], 0), second)
        third, fourth = pair[:count], pair[count:]
        for i, value in enumerate((product, second, third, inverse_t)):
            chain[step, i] = value
        blend = 0.25 * (13.0 * packs.unit - 15.0 * product + 7.0 * second - third)
        product = 0.25 * (13.0 * product - 15.0 * second + 7.0 * third - fourth)
        inverse_t = packs.times(blend, inverse_t)
    marks[3] = inverse_t
    def tall_scores(values, wide):
        high, low = halves(values * scale)
        both = mm(cat([packs.block(high), packs.block(low)], 0), wide, 1, 0)
        return both[:head_width] + both[head_width:]

    def per_head(value):
        return value.reshape(nh, count, slot)

    scores = per_head(tall_scores(k_marks, queries))
    powers = jnp.exp(scores - jnp.max(scores, axis=1, keepdims=True))
    first = (powers * (1.0 / jnp.sum(powers, axis=1, keepdims=True))).reshape(head_width, slot)
    a1[...] = first
    scores = jnp.where(live, tall_scores(q_marks, keys), -1e9)
    powers = jnp.exp(scores - jnp.max(scores, axis=1, keepdims=True))
    third = powers * (1.0 / jnp.sum(powers, axis=1, keepdims=True))
    a3[...] = third
    values = jnp.where(live, packed[2 * head_width :].astype(F32), 0.0).astype(BF16)
    t_high, t_low = halves(third)
    summary_t = packs.diagonal(mm(values, t_high, 1, 1) + mm(values, t_low, 1, 1))
    weights_t = packs.times(summary_t, inverse_t)
    marks[4] = summary_t
    marks[5] = weights_t
    w_high, w_low = halves(weights_t)
    f_high, f_low = halves(first)
    mixed = mm(cat([packs.block(w_high), packs.block(w_low)], 0), f_high, 1, 0)
    mixed = mixed[:head_width] + mixed[head_width:] + mm(packs.block(w_high), f_low, 1, 0)
    for h in range(nh):
        part = slice(DIM * h, DIM * (h + 1))
        conv = unwindow(mm(windows(values[part]), bands[0][h], 1, 1), DIM)
        att[part] = jnp.where(live, mixed[part] + conv, 0.0).astype(BF16)
    mine = pl.ds(pl.multiple_of(rows * me, rows), rows)
    own_rows = pl.ds(pl.multiple_of(head_width * me, 64), head_width)
    att_sent = []
    for k in (2, 3, 1):
        lanes = pl.ds(pl.multiple_of(rows * (me ^ k), rows), rows)
        att_sent.append(send(att.at[:, lanes], heads.at[own_rows], (dp, me ^ k)))
    heads[own_rows] = att[:, mine]
    wout_fetch.wait()
    tok_fetch.wait()
    for copy in att_sent:
        copy.wait()
    heads_sent = send(heads, heads_x, mate)
    branch = mm(heads[...], w_out[...], 0, 0)
    normed, root_one = norm_forward(tok[...].astype(F32) + branch)
    norm1_ref[...] = normed
    first_norm = normed * gain_ref[0:1] + shift_ref[0:1]
    first_ref[...] = first_norm
    low = first_norm.astype(BF16)
    low_t[...] = low.T
    low_sent = send(low_t, low_x, mate)
    wup_fetch.wait()
    wdown_fetch.wait()
    second_sum = None
    act_sent = []
    for i in range(quarters):
        cols = slice(block * i, block * (i + 1))
        active, slope_part = gelu_pair(mm(low, w_up[:, cols], 1, 0))
        active = active.astype(BF16)
        act[:rows, cols] = active
        act_sent.append(send(act.at[:rows, cols], act.at[rows:, cols], mate))
        slope[:, cols] = slope_part
        part = mm(active, w_down[cols, :], 1, 0)
        second_sum = part if second_sum is None else second_sum + part
    normed_two, root_two = norm_forward(first_ref[...] + second_sum)
    out_v[...] = (normed_two * gain_ref[1:2] + shift_ref[1:2]).astype(BF16)
    stores = [fetch(out_v, out_hbm)]
    grad_fetch.wait()
    spot = me * rows + lax.broadcasted_iota(jnp.int32, (rows, 1), 0)
    cotangent = jnp.where(spot < length, grad_in[...].astype(F32), 0.0)
    sum_s[0] = jnp.zeros(sum_s.shape[1:], F32)
    sum_s[0, 1:2] = jnp.sum(cotangent * normed_two, axis=0, keepdims=True)
    sum_s[0, 3:4] = jnp.sum(cotangent, axis=0, keepdims=True)
    g_two = norm_backward(cotangent, gain_ref[1:2], normed_two, root_two)
    gr1_ref[...] = g_two
    g_low = g_two.astype(BF16)
    gst[...] = g_low.T
    gst_sent = send(gst, gst_x, mate)
    for copy in act_sent:
        copy.wait()
    gst_sent.wait()
    lead = cat(
        [
            cat(
                [
                    ref[pl.ds(pl.multiple_of(head_width * (2 * x + core), 64), head_width), :]
                    for ref in (gst, gst_x)
                ],
                1,
            )
            for x in range(2)
        ],
        0,
    )
    for pair in range(4):
        total = mm(lead, act[:, 2 * down_cols * pair : 2 * down_cols * (pair + 1)], 1, 0)
        total = total.astype(BF16)
        for x in range(2):
            for inner in range(2):
                at = {"x": x, "y": inner, "l": pair % 2, "h": pair // 2}
                for q in range(3):
                    top = head_width * x + 64 * q
                    acc_down[q, position(DOWN_ORDERS[q], at)] = total[
                        top : top + 64, down_cols * inner : down_cols * (inner + 1)
                    ]
    downs = [spread(acc_down.at[q], got_down.at[q], DOWN_ORDERS[q]) for q in range(3)]
    for chunk in downs:
        chunk.start()
    g_first = gr1_ref[...]
    gh_sent = []
    for i in range(quarters):
        cols = slice(block * i, block * (i + 1))
        part = (slope[:, cols] * mm(g_low, w_down[cols, :], 1, 1)).astype(BF16)
        gh[:, cols] = part
        g_first = g_first + mm(part, w_up[:, cols], 1, 1)
        if i % 2:
            lanes = pl.ds(pl.multiple_of(block * (i - core), 128), block)
            gh_sent.append(send(gh.at[:, lanes], gh_x.at[i // 2], mate))
    normed = norm1_ref[...]
    sum_s[0, 0:1] = jnp.sum(g_first * normed, axis=0, keepdims=True)
    sum_s[0, 2:3] = jnp.sum(g_first, axis=0, keepdims=True)
    g_one = norm_backward(g_first, gain_ref[0:1], normed, root_one)
    gr1_ref[...] = g_one
    g_branch = g_one.astype(BF16)
    gb[...] = g_branch
    gatt[...] = mm(w_out[...], g_branch, 1, 1).astype(BF16)
    g_sent = []
    for k in (2, 3, 1):
        src = gatt.at[pl.ds(pl.multiple_of(head_width * (me ^ k), 64), head_width)]
        g_sent.append(send(src, g_in.at[:, mine], (dp, me ^ k)))
    gb_sent = send(gb, gb_x, mate)
    g_in[:, mine] = gatt[own_rows]
    low_sent.wait()
    for copy in gh_sent:
        copy.wait()
    lead = cat([low_t[...], low_x[...]], 1)
    ups = [spread(acc_up.at[q], got_up.at[q], UP_ORDERS[q]) for q in range(3)]
    for q in range(3):
        for x in range(2):
            lanes = pl.ds(pl.multiple_of(block * (2 * x + core) + 256 * q, 128), 256)
            side = cat([gh[:, lanes], gh_x[x, :, 256 * q : 256 * (q + 1)]], 0)
            total = mm(lead, side, 1, 0).astype(BF16)
            for d in range(8):
                at = {"x": x, "y": d % 2, "l": d // 2 % 2, "h": d // 4}
                acc_up[q, position(UP_ORDERS[q], at)] = total[
                    band_rows * d : band_rows * (d + 1)
                ]
        ups[q].start()
    for chunk in downs:
        chunk.step()
    heads_sent.wait()
    gb_sent.wait()
    lead = cat([heads[...], heads_x[...]], 1)
    both = cat([gb[...], gb_x[...]], 0)
    band_half = band_rows // 2

    def folded(total, d):
        top = band_rows * d
        return cat([total[top : top + band_half], total[top + band_half : top + band_rows]], 1)

    for x in range(2):
        left_cols = both[:, 2 * head_width * x : 2 * head_width * x + head_width]
        right_cols = both[:, 2 * head_width * x + head_width : 2 * head_width * (x + 1)]
        total = mm(lead, jnp.where(core == 0, left_cols, right_cols), 1, 0).astype(BF16)
        for d in range(8):
            at = {"x": x, "y": d % 2, "l": d // 2 % 2, "h": d // 4}
            acc_out[position(OUT_ORDER, at)] = folded(total, d)
    outs = spread(acc_out, got_out, OUT_ORDER)
    outs.start()
    tokens_t = everyone[...].reshape(slot, width).T
    for copy in g_sent:
        copy.wait()
    grad = jnp.where(live, g_in[...].astype(F32), 0.0).astype(BF16)
    values = jnp.where(live, packed[2 * head_width :].astype(F32), 0.0).astype(BF16)
    first, third = a1[...], a3[...]
    inverse_t, summary_t, weights_t = marks[3], marks[4], marks[5]
    f_high, f_low = halves(first)
    t_high, t_low = halves(third)
    g_weights = packs.diagonal(mm(f_high, grad, 1, 1) + mm(f_low, grad, 1, 1))
    g_summary = packs.times(inverse_t, g_weights)
    s_high, s_low = halves(g_summary)
    g_values = mm(packs.block(s_high), t_high, 0, 0) + mm(packs.block(s_low), t_high, 0, 0)
    g_values = g_values + mm(packs.block(s_high), t_low, 0, 0)
    flip_rows = lax.broadcasted_iota(jnp.int32, (128, 128), 0)
    flip_cols = lax.broadcasted_iota(jnp.int32, (128, 128), 1)
    flip = (flip_rows + flip_cols == 127).astype(F32).astype(BF16)
    for h in range(nh):
        part = slice(DIM * h, DIM * (h + 1))
        g_wide = windows(grad[part])
        total = g_values[part] + unwindow(mm(g_wide, bands[1][h], 1, 1), DIM)
        gproj[2 * head_width + DIM * h : 2 * head_width + DIM * (h + 1)] = jnp.where(
            live, total, 0.0
        ).astype(BF16)
        turned = mm(g_wide[:, 128:256], flip, 1, 0).astype(BF16)
        gram = mm(turned, windows(values[part]), 0, 0)
        gram = pltpu.roll(gram, 384 - 127, 1, stride=1, stride_axis=0)
        found = pltpu.roll(jnp.sum(gram, axis=0, keepdims=True), 384 - 112, 1)
        at = lax.broadcasted_iota(jnp.int32, found.shape, 1)
        sum_s[0, pl.ds(4 + nh * me + h, 1), 0:384] = jnp.where(at < TAPS, found, 0.0)
    p_sent = []

    def share(part):
        own = gproj.at[head_width * part : head_width * (part + 1)]
        dst = pl.ds(pl.multiple_of(width * part + head_width * me, 64), head_width)
        for k in (2, 3, 1):
            lanes = pl.ds(pl.multiple_of(rows * (me ^ k), rows), rows)
            p_sent.append(send(own.at[:, lanes], gp_in.at[dst], (dp, me ^ k)))
        gp_in[dst] = own[:, mine]

    projs = [spread(acc_qkv.at[j], got_qkv.at[j], QKV_ORDERS[j]) for j in range(3)]

    def qkv_gradient(part):
        total = mm(tokens_t, gproj[head_width * part : head_width * (part + 1)], 1, 1)
        total = total.astype(BF16)
        for d in range(8):
            at = {"y": d % 2, "l": d // 2 % 2, "h": d // 4}
            acc_qkv[part, position(QKV_ORDERS[part], at)] = folded(total, d)
        projs[part].start()

    share(2)
    qkv_gradient(2)
    sums = [mate] + [bits[name][1] for name in ("x", "y", "l", "h")]
    sum_base = reserve(5)

    def sum_start(k):
        copy = copy_to(sum_s.at[k], sum_r.at[k], sems, sum_base + k, sums[k])
        copy.start()
        return copy

    def sum_step(k, copy):
        copy.wait()
        total = sum_s[k] + sum_r[k]
        if k == 4:
            return total
        sum_s[k + 1] = total
        return sum_start(k + 1)

    pending = sum_start(0)
    outer = packs.times(g_weights, summary_t)
    hold = jnp.zeros_like(outer)
    for step in reversed(range(NEWTON)):
        product, second, cube, inverse_t = [chain[step, i] for i in range(4)]
        blend = 0.25 * (13.0 * packs.unit - 15.0 * product + 7.0 * second - cube)
        inner = packs.times(inverse_t, outer)
        by_inner = packs.times(cat([product, second], 0), inner)
        zero_th, once, twice = inner, by_inner[:count], by_inner[count:]
        if step < NEWTON - 1:
            by_hold = packs.times(cat([product, second, cube], 0), hold)
            zero_th = zero_th + by_hold[:count]
            once = once + by_hold[count : 2 * count]
            twice = twice + by_hold[2 * count :]
        rest = packs.times(zero_th, 7.0 * product - second - 15.0 * packs.unit)
        rest = rest + packs.times(once, 7.0 * packs.unit - product) - twice
        pair = packs.times(cat([outer, hold], 0), blend)
        outer, hold = pair[:count], pair[count:] + 0.25 * rest
    w_high, w_low = halves(weights_t)
    g_tall = mm(packs.block(w_high), grad, 0, 0) + mm(packs.block(w_low), grad, 0, 0)
    along = jnp.sum(per_head(g_tall * first), axis=1, keepdims=True)
    g_one = first * (per_head(g_tall) - along).reshape(head_width, slot)
    g_tall = mm(cat([packs.block(s_high), packs.block(s_low)], 0), values, 1, 0)
    g_tall = g_tall[:head_width] + g_tall[head_width:]
    g_three = third * (g_tall - jnp.sum(g_tall * third, axis=1, keepdims=True))
    queries = packed[:head_width]
    keys = packed[head_width : 2 * head_width]

    def tall_marks(high, low, wide):
        both = mm(cat([high, low], 0), wide, 1, 1)
        return packs.diagonal(both[:head_width] + both[head_width:]) * scale

    one_high, one_low = halves(g_one)
    three_high, three_low = halves(g_three)
    g_k_marks = tall_marks(one_high, one_low, queries)
    g_q_marks = tall_marks(three_high, three_low, keys)
    q_marks, k_marks, middle = marks[0], marks[1], marks[2]
    inverse_t = chain[0, 3]
    col_sums = jnp.sum(middle, axis=0, keepdims=True)
    row_sums = packs.row_sum(middle)
    col_top = packs.row_max(col_sums)
    row_top = jnp.max(row_sums, axis=0, keepdims=True)
    norm = 1.0 / (col_top * row_top)
    g_start_t = packs.turn(outer) + packs.times(packs.turn(hold), middle)
    g_norm = -packs.row_sum(jnp.sum(g_start_t * inverse_t, axis=0, keepdims=True)) * norm
    col_hit = (col_sums == col_top).astype(F32)
    row_hit = (row_sums == row_top).astype(F32)
    col_hit = col_hit / packs.row_sum(col_hit)
    row_hit = row_hit / jnp.sum(row_hit, axis=0, keepdims=True)
    g_middle = packs.times(hold, inverse_t) + g_start_t * norm
    g_middle = g_middle + g_norm * (row_top * col_hit + col_top * row_hit)
    g_two_s = middle * (g_middle - packs.row_sum(g_middle * middle))
    g_q_marks = g_q_marks + packs.times(g_two_s, k_marks)
    g_k_marks = g_k_marks + packs.times(packs.turn(g_two_s), q_marks)
    for base, other, g_own, high in (
        (0, k_marks, g_q_marks, one_high),
        (head_width, q_marks, g_k_marks, three_high),
    ):
        m_high, m_low = halves(other)
        l_high, l_low = halves(g_own * share_of)
        total = mm(packs.block(m_high), high, 0, 0) + mm(packs.block(m_low), high, 0, 0)
        total = total + mm(cat([l_high, l_low], 0), cat([member, member], 0), 0, 0)
        gproj[base : base + head_width] = (total * scale).astype(BF16)
    share(0)
    share(1)
    for chunk in downs:
        chunk.step()
    for chunk in ups:
        chunk.step()
    outs.step()
    pending = sum_step(0, pending)
    qkv_gradient(0)
    qkv_gradient(1)
    for chunk in downs:
        chunk.step()
    projs[2].step()
    pending = sum_step(1, pending)
    for chunk in ups:
        chunk.step()
    outs.step()
    projs[0].step()
    projs[1].step()
    projs[2].step()
    pending = sum_step(2, pending)
    for q in range(3):
        gdown_v[:, 64 * q : 64 * (q + 1)] = downs[q].finish().T
    stores.append(fetch(gdown_v, gdown_hbm))
    for copy in p_sent:
        copy.wait()
    in_v[...] = (gr1_ref[...] + mm(gp_in[...], w_qkv[...], 0, 1)).astype(BF16)
    stores.append(fetch(in_v, in_hbm))
    projs[0].step()
    projs[1].step()
    pending = sum_step(3, pending)
    for chunk in ups:
        chunk.step()
    outs.step()
    last = reserve(3)
    for part in (2, 0, 1):
        total = projs[part].finish()
        goal = quarters * part + me
        dest, where = lax.div(goal, 3), lax.rem(goal, 3)

        @pl.when(dest == me)
        def _():
            slots[where] = total

        @pl.when(dest != me)
        def _():
            fin[part] = total
            pltpu.make_async_remote_copy(
                src_ref=fin.at[part], dst_ref=slots.at[where],
                send_sem=sems.at[0, last + part], recv_sem=sems.at[1, last + where],
                device_id=(dp, dest), device_id_type=MESH,
            ).start()

    for q in range(3):
        gup_v[:, 256 * q : 256 * (q + 1)] = ups[q].finish()
    stores.append(fetch(gup_v, gup_hbm))
    total = outs.finish()
    gout_v[:band_half] = total[:, :head_width]
    gout_v[band_half:] = total[:, head_width:]
    stores.append(fetch(gout_v, gout_hbm))
    total = sum_step(4, pending)
    ggain_v[...] = total[0:2]
    gshift_v[...] = total[2:4]
    gtaps_v[...] = total[4:16, :TAPS]
    stores.append(fetch(ggain_v, ggain_hbm))
    stores.append(fetch(gshift_v, gshift_hbm))
    stores.append(fetch(gtaps_v, gtaps_hbm))
    for index in range(3):
        goal = quarters * index + me
        source = lax.rem(3 * me + index, quarters)

        @pl.when(lax.div(goal, 3) != me)
        def _():
            copy_to(fin.at[index], slots.at[0], sems, last + index, mate).wait_send()

        @pl.when(source != me)
        def _():
            copy_to(fin.at[0], slots.at[index], sems, last + index, mate).wait_recv()

    for index in range(3):
        got = slots[index]
        cols = slice(head_width * index, head_width * (index + 1))
        gqkv_v[:band_half, cols] = got[:, :head_width]
        gqkv_v[band_half:, cols] = got[:, head_width:]
    stores.append(fetch(gqkv_v, gqkv_hbm))
    for copy in stores:
        copy.wait()


def final_kernel(*refs):
    sem = refs[-1]
    count = (len(refs) - 1) // 3
    inward = [
        pltpu.make_async_copy(refs[i], refs[2 * count + i], sem.at[0, i]) for i in range(count)
    ]
    outward = [
        pltpu.make_async_copy(refs[2 * count + i], refs[count + i], sem.at[1, i])
        for i in range(count)
    ]
    for copy in inward:
        copy.start()
    for got, put in zip(inward, outward):
        got.wait()
        put.start()
    for copy in outward:
        copy.wait()


def per_device_fast(
    tokens, w_qkv, w_out, w_up, w_down, norm_gains, norm_shifts, conv_kernels, seq_lengths,
    seg_bounds, out_grad,
):
    rows, width = tokens.shape
    ff = w_up.shape[1]
    head_width = width // 4
    slot = 4 * rows
    band, down_cols = width // 8, ff // 8
    whole = pl.BlockSpec(memory_space=VMEM)
    anywhere = pl.BlockSpec(memory_space=pl.ANY)
    shape = jax.ShapeDtypeStruct
    outs = (
        shape((rows, width), BF16),
        shape((rows, width), BF16),
        shape((band, w_qkv.shape[1] // 4), F32),
        shape((band, width // 4), F32),
        shape((band, ff // 4), F32),
        shape((down_cols, width // 4), F32),
        shape(norm_gains.shape, F32),
        shape(norm_shifts.shape, F32),
        shape(conv_kernels.shape, F32),
    )
    found = pl.pallas_call(
        main_kernel,
        out_shape=outs,
        in_specs=[anywhere] * 6
        + [whole] * 3
        + [pl.BlockSpec(memory_space=pltpu.SMEM), whole],
        out_specs=[anywhere] * 9,
        scratch_shapes=[
            VMEM((rows, width), BF16), VMEM((rows, width), BF16),
            VMEM(w_qkv.shape, BF16), VMEM(w_out.shape, BF16),
            VMEM(w_up.shape, BF16), VMEM(w_down.shape, BF16),
            pltpu.SemaphoreType.DMA((32,)), pltpu.SemaphoreType.DMA((2, 120)),
            VMEM((4, rows, width), BF16),
            VMEM((3, 256, width), BF16),
            VMEM((2, conv_kernels.shape[0], 384), F32),
            VMEM((3 * head_width, slot), BF16),
            VMEM((head_width, slot), F32), VMEM((head_width, slot), F32),
            VMEM((NEWTON, 4, DIM, head_width), F32),
            VMEM((6, DIM, head_width), F32),
            VMEM((head_width, slot), BF16),
            VMEM((width, rows), BF16), VMEM((width, rows), BF16),
            VMEM((width, rows), BF16), VMEM((width, rows), BF16),
            VMEM((2 * rows, ff), BF16),
            VMEM((width, rows), BF16), VMEM((width, rows), BF16),
            VMEM((rows, ff), F32),
            VMEM((rows, ff), BF16), VMEM((2, rows, ff // 4), BF16),
            VMEM((rows, width), BF16), VMEM((rows, width), BF16),
            VMEM((width, rows), BF16),
            VMEM((head_width, slot), BF16),
            VMEM((3 * head_width, slot), BF16),
            VMEM((3 * width, rows), BF16),
            VMEM((rows, width), F32), VMEM((rows, width), F32), VMEM((rows, width), F32),
            VMEM((5, 16, width), F32), VMEM((5, 16, width), F32),
            VMEM((3, band // 2, 2 * head_width), F32),
            VMEM((3, band // 2, 2 * head_width), F32),
            VMEM((3, 16, 64, down_cols), BF16), VMEM((3, 15, 64, down_cols), BF16),
            VMEM((3, 16, band, 256), BF16), VMEM((3, 15, band, 256), BF16),
            VMEM((16, band // 2, 2 * head_width), BF16),
            VMEM((15, band // 2, 2 * head_width), BF16),
            VMEM((3, 8, band // 2, 2 * head_width), BF16),
            VMEM((3, 7, band // 2, 2 * head_width), BF16),
        ]
        + [VMEM(out.shape, out.dtype) for out in outs],
        compiler_params=pltpu.CompilerParams(
            collective_id=0, has_side_effects=True, vmem_limit_bytes=63 * 2**20
        ),
        name="main_kernel",
    )(
        tokens, out_grad, w_qkv, w_out, w_up, w_down, norm_gains, norm_shifts, conv_kernels,
        seq_lengths, seg_bounds,
    )
    return pl.pallas_call(
        final_kernel,
        out_shape=outs,
        in_specs=[anywhere] * 9,
        out_specs=[anywhere] * 9,
        scratch_shapes=[VMEM(out.shape, out.dtype) for out in outs]
        + [pltpu.SemaphoreType.DMA((2, 9))],
        name="final_kernel",
    )(*found)


highest = lax.Precision.HIGHEST
epsilon = 1e-05


def layer_norm(values, gain, shift):
    center = jnp.mean(values, axis=-1, keepdims=True)
    centred = values - center
    spread_sq = jnp.mean(centred * centred, axis=-1, keepdims=True)
    return centred * lax.rsqrt(spread_sq + epsilon) * gain + shift


def exact_gelu(values):
    return jax.nn.gelu(values, approximate=False)


def shifted_conv(values, kernel):
    slot_len = values.shape[0]
    taps = kernel.shape[0]
    half_width = taps // 2
    padded = jnp.pad(values, ((half_width, half_width), (0, 0)))
    total = jnp.zeros_like(values)
    for offset in range(taps):
        total = total + kernel[offset] * padded[offset : offset + slot_len]
    return total


def nystrom_head(queries, keys, values, kernel, length, bounds):
    slot_len = queries.shape[0]
    mark_count = bounds.shape[0] - 1
    head_dim = queries.shape[1]
    places = jnp.arange(slot_len, dtype=jnp.int32)
    valid = places < length
    weight_mask = valid.astype(jnp.float32)[:, None]
    scaling = head_dim ** (-0.25)
    queries = queries * weight_mask * scaling
    keys = keys * weight_mask * scaling
    values = values * weight_mask
    member = ((places[None, :] >= bounds[:-1, None]) & (places[None, :] < bounds[1:, None])).astype(
        jnp.float32
    )
    counts = (bounds[1:] - bounds[:-1]).astype(jnp.float32)[:, None]
    query_marks = jnp.dot(member, queries, precision=highest) / counts
    key_marks = jnp.dot(member, keys, precision=highest) / counts
    first = jax.nn.softmax(jnp.dot(queries, key_marks.T, precision=highest), axis=-1)
    middle = jax.nn.softmax(jnp.dot(query_marks, key_marks.T, precision=highest), axis=-1)
    third_scores = jnp.dot(query_marks, keys.T, precision=highest)
    third = jax.nn.softmax(jnp.where(valid[None, :], third_scores, -1000000000.0), axis=-1)
    inverse = middle.T / (jnp.max(jnp.sum(middle, axis=0)) * jnp.max(jnp.sum(middle, axis=1)))
    identity = jnp.eye(mark_count, dtype=jnp.float32)
    for _ in range(NEWTON):
        product = jnp.dot(middle, inverse, precision=highest)
        inner = 7.0 * identity - product
        inner = 15.0 * identity - jnp.dot(product, inner, precision=highest)
        inner = 13.0 * identity - jnp.dot(product, inner, precision=highest)
        inverse = 0.25 * jnp.dot(inverse, inner, precision=highest)
    summary = jnp.dot(third, values, precision=highest)
    mixed = jnp.dot(first, jnp.dot(inverse, summary, precision=highest), precision=highest)
    return (mixed + shifted_conv(values, kernel)) * weight_mask


def attend(packed, kernels, lengths, bounds):
    seq_count = lengths.shape[0]
    head_count = kernels.shape[0]
    head_dim = packed.shape[-1] // (3 * head_count)
    grouped = packed.reshape(seq_count, -1, 3, head_count, head_dim)
    over_heads = jax.vmap(nystrom_head, in_axes=(1, 1, 1, 0, None, None), out_axes=1)
    over_seqs = jax.vmap(over_heads, in_axes=(0, 0, 0, None, 0, 0))
    result = over_seqs(
        grouped[:, :, 0], grouped[:, :, 1], grouped[:, :, 2], kernels, lengths, bounds
    )
    return result.reshape(seq_count * grouped.shape[1], head_count * head_dim)


def row_contract(left, right):
    return lax.dot_general(
        left, right, (((0,), (0,)), ((), ())), preferred_element_type=jnp.float32
    )


def to_blocks(matrix, dp_count, quarters):
    total_rows, total_cols = matrix.shape
    shaped = matrix.reshape(dp_count, total_rows // dp_count, quarters, total_cols // quarters)
    return shaped.transpose(0, 2, 1, 3).reshape(total_rows * quarters, total_cols // quarters)


def per_device(
    tokens,
    w_qkv,
    w_out,
    w_up,
    w_down,
    norm_gains,
    norm_shifts,
    conv_kernels,
    seq_lengths,
    seg_bounds,
    out_grad,
):
    quarters = lax.axis_size("head")
    quarter = lax.axis_index("head")
    dp_count = lax.axis_size("dp")
    tok_rows, width = tokens.shape
    seq_count = seq_lengths.shape[0]
    group_rows = tok_rows * quarters
    slot_len = group_rows // seq_count
    head_count, kernel_len = conv_kernels.shape
    local_heads = head_count // quarters
    head_width = w_qkv.shape[1] // (3 * quarters)
    places = quarter * tok_rows + jnp.arange(tok_rows, dtype=jnp.int32)
    owners = places // slot_len
    within = places % slot_len
    limits = jnp.sum(
        jnp.where(
            owners[:, None] == jnp.arange(seq_count, dtype=jnp.int32)[None, :],
            seq_lengths[None, :],
            0,
        ),
        axis=1,
    )
    live = (within < limits).astype(jnp.float32)[:, None]
    local_kernels = lax.dynamic_slice_in_dim(
        conv_kernels.astype(jnp.float32), quarter * local_heads, local_heads, 0
    )
    projected = jnp.dot(tokens, w_qkv, preferred_element_type=jnp.float32).astype(jnp.bfloat16)
    packed = lax.all_to_all(
        projected.reshape(tok_rows, 3, quarters, head_width),
        "head",
        split_axis=2,
        concat_axis=0,
        tiled=True,
    )
    packed_rows = packed.reshape(group_rows, 3 * head_width)

    def attention_piece(packed_in, kernel_in):
        return attend(packed_in, kernel_in, seq_lengths, seg_bounds)

    attended, attention_back = jax.vjp(
        attention_piece, packed_rows.astype(jnp.float32), local_kernels
    )
    attended_low = attended.astype(jnp.bfloat16)
    heads_rows = lax.all_to_all(
        attended_low.reshape(group_rows, 1, head_width),
        "head",
        split_axis=0,
        concat_axis=1,
        tiled=True,
    ).reshape(tok_rows, width)
    branch = jnp.dot(heads_rows, w_out, preferred_element_type=jnp.float32)
    first_in = tokens.astype(jnp.float32) + branch
    first_norm, first_back = jax.vjp(layer_norm, first_in, norm_gains[0], norm_shifts[0])
    first_low = first_norm.astype(jnp.bfloat16)
    hidden = jnp.dot(first_low, w_up, preferred_element_type=jnp.float32)
    activated, gelu_back = jax.vjp(exact_gelu, hidden)
    act_low = activated.astype(jnp.bfloat16)
    second = jnp.dot(act_low, w_down, preferred_element_type=jnp.float32)
    output, second_back = jax.vjp(layer_norm, first_norm + second, norm_gains[1], norm_shifts[1])
    cotangent = out_grad.astype(jnp.float32) * live
    grad_second_in, grad_gain_two, grad_shift_two = second_back(cotangent)
    grad_second = grad_second_in.astype(jnp.bfloat16)
    grad_down = row_contract(act_low, grad_second)
    grad_act = jnp.dot(grad_second, w_down.T, preferred_element_type=jnp.float32)
    grad_hidden = gelu_back(grad_act)[0].astype(jnp.bfloat16)
    grad_up = row_contract(first_low, grad_hidden)
    grad_first = grad_second_in + jnp.dot(grad_hidden, w_up.T, preferred_element_type=jnp.float32)
    grad_first_in, grad_gain_one, grad_shift_one = first_back(grad_first)
    grad_branch = grad_first_in.astype(jnp.bfloat16)
    grad_wout = row_contract(heads_rows, grad_branch)
    grad_heads = jnp.dot(grad_branch, w_out.T, preferred_element_type=jnp.float32).astype(
        jnp.bfloat16
    )
    heads_grad = lax.all_to_all(
        grad_heads.reshape(tok_rows, quarters, head_width),
        "head",
        split_axis=1,
        concat_axis=0,
        tiled=True,
    ).reshape(group_rows, head_width)
    grad_packed, grad_local_kernels = attention_back(heads_grad.astype(jnp.float32))
    grad_packed_low = grad_packed.astype(jnp.bfloat16).reshape(group_rows, 3, 1, head_width)
    grad_projected = lax.all_to_all(
        grad_packed_low, "head", split_axis=0, concat_axis=2, tiled=True
    ).reshape(tok_rows, 3 * quarters * head_width)
    grad_wqkv = row_contract(tokens, grad_projected)
    input_grad = (
        grad_first_in + jnp.dot(grad_projected, w_qkv.T, preferred_element_type=jnp.float32)
    ).astype(jnp.bfloat16)
    kernel_full = lax.dynamic_update_slice_in_dim(
        jnp.zeros((head_count, kernel_len), jnp.float32),
        grad_local_kernels,
        quarter * local_heads,
        0,
    )
    small_sums = lax.psum(
        (
            jnp.stack([grad_gain_one, grad_gain_two]),
            jnp.stack([grad_shift_one, grad_shift_two]),
            kernel_full,
        ),
        ("dp", "head"),
    )
    blocked_qkv = to_blocks(grad_wqkv, dp_count, quarters)
    blocked_out = to_blocks(grad_wout, dp_count, quarters)
    blocked_up = to_blocks(grad_up, dp_count, quarters)
    blocked_down = to_blocks(grad_down, dp_count, quarters)
    weight_sums = (
        lax.psum_scatter(blocked_qkv, ("dp", "head"), scatter_dimension=0, tiled=True),
        lax.psum_scatter(blocked_out, ("dp", "head"), scatter_dimension=0, tiled=True),
        lax.psum_scatter(blocked_up, ("dp", "head"), scatter_dimension=0, tiled=True),
        lax.psum_scatter(blocked_down, ("dp", "head"), scatter_dimension=0, tiled=True),
    )
    return (
        output.astype(jnp.bfloat16),
        input_grad,
        weight_sums[0],
        weight_sums[1],
        weight_sums[2],
        weight_sums[3],
        small_sums[0],
        small_sums[1],
        small_sums[2],
    )


def solution(mesh):
    placed = (
        P(("dp", "head"), None),
        P(),
        P(),
        P(),
        P(),
        P(),
        P(),
        P(),
        P("dp"),
        P("dp", None),
        P(("dp", "head"), None),
    )
    aligned = mesh.shape["dp"] == 8 and mesh.shape["head"] == 4
    return jax.shard_map(
        per_device_fast if aligned else per_device,
        mesh=mesh,
        in_specs=placed,
        out_specs=(
            P(("dp", "head"), None),
            P(("dp", "head"), None),
            P("dp", "head"),
            P("dp", "head"),
            P("dp", "head"),
            P("dp", "head"),
            P(),
            P(),
            P(),
        ),
        check_vma=False,
    )
```

```python
import jax
import jax.numpy as jnp
from jax import lax
from jax.sharding import PartitionSpec as P
from jax.experimental import pallas as pl
from jax.experimental.pallas import tpu as pltpu

MESH = pl.DeviceIdType.MESH
NEWTON = 6
F32 = jnp.float32
BF16 = jnp.bfloat16
VMEM = pltpu.VMEM
HEADS_HERE = 3
DIM = 64
TAPS = 33


def mm(a, b, ca, cb):
    return lax.dot_general(a, b, (((ca,), (cb,)), ((), ())), preferred_element_type=F32)


def halves(value):
    high = value.astype(BF16)
    return high, (value - high.astype(F32)).astype(BF16)


def cat(parts, axis):
    return jnp.concatenate(parts, axis=axis)


class Packs:
    def __init__(self):
        lane = lax.broadcasted_iota(jnp.int32, (1, HEADS_HERE * DIM), 1)
        self.hit = [(lane // DIM == h).astype(F32) for h in range(HEADS_HERE)]
        self.low_hit = [h.astype(BF16) for h in self.hit]
        rows = lax.broadcasted_iota(jnp.int32, (DIM, HEADS_HERE * DIM), 0)
        cols = lax.broadcasted_iota(jnp.int32, (DIM, HEADS_HERE * DIM), 1)
        self.unit = (rows == cols % DIM).astype(F32)

    def block(self, low):
        return cat([low * h for h in self.low_hit], 0)

    def times(self, lhs, rhs, side=0):
        rows = lhs.shape[0]
        l_high, l_low = halves(lhs)
        r_high, r_low = halves(rhs)
        both = mm(cat([l_high, l_low], 0), self.block(r_high), 1, side)
        return both[:rows] + both[rows:] + mm(l_high, self.block(r_low), 1, side)

    def diagonal(self, full):
        total = full[:DIM] * self.hit[0]
        for h in range(1, HEADS_HERE):
            total = total + full[DIM * h : DIM * (h + 1)] * self.hit[h]
        return total

    def turn(self, value):
        tall = value.T
        return cat([tall[DIM * h : DIM * (h + 1)] for h in range(HEADS_HERE)], 1)

    def each(self, values):
        total = values[0] * self.hit[0]
        for h in range(1, HEADS_HERE):
            total = total + values[h] * self.hit[h]
        return total

    def row_max(self, value):
        return self.each(
            [
                jnp.max(jnp.where(h > 0, value, -jnp.inf), axis=1, keepdims=True)
                for h in self.hit
            ]
        )

    def row_sum(self, value):
        return self.each([jnp.sum(value * h, axis=1, keepdims=True) for h in self.hit])


def expand(block_low, lhs_side, wide):
    return mm(block_low, wide, lhs_side, 0)


def toeplitz(base):
    rows = jnp.broadcast_to(base, (128, base.shape[1]))
    return pltpu.roll(rows, 0, 1, stride=1, stride_axis=0).astype(BF16)


def windows(mat):
    zero = jnp.zeros((mat.shape[0], 128), mat.dtype)
    wide = cat([zero, mat, zero], 1)
    return cat([wide[:, 128 * b : 128 * b + 384] for b in range(mat.shape[1] // 128)], 0)


def unwindow(stacked, rows):
    return cat([stacked[rows * b : rows * (b + 1)] for b in range(stacked.shape[0] // rows)], 1)


def gelu_pair(hidden):
    tail = jnp.exp(-0.5 * hidden * hidden)
    t = 1.0 / (1.0 + 0.23164190 * jnp.abs(hidden))
    poly = 1.330274429
    for term in (-1.821255978, 1.781477937, -0.356563782, 0.319381530):
        poly = poly * t + term
    density = 0.3989422804014327 * tail
    below = density * poly * t
    normal = jnp.where(hidden >= 0.0, 1.0 - below, below)
    return hidden * normal, normal + hidden * density


def norm_forward(values):
    center = jnp.mean(values, axis=-1, keepdims=True)
    centred = values - center
    spread = jnp.mean(centred * centred, axis=-1, keepdims=True)
    root = lax.rsqrt(spread + 1e-5)
    return centred * root, root


def norm_backward(grad, gain, normed, root):
    scaled = grad * gain
    center = jnp.mean(scaled, axis=-1, keepdims=True)
    along = jnp.mean(scaled * normed, axis=-1, keepdims=True)
    return root * (scaled - center - normed * along)


def copy_to(src, dst, sems, index, device):
    return pltpu.make_async_remote_copy(
        src_ref=src,
        dst_ref=dst,
        send_sem=sems.at[0, index],
        recv_sem=sems.at[1, index],
        device_id=device,
        device_id_type=MESH,
    )


def greet(devices):
    barrier = pltpu.get_barrier_semaphore()
    for device in devices:
        pl.semaphore_signal(barrier, inc=1, device_id=device, device_id_type=MESH)
    pl.semaphore_wait(barrier, len(devices))


class Spread:
    def __init__(self, acc, got, bits, sems, base):
        self.acc, self.got, self.bits, self.sems, self.base = acc, got, bits, sems, base
        self.blocks = acc.shape[0]
        self.stage = 0
        self.offset = 0
        self.at = 0
        self.sent = []

    def start(self):
        bit, device = self.bits[self.stage]
        size = self.blocks >> (self.stage + 1)
        self.keep = self.offset + bit * size
        other = self.offset + (1 - bit) * size
        self.flight = copy_to(
            self.acc.at[pl.ds(other, size)], self.got.at[pl.ds(self.at, size)],
            self.sems, self.base + self.stage, device,
        )
        self.flight.start()
        self.size = size

    def take(self):
        self.flight.wait_recv()
        self.sent.append(self.flight)
        mine, new = pl.ds(self.keep, self.size), pl.ds(self.at, self.size)
        self.at += self.size
        self.offset = self.keep
        self.stage += 1
        if self.stage == len(self.bits):
            return self.acc[mine].astype(F32) + self.got[new].astype(F32)
        self.acc[mine] = self.acc[mine] + self.got[new]
        return None

    def step(self):
        self.take()
        self.start()

    def finish(self):
        total = self.take()
        for sent in self.sent:
            sent.wait_send()
        return total[0]


def position(order, values):
    spot = 0
    for name in order:
        spot = 2 * spot + values[name]
    return spot


DOWN_ORDERS = ("lyxh", "yxlh", "xlyh")
UP_ORDERS = ("ylxh", "xylh", "xylh")
OUT_ORDER = "lyhx"
SUM_ORDER = "chlxy"
QKV_ORDERS = ("ylh", "ylh", "ylh")
SCHEDULE = (
    "DG", "FB", "UG0", "OG", "D0", "D1", "D2", "AV", "S0", "O", "QG2", "S1", "NB1", "U0",
    "D1", "UG1", "NB2", "D2", "UG2", "SM", "S2", "D0", "MM", "O", "QG0", "U0", "QG1", "D1",
    "P2", "S3", "D2", "U1", "O", "P0", "D1", "P2", "P1", "D2", "U2", "P0", "U1", "P2", "D0",
    "P1", "P0", "U2", "U1", "D0", "IN", "P1", "U0", "U2", "S4", "O", "U1", "S5", "U0", "U2",
    "GQ",
)


def main_kernel(
    tok_hbm, grad_hbm, wqkv_hbm, wout_hbm, wup_hbm, wdown_hbm,
    gain_ref, shift_ref, taps_ref, len_ref, bounds_ref,
    out_hbm, in_hbm, gqkv_hbm, gout_hbm, gup_hbm, gdown_hbm, ggain_hbm, gshift_hbm, gtaps_hbm,
    tok, grad_in, w_qkv, w_out, w_up, w_down, lsem, sems,
    everyone, wt, bases, packed, a1, a3, chain, marks, att, heads, heads_x,
    low_t, low_x, act, gst, gst_x, slope, gh, gh_x, gb, gb_x, gatt, g_in, gproj, gp_in,
    first_ref, norm1_ref, gr1_ref, sum_s, sum_r, fin, slots,
    acc_down, got_down, acc_up, got_up, acc_out, got_out, acc_qkv, got_qkv,
    out_v, in_v, gqkv_v, gout_v, gup_v, gdown_v, ggain_v, gshift_v, gtaps_v,
):
    dp = lax.axis_index("dp")
    me = lax.axis_index("head")
    quarters = 4
    rows, width = tok.shape
    slot = rows * quarters
    hidden_width = w_up.shape[1]
    block = hidden_width // quarters
    head_width = width // quarters
    count = DIM
    nh = HEADS_HERE
    band_rows = width // 8
    down_cols = hidden_width // 8
    core = lax.rem(me, 2)
    mate = (dp, me ^ 1)
    bits = {
        "x": (lax.div(me, 2), (dp, me ^ 2)),
        "y": (lax.rem(dp, 2), (dp ^ 1, me)),
        "l": (lax.rem(lax.div(dp, 2), 2), (dp ^ 2, me)),
        "h": (lax.div(dp, 4), (dp ^ 4, me)),
    }
    counter = iter(range(200))
    local = iter(range(40))

    def fetch(src, dst):
        copy = pltpu.make_async_copy(src, dst, lsem.at[next(local)])
        copy.start()
        return copy

    def send(src, dst, device):
        copy = copy_to(src, dst, sems, next(counter), device)
        copy.start()
        return copy

    def reserve(n):
        base = next(counter)
        for _ in range(n - 1):
            next(counter)
        return base

    def spread(acc, got, order):
        return Spread(acc, got, [bits[name] for name in order], sems, reserve(len(order)))

    own_fetch = fetch(tok_hbm, everyone.at[me])
    tok_fetch = fetch(tok_hbm, tok)
    wqkv_fetch = fetch(wqkv_hbm, w_qkv)
    greet([(dp, me ^ k) for k in (1, 2, 3)] + [(dp ^ k, me) for k in (1, 2, 4)])
    half = rows // 2
    far = []
    for piece in range(2):
        part = pl.ds(piece * half, half)
        far.append(send(tok_hbm.at[part], everyone.at[me, part], (dp, me ^ 2)))
    near = send(tok_hbm, everyone.at[me], mate)
    wqkv_fetch.wait()
    wout_fetch = fetch(wout_hbm, w_out)
    wup_fetch = fetch(wup_hbm, w_up)
    wdown_fetch = fetch(wdown_hbm, w_down)
    grad_fetch = fetch(grad_hbm, grad_in)
    odd = lax.rem(me, 2)
    for part in range(3):
        start = pl.multiple_of(part * width + 2 * head_width * lax.div(me, 2) + 128 * odd, 128)
        wt[part] = w_qkv[:, pl.ds(start, 256)].T
    w_own = cat(
        [wt[part, pl.ds(pl.multiple_of(64 * odd, 64), head_width), :] for part in range(3)], 0
    )
    packs = Packs()
    lane = lax.broadcasted_iota(jnp.int32, (TAPS, 384), 1)
    tap = lax.broadcasted_iota(jnp.int32, (TAPS, 384), 0)
    for turn, spots in enumerate((tap + 112, 144 - tap)):
        bases[turn] = mm(taps_ref[...], (lane == spots).astype(F32).astype(BF16), 1, 0)
    bands = [
        [toeplitz(bases[turn, pl.ds(nh * me + h, 1), :]) for h in range(nh)] for turn in range(2)
    ]
    edges = bounds_ref[...].astype(F32)
    low_edge = jnp.broadcast_to(edges[:, :count], (count, count)).T[:, 0:1]
    high_edge = jnp.broadcast_to(edges[:, 1 : count + 1], (count, count)).T[:, 0:1]
    place = lax.broadcasted_iota(jnp.int32, (count, slot), 1).astype(F32)
    member = ((place >= low_edge) & (place < high_edge)).astype(F32).astype(BF16)
    share_of = 1.0 / (high_edge - low_edge)
    length = len_ref[0]
    live = lax.broadcasted_iota(jnp.int32, (1, slot), 1) < length
    scale = DIM ** (-0.25)

    def project(which):
        lanes = pl.ds(pl.multiple_of(rows * which, rows), rows)
        packed[:, lanes] = mm(w_own, everyone[which], 1, 1).astype(BF16)

    own_fetch.wait()
    project(me)
    near.wait()
    project(me ^ 1)
    onward = []
    for piece in range(2):
        part = pl.ds(piece * half, half)
        far[piece].wait()
        onward.append(send(everyone.at[me ^ 2, part], everyone.at[me ^ 2, part], mate))
    project(me ^ 2)
    for copy in onward:
        copy.wait()
    project(me ^ 3)
    queries = packed[:head_width]
    keys = packed[head_width : 2 * head_width]
    q_marks = mm(member, queries, 1, 1) * (scale * share_of)
    k_marks = mm(member, keys, 1, 1) * (scale * share_of)
    marks[0] = q_marks
    marks[1] = k_marks
    scores = packs.times(q_marks, k_marks, 1)
    powers = jnp.exp(scores - packs.row_max(scores))
    middle = powers / packs.row_sum(powers)
    marks[2] = middle
    col_sums = jnp.sum(middle, axis=0, keepdims=True)
    col_top = packs.row_max(col_sums)
    row_top = jnp.max(packs.row_sum(middle), axis=0, keepdims=True)
    inverse_t = middle / (col_top * row_top)
    product = packs.times(inverse_t, middle, 1)
    for step in range(NEWTON):
        second = packs.times(product, product)
        pair = packs.times(cat([product, second], 0), second)
        third, fourth = pair[:count], pair[count:]
        for i, value in enumerate((product, second, third, inverse_t)):
            chain[step, i] = value
        blend = 0.25 * (13.0 * packs.unit - 15.0 * product + 7.0 * second - third)
        product = 0.25 * (13.0 * product - 15.0 * second + 7.0 * third - fourth)
        inverse_t = packs.times(blend, inverse_t)
    marks[3] = inverse_t
    def tall_scores(values, wide):
        high, low = halves(values * scale)
        both = mm(cat([packs.block(high), packs.block(low)], 0), wide, 1, 0)
        return both[:head_width] + both[head_width:]

    def per_head(value):
        return value.reshape(nh, count, slot)

    scores = per_head(tall_scores(k_marks, queries))
    powers = jnp.exp(scores - jnp.max(scores, axis=1, keepdims=True))
    first = (powers * (1.0 / jnp.sum(powers, axis=1, keepdims=True))).reshape(head_width, slot)
    a1[...] = first
    scores = jnp.where(live, tall_scores(q_marks, keys), -1e9)
    powers = jnp.exp(scores - jnp.max(scores, axis=1, keepdims=True))
    third = powers * (1.0 / jnp.sum(powers, axis=1, keepdims=True))
    a3[...] = third
    values = jnp.where(live, packed[2 * head_width :].astype(F32), 0.0).astype(BF16)
    t_high, t_low = halves(third)
    summary_t = packs.diagonal(mm(values, t_high, 1, 1) + mm(values, t_low, 1, 1))
    weights_t = packs.times(summary_t, inverse_t)
    marks[4] = summary_t
    marks[5] = weights_t
    w_high, w_low = halves(weights_t)
    f_high, f_low = halves(first)
    mixed = mm(cat([packs.block(w_high), packs.block(w_low)], 0), f_high, 1, 0)
    mixed = mixed[:head_width] + mixed[head_width:] + mm(packs.block(w_high), f_low, 1, 0)
    for h in range(nh):
        part = slice(DIM * h, DIM * (h + 1))
        conv = unwindow(mm(windows(values[part]), bands[0][h], 1, 1), DIM)
        att[part] = jnp.where(live, mixed[part] + conv, 0.0).astype(BF16)
    mine = pl.ds(pl.multiple_of(rows * me, rows), rows)
    own_rows = pl.ds(pl.multiple_of(head_width * me, 64), head_width)
    att_sent = []
    for k in (2, 3, 1):
        lanes = pl.ds(pl.multiple_of(rows * (me ^ k), rows), rows)
        att_sent.append(send(att.at[:, lanes], heads.at[own_rows], (dp, me ^ k)))
    heads[own_rows] = att[:, mine]
    wout_fetch.wait()
    tok_fetch.wait()
    for copy in att_sent:
        copy.wait()
    heads_sent = send(heads, heads_x, mate)
    branch = mm(heads[...], w_out[...], 0, 0)
    normed, root_one = norm_forward(tok[...].astype(F32) + branch)
    norm1_ref[...] = normed
    first_norm = normed * gain_ref[0:1] + shift_ref[0:1]
    first_ref[...] = first_norm
    low = first_norm.astype(BF16)
    low_t[...] = low.T
    low_sent = send(low_t, low_x, mate)
    wup_fetch.wait()
    wdown_fetch.wait()
    second_sum = None
    act_sent = []
    for i in range(quarters):
        cols = slice(block * i, block * (i + 1))
        active, slope_part = gelu_pair(mm(low, w_up[:, cols], 1, 0))
        active = active.astype(BF16)
        act[:rows, cols] = active
        act_sent.append(send(act.at[:rows, cols], act.at[rows:, cols], mate))
        slope[:, cols] = slope_part
        part = mm(active, w_down[cols, :], 1, 0)
        second_sum = part if second_sum is None else second_sum + part
    normed_two, root_two = norm_forward(first_ref[...] + second_sum)
    out_v[...] = (normed_two * gain_ref[1:2] + shift_ref[1:2]).astype(BF16)
    stores = [fetch(out_v, out_hbm)]
    grad_fetch.wait()
    spot = me * rows + lax.broadcasted_iota(jnp.int32, (rows, 1), 0)
    cotangent = jnp.where(spot < length, grad_in[...].astype(F32), 0.0)
    sum_s[0] = jnp.zeros(sum_s.shape[1:], F32)
    sum_s[0, 1:2] = jnp.sum(cotangent * normed_two, axis=0, keepdims=True)
    sum_s[0, 3:4] = jnp.sum(cotangent, axis=0, keepdims=True)
    g_two = norm_backward(cotangent, gain_ref[1:2], normed_two, root_two)
    gr1_ref[...] = g_two
    g_low = g_two.astype(BF16)
    gst[...] = g_low.T
    gst_sent = send(gst, gst_x, mate)
    for copy in act_sent:
        copy.wait()
    gst_sent.wait()
    s = {}
    downs = [spread(acc_down.at[q], got_down.at[q], DOWN_ORDERS[q]) for q in range(3)]
    ups = [spread(acc_up.at[q], got_up.at[q], UP_ORDERS[q]) for q in range(3)]
    outs = spread(acc_out, got_out, OUT_ORDER)
    projs = [spread(acc_qkv.at[j], got_qkv.at[j], QKV_ORDERS[j]) for j in range(3)]
    sum_base = reserve(5)
    last = reserve(3)
    band_half = band_rows // 2
    p_sent = []

    def folded(total, d):
        top = band_rows * d
        return cat([total[top : top + band_half], total[top + band_half : top + band_rows]], 1)

    def places(x, d):
        return {"x": x, "y": d % 2, "l": d // 2 % 2, "h": d // 4}

    def down_gradient():
        tops = [pl.ds(pl.multiple_of(head_width * (2 * x + core), 64), head_width) for x in (0, 1)]
        lead = cat([cat([gst[top, :], gst_x[top, :]], 1) for top in tops], 0)
        for pair in range(4):
            total = mm(lead, act[:, 2 * down_cols * pair : 2 * down_cols * (pair + 1)], 1, 0)
            total = total.astype(BF16)
            for x in range(2):
                for inner in range(2):
                    at = places(x, 2 * pair + inner)
                    for q in range(3):
                        top = head_width * x + 64 * q
                        acc_down[q, position(DOWN_ORDERS[q], at)] = total[
                            top : top + 64, down_cols * inner : down_cols * (inner + 1)
                        ]
        for chunk in downs:
            chunk.start()

    def forward_back():
        g_first = gr1_ref[...]
        s["gh"] = []
        for i in range(quarters):
            cols = slice(block * i, block * (i + 1))
            part = (slope[:, cols] * mm(g_low, w_down[cols, :], 1, 1)).astype(BF16)
            gh[:, cols] = part
            g_first = g_first + mm(part, w_up[:, cols], 1, 1)
            if i % 2:
                lanes = pl.ds(pl.multiple_of(block * (i - core), 128), block)
                s["gh"].append(send(gh.at[:, lanes], gh_x.at[i // 2], mate))
        normed = norm1_ref[...]
        sum_s[0, 0:1] = jnp.sum(g_first * normed, axis=0, keepdims=True)
        sum_s[0, 2:3] = jnp.sum(g_first, axis=0, keepdims=True)
        g_one = norm_backward(g_first, gain_ref[0:1], normed, root_one)
        gr1_ref[...] = g_one
        g_branch = g_one.astype(BF16)
        gb[...] = g_branch
        gatt[...] = mm(w_out[...], g_branch, 1, 1).astype(BF16)
        s["g"] = []
        for k in (2, 3, 1):
            src = gatt.at[pl.ds(pl.multiple_of(head_width * (me ^ k), 64), head_width)]
            s["g"].append(send(src, g_in.at[:, mine], (dp, me ^ k)))
        s["gb"] = send(gb, gb_x, mate)
        g_in[:, mine] = gatt[own_rows]

    def up_gradient(q):
        if q == 0:
            low_sent.wait()
            for copy in s["gh"]:
                copy.wait()
            s["lead"] = cat([low_t[...], low_x[...]], 1)
        for x in range(2):
            lanes = pl.ds(pl.multiple_of(block * (2 * x + core) + 256 * q, 128), 256)
            side = cat([gh[:, lanes], gh_x[x, :, 256 * q : 256 * (q + 1)]], 0)
            total = mm(s["lead"], side, 1, 0).astype(BF16)
            for d in range(8):
                acc_up[q, position(UP_ORDERS[q], places(x, d))] = total[
                    band_rows * d : band_rows * (d + 1)
                ]
        ups[q].start()

    def out_gradient():
        heads_sent.wait()
        s["gb"].wait()
        lead = cat([heads[...], heads_x[...]], 1)
        both = cat([gb[...], gb_x[...]], 0)
        for x in range(2):
            left_cols = both[:, 2 * head_width * x : 2 * head_width * x + head_width]
            right_cols = both[:, 2 * head_width * x + head_width : 2 * head_width * (x + 1)]
            total = mm(lead, jnp.where(core == 0, left_cols, right_cols), 1, 0).astype(BF16)
            for d in range(8):
                acc_out[position(OUT_ORDER, places(x, d))] = folded(total, d)
        outs.start()

    def share(part):
        own = gproj.at[head_width * part : head_width * (part + 1)]
        dst = pl.ds(pl.multiple_of(width * part + head_width * me, 64), head_width)
        for k in (2, 3, 1):
            lanes = pl.ds(pl.multiple_of(rows * (me ^ k), rows), rows)
            p_sent.append(send(own.at[:, lanes], gp_in.at[dst], (dp, me ^ k)))
        gp_in[dst] = own[:, mine]

    def values_back():
        s["tokens_t"] = everyone[...].reshape(slot, width).T
        for copy in s["g"]:
            copy.wait()
        grad = jnp.where(live, g_in[...].astype(F32), 0.0).astype(BF16)
        values = jnp.where(live, packed[2 * head_width :].astype(F32), 0.0).astype(BF16)
        f_high, f_low = halves(a1[...])
        t_high, t_low = halves(a3[...])
        g_weights = packs.diagonal(mm(f_high, grad, 1, 1) + mm(f_low, grad, 1, 1))
        s_high, s_low = halves(packs.times(marks[3], g_weights))
        g_values = mm(packs.block(s_high), t_high, 0, 0) + mm(packs.block(s_low), t_high, 0, 0)
        g_values = g_values + mm(packs.block(s_high), t_low, 0, 0)
        flip_rows = lax.broadcasted_iota(jnp.int32, (128, 128), 0)
        flip_cols = lax.broadcasted_iota(jnp.int32, (128, 128), 1)
        flip = (flip_rows + flip_cols == 127).astype(F32).astype(BF16)
        for h in range(nh):
            part = slice(DIM * h, DIM * (h + 1))
            g_wide = windows(grad[part])
            total = g_values[part] + unwindow(mm(g_wide, bands[1][h], 1, 1), DIM)
            gproj[2 * head_width + DIM * h : 2 * head_width + DIM * (h + 1)] = jnp.where(
                live, total, 0.0
            ).astype(BF16)
            turned = mm(g_wide[:, 128:256], flip, 1, 0).astype(BF16)
            gram = mm(turned, windows(values[part]), 0, 0)
            gram = pltpu.roll(gram, 384 - 127, 1, stride=1, stride_axis=0)
            found = pltpu.roll(jnp.sum(gram, axis=0, keepdims=True), 384 - 112, 1)
            at = lax.broadcasted_iota(jnp.int32, (1, 128), 1)
            lanes = pl.ds(pl.multiple_of(128 * me, 128), 128)
            sum_s[0, 4 + h : 5 + h, lanes] = jnp.where(at < TAPS, found[:, :128], 0.0)
        s.update(grad=grad, values=values, s_high=s_high, s_low=s_low)
        s["outer"] = packs.times(g_weights, marks[4])
        s["hold"] = jnp.zeros_like(s["outer"])
        share(2)

    def qkv_gradient(part):
        total = mm(s["tokens_t"], gproj[head_width * part : head_width * (part + 1)], 1, 1)
        total = total.astype(BF16)
        for d in range(8):
            acc_qkv[part, position(QKV_ORDERS[part], places(0, d))] = folded(total, d)
        projs[part].start()

    sums = [mate if name == "c" else bits[name][1] for name in SUM_ORDER]

    def sum_step(k):
        if k:
            s["sum"].wait()
            total = sum_s[k - 1] + sum_r[k - 1]
            if k == 5:
                ggain_v[...] = total[0:2]
                gshift_v[...] = total[2:4]
                for n in range(gtaps_v.shape[0]):
                    at = 128 * (n // nh)
                    row = 4 + n % nh
                    gtaps_v[n : n + 1] = total[row : row + 1, at : at + TAPS]
                stores.append(fetch(ggain_v, ggain_hbm))
                stores.append(fetch(gshift_v, gshift_hbm))
                stores.append(fetch(gtaps_v, gtaps_hbm))
                return
            sum_s[k] = total
        s["sum"] = copy_to(sum_s.at[k], sum_r.at[k], sems, sum_base + k, sums[k])
        s["sum"].start()

    def newton_back(steps):
        outer, hold = s["outer"], s["hold"]
        for step in steps:
            product, second, cube, inverse_t = [chain[step, i] for i in range(4)]
            blend = 0.25 * (13.0 * packs.unit - 15.0 * product + 7.0 * second - cube)
            inner = packs.times(inverse_t, outer)
            by_inner = packs.times(cat([product, second], 0), inner)
            zero_th, once, twice = inner, by_inner[:count], by_inner[count:]
            if step < NEWTON - 1:
                by_hold = packs.times(cat([product, second, cube], 0), hold)
                zero_th = zero_th + by_hold[:count]
                once = once + by_hold[count : 2 * count]
                twice = twice + by_hold[2 * count :]
            rest = packs.times(zero_th, 7.0 * product - second - 15.0 * packs.unit)
            rest = rest + packs.times(once, 7.0 * packs.unit - product) - twice
            pair = packs.times(cat([outer, hold], 0), blend)
            outer, hold = pair[:count], pair[count:] + 0.25 * rest
        s["outer"], s["hold"] = outer, hold

    def softmax_back():
        first, third = a1[...], a3[...]
        w_high, w_low = halves(marks[5])
        g_tall = mm(packs.block(w_high), s["grad"], 0, 0) + mm(packs.block(w_low), s["grad"], 0, 0)
        along = jnp.sum(per_head(g_tall * first), axis=1, keepdims=True)
        g_one = first * (per_head(g_tall) - along).reshape(head_width, slot)
        g_tall = mm(cat([packs.block(s["s_high"]), packs.block(s["s_low"])], 0), s["values"], 1, 0)
        g_tall = g_tall[:head_width] + g_tall[head_width:]
        g_three = third * (g_tall - jnp.sum(g_tall * third, axis=1, keepdims=True))

        def tall_marks(high, low, wide):
            both = mm(cat([high, low], 0), wide, 1, 1)
            return packs.diagonal(both[:head_width] + both[head_width:]) * scale

        one_high, one_low = halves(g_one)
        three_high, three_low = halves(g_three)
        s["g_k"] = tall_marks(one_high, one_low, packed[:head_width])
        s["g_q"] = tall_marks(three_high, three_low, packed[head_width : 2 * head_width])
        s["one"], s["three"] = one_high, three_high

    def middle_back():
        q_marks, k_marks, middle = marks[0], marks[1], marks[2]
        outer, hold = s["outer"], s["hold"]
        inverse_t = chain[0, 3]
        col_sums = jnp.sum(middle, axis=0, keepdims=True)
        row_sums = packs.row_sum(middle)
        col_top = packs.row_max(col_sums)
        row_top = jnp.max(row_sums, axis=0, keepdims=True)
        norm = 1.0 / (col_top * row_top)
        g_start_t = packs.turn(outer) + packs.times(packs.turn(hold), middle)
        g_norm = -packs.row_sum(jnp.sum(g_start_t * inverse_t, axis=0, keepdims=True)) * norm
        col_hit = (col_sums == col_top).astype(F32)
        row_hit = (row_sums == row_top).astype(F32)
        col_hit = col_hit / packs.row_sum(col_hit)
        row_hit = row_hit / jnp.sum(row_hit, axis=0, keepdims=True)
        g_middle = packs.times(hold, inverse_t) + g_start_t * norm
        g_middle = g_middle + g_norm * (row_top * col_hit + col_top * row_hit)
        g_two_s = middle * (g_middle - packs.row_sum(g_middle * middle))
        g_q_marks = s["g_q"] + packs.times(g_two_s, k_marks)
        g_k_marks = s["g_k"] + packs.times(packs.turn(g_two_s), q_marks)
        for part, other, g_own, high in (
            (0, k_marks, g_q_marks, s["one"]),
            (1, q_marks, g_k_marks, s["three"]),
        ):
            m_high, m_low = halves(other)
            l_high, l_low = halves(g_own * share_of)
            total = mm(packs.block(m_high), high, 0, 0) + mm(packs.block(m_low), high, 0, 0)
            total = total + mm(cat([l_high, l_low], 0), cat([member, member], 0), 0, 0)
            gproj[head_width * part : head_width * (part + 1)] = (total * scale).astype(BF16)
            share(part)

    def input_gradient():
        wqkv = w_qkv[...]
        for copy in p_sent:
            copy.wait()
        in_v[...] = (gr1_ref[...] + mm(gp_in[...], wqkv, 0, 1)).astype(BF16)
        stores.append(fetch(in_v, in_hbm))

    def finish_down(q):
        gdown_v[64 * q : 64 * (q + 1)] = downs[q].finish()
        s["downs"] = s.get("downs", 0) + 1
        if s["downs"] == 3:
            stores.append(fetch(gdown_v, gdown_hbm))

    def finish_up(q):
        gup_v[:, 256 * q : 256 * (q + 1)] = ups[q].finish()
        s["ups"] = s.get("ups", 0) + 1
        if s["ups"] == 3:
            stores.append(fetch(gup_v, gup_hbm))

    def finish_out():
        total = outs.finish()
        gout_v[:band_half] = total[:, :head_width]
        gout_v[band_half:] = total[:, head_width:]
        stores.append(fetch(gout_v, gout_hbm))

    def finish_proj(part):
        total = projs[part].finish()
        goal = quarters * part + me
        dest, where = lax.div(goal, 3), lax.rem(goal, 3)

        @pl.when(dest == me)
        def _():
            slots[where] = total

        @pl.when(dest != me)
        def _():
            fin[part] = total
            pltpu.make_async_remote_copy(
                src_ref=fin.at[part], dst_ref=slots.at[where],
                send_sem=sems.at[0, last + part], recv_sem=sems.at[1, last + where],
                device_id=(dp, dest), device_id_type=MESH,
            ).start()

    def collect():
        for index in range(3):
            goal = quarters * index + me
            source = lax.rem(3 * me + index, quarters)

            @pl.when(lax.div(goal, 3) != me)
            def _():
                copy_to(fin.at[index], slots.at[0], sems, last + index, mate).wait_send()

            @pl.when(source != me)
            def _():
                copy_to(fin.at[0], slots.at[index], sems, last + index, mate).wait_recv()

        for index in range(3):
            got = slots[index]
            cols = slice(head_width * index, head_width * (index + 1))
            gqkv_v[:band_half, cols] = got[:, :head_width]
            gqkv_v[band_half:, cols] = got[:, head_width:]
        stores.append(fetch(gqkv_v, gqkv_hbm))

    table = {
        "DG": down_gradient, "FB": forward_back, "OG": out_gradient, "AV": values_back,
        "SM": softmax_back, "MM": middle_back, "IN": input_gradient, "GQ": collect,
        "NB1": lambda: newton_back((5, 4, 3)), "NB2": lambda: newton_back((2, 1, 0)),
    }
    for q in range(3):
        table["UG%d" % q] = lambda q=q: up_gradient(q)
        table["QG%d" % q] = lambda q=q: qkv_gradient(q)
    for k in range(6):
        table["S%d" % k] = lambda k=k: sum_step(k)
    names = {"O": (outs, finish_out)}
    for q in range(3):
        names["D%d" % q] = (downs[q], lambda q=q: finish_down(q))
        names["U%d" % q] = (ups[q], lambda q=q: finish_up(q))
        names["P%d" % q] = (projs[q], lambda q=q: finish_proj(q))
    for item in SCHEDULE:
        if item in table:
            table[item]()
        else:
            chunk, finish = names[item]
            if chunk.stage == len(chunk.bits) - 1:
                finish()
            else:
                chunk.step()
    for copy in stores:
        copy.wait()


def final_kernel(*refs):
    sem = refs[-1]
    count = (len(refs) - 1) // 3
    inward = [
        pltpu.make_async_copy(refs[i], refs[2 * count + i], sem.at[0, i]) for i in range(count)
    ]
    outward = [
        pltpu.make_async_copy(refs[2 * count + i], refs[count + i], sem.at[1, i])
        for i in range(count)
    ]
    for copy in inward:
        copy.start()
    for got, put in zip(inward, outward):
        got.wait()
        put.start()
    for copy in outward:
        copy.wait()


def per_device_fast(
    tokens, w_qkv, w_out, w_up, w_down, norm_gains, norm_shifts, conv_kernels, seq_lengths,
    seg_bounds, out_grad,
):
    rows, width = tokens.shape
    ff = w_up.shape[1]
    head_width = width // 4
    slot = 4 * rows
    band, down_cols = width // 8, ff // 8
    whole = pl.BlockSpec(memory_space=VMEM)
    anywhere = pl.BlockSpec(memory_space=pl.ANY)
    shape = jax.ShapeDtypeStruct
    outs = (
        shape((rows, width), BF16),
        shape((rows, width), BF16),
        shape((band, w_qkv.shape[1] // 4), F32),
        shape((band, width // 4), F32),
        shape((band, ff // 4), F32),
        shape((width // 4, down_cols), F32),
        shape(norm_gains.shape, F32),
        shape(norm_shifts.shape, F32),
        shape(conv_kernels.shape, F32),
    )
    found = pl.pallas_call(
        main_kernel,
        out_shape=outs,
        in_specs=[anywhere] * 6
        + [whole] * 3
        + [pl.BlockSpec(memory_space=pltpu.SMEM), whole],
        out_specs=[anywhere] * 9,
        scratch_shapes=[
            VMEM((rows, width), BF16), VMEM((rows, width), BF16),
            VMEM(w_qkv.shape, BF16), VMEM(w_out.shape, BF16),
            VMEM(w_up.shape, BF16), VMEM(w_down.shape, BF16),
            pltpu.SemaphoreType.DMA((32,)), pltpu.SemaphoreType.DMA((2, 120)),
            VMEM((4, rows, width), BF16),
            VMEM((3, 256, width), BF16),
            VMEM((2, conv_kernels.shape[0], 384), F32),
            VMEM((3 * head_width, slot), BF16),
            VMEM((head_width, slot), F32), VMEM((head_width, slot), F32),
            VMEM((NEWTON, 4, DIM, head_width), F32),
            VMEM((6, DIM, head_width), F32),
            VMEM((head_width, slot), BF16),
            VMEM((width, rows), BF16), VMEM((width, rows), BF16),
            VMEM((width, rows), BF16), VMEM((width, rows), BF16),
            VMEM((2 * rows, ff), BF16),
            VMEM((width, rows), BF16), VMEM((width, rows), BF16),
            VMEM((rows, ff), F32),
            VMEM((rows, ff), BF16), VMEM((2, rows, ff // 4), BF16),
            VMEM((rows, width), BF16), VMEM((rows, width), BF16),
            VMEM((width, rows), BF16),
            VMEM((head_width, slot), BF16),
            VMEM((3 * head_width, slot), BF16),
            VMEM((3 * width, rows), BF16),
            VMEM((rows, width), F32), VMEM((rows, width), F32), VMEM((rows, width), F32),
            VMEM((5, 8, width), F32), VMEM((5, 8, width), F32),
            VMEM((3, band // 2, 2 * head_width), F32),
            VMEM((3, band // 2, 2 * head_width), F32),
            VMEM((3, 16, 64, down_cols), BF16), VMEM((3, 15, 64, down_cols), BF16),
            VMEM((3, 16, band, 256), BF16), VMEM((3, 15, band, 256), BF16),
            VMEM((16, band // 2, 2 * head_width), BF16),
            VMEM((15, band // 2, 2 * head_width), BF16),
            VMEM((3, 8, band // 2, 2 * head_width), BF16),
            VMEM((3, 7, band // 2, 2 * head_width), BF16),
        ]
        + [VMEM(out.shape, out.dtype) for out in outs],
        compiler_params=pltpu.CompilerParams(
            collective_id=0, has_side_effects=True, vmem_limit_bytes=63 * 2**20
        ),
        name="main_kernel",
    )(
        tokens, out_grad, w_qkv, w_out, w_up, w_down, norm_gains, norm_shifts, conv_kernels,
        seq_lengths, seg_bounds,
    )
    copied = pl.pallas_call(
        final_kernel,
        out_shape=outs,
        in_specs=[anywhere] * 9,
        out_specs=[anywhere] * 9,
        scratch_shapes=[VMEM(out.shape, out.dtype) for out in outs]
        + [pltpu.SemaphoreType.DMA((2, 9))],
        name="final_kernel",
    )(*found)
    copied = tuple(copied)
    return copied[:5] + (copied[5].T,) + copied[6:]


highest = lax.Precision.HIGHEST
epsilon = 1e-05


def layer_norm(values, gain, shift):
    center = jnp.mean(values, axis=-1, keepdims=True)
    centred = values - center
    spread_sq = jnp.mean(centred * centred, axis=-1, keepdims=True)
    return centred * lax.rsqrt(spread_sq + epsilon) * gain + shift


def exact_gelu(values):
    return jax.nn.gelu(values, approximate=False)


def shifted_conv(values, kernel):
    slot_len = values.shape[0]
    taps = kernel.shape[0]
    half_width = taps // 2
    padded = jnp.pad(values, ((half_width, half_width), (0, 0)))
    total = jnp.zeros_like(values)
    for offset in range(taps):
        total = total + kernel[offset] * padded[offset : offset + slot_len]
    return total


def nystrom_head(queries, keys, values, kernel, length, bounds):
    slot_len = queries.shape[0]
    mark_count = bounds.shape[0] - 1
    head_dim = queries.shape[1]
    places = jnp.arange(slot_len, dtype=jnp.int32)
    valid = places < length
    weight_mask = valid.astype(jnp.float32)[:, None]
    scaling = head_dim ** (-0.25)
    queries = queries * weight_mask * scaling
    keys = keys * weight_mask * scaling
    values = values * weight_mask
    member = ((places[None, :] >= bounds[:-1, None]) & (places[None, :] < bounds[1:, None])).astype(
        jnp.float32
    )
    counts = (bounds[1:] - bounds[:-1]).astype(jnp.float32)[:, None]
    query_marks = jnp.dot(member, queries, precision=highest) / counts
    key_marks = jnp.dot(member, keys, precision=highest) / counts
    first = jax.nn.softmax(jnp.dot(queries, key_marks.T, precision=highest), axis=-1)
    middle = jax.nn.softmax(jnp.dot(query_marks, key_marks.T, precision=highest), axis=-1)
    third_scores = jnp.dot(query_marks, keys.T, precision=highest)
    third = jax.nn.softmax(jnp.where(valid[None, :], third_scores, -1000000000.0), axis=-1)
    inverse = middle.T / (jnp.max(jnp.sum(middle, axis=0)) * jnp.max(jnp.sum(middle, axis=1)))
    identity = jnp.eye(mark_count, dtype=jnp.float32)
    for _ in range(NEWTON):
        product = jnp.dot(middle, inverse, precision=highest)
        inner = 7.0 * identity - product
        inner = 15.0 * identity - jnp.dot(product, inner, precision=highest)
        inner = 13.0 * identity - jnp.dot(product, inner, precision=highest)
        inverse = 0.25 * jnp.dot(inverse, inner, precision=highest)
    summary = jnp.dot(third, values, precision=highest)
    mixed = jnp.dot(first, jnp.dot(inverse, summary, precision=highest), precision=highest)
    return (mixed + shifted_conv(values, kernel)) * weight_mask


def attend(packed, kernels, lengths, bounds):
    seq_count = lengths.shape[0]
    head_count = kernels.shape[0]
    head_dim = packed.shape[-1] // (3 * head_count)
    grouped = packed.reshape(seq_count, -1, 3, head_count, head_dim)
    over_heads = jax.vmap(nystrom_head, in_axes=(1, 1, 1, 0, None, None), out_axes=1)
    over_seqs = jax.vmap(over_heads, in_axes=(0, 0, 0, None, 0, 0))
    result = over_seqs(
        grouped[:, :, 0], grouped[:, :, 1], grouped[:, :, 2], kernels, lengths, bounds
    )
    return result.reshape(seq_count * grouped.shape[1], head_count * head_dim)


def row_contract(left, right):
    return lax.dot_general(
        left, right, (((0,), (0,)), ((), ())), preferred_element_type=jnp.float32
    )


def to_blocks(matrix, dp_count, quarters):
    total_rows, total_cols = matrix.shape
    shaped = matrix.reshape(dp_count, total_rows // dp_count, quarters, total_cols // quarters)
    return shaped.transpose(0, 2, 1, 3).reshape(total_rows * quarters, total_cols // quarters)


def per_device(
    tokens,
    w_qkv,
    w_out,
    w_up,
    w_down,
    norm_gains,
    norm_shifts,
    conv_kernels,
    seq_lengths,
    seg_bounds,
    out_grad,
):
    quarters = lax.axis_size("head")
    quarter = lax.axis_index("head")
    dp_count = lax.axis_size("dp")
    tok_rows, width = tokens.shape
    seq_count = seq_lengths.shape[0]
    group_rows = tok_rows * quarters
    slot_len = group_rows // seq_count
    head_count, kernel_len = conv_kernels.shape
    local_heads = head_count // quarters
    head_width = w_qkv.shape[1] // (3 * quarters)
    places = quarter * tok_rows + jnp.arange(tok_rows, dtype=jnp.int32)
    owners = places // slot_len
    within = places % slot_len
    limits = jnp.sum(
        jnp.where(
            owners[:, None] == jnp.arange(seq_count, dtype=jnp.int32)[None, :],
            seq_lengths[None, :],
            0,
        ),
        axis=1,
    )
    live = (within < limits).astype(jnp.float32)[:, None]
    local_kernels = lax.dynamic_slice_in_dim(
        conv_kernels.astype(jnp.float32), quarter * local_heads, local_heads, 0
    )
    projected = jnp.dot(tokens, w_qkv, preferred_element_type=jnp.float32).astype(jnp.bfloat16)
    packed = lax.all_to_all(
        projected.reshape(tok_rows, 3, quarters, head_width),
        "head",
        split_axis=2,
        concat_axis=0,
        tiled=True,
    )
    packed_rows = packed.reshape(group_rows, 3 * head_width)

    def attention_piece(packed_in, kernel_in):
        return attend(packed_in, kernel_in, seq_lengths, seg_bounds)

    attended, attention_back = jax.vjp(
        attention_piece, packed_rows.astype(jnp.float32), local_kernels
    )
    attended_low = attended.astype(jnp.bfloat16)
    heads_rows = lax.all_to_all(
        attended_low.reshape(group_rows, 1, head_width),
        "head",
        split_axis=0,
        concat_axis=1,
        tiled=True,
    ).reshape(tok_rows, width)
    branch = jnp.dot(heads_rows, w_out, preferred_element_type=jnp.float32)
    first_in = tokens.astype(jnp.float32) + branch
    first_norm, first_back = jax.vjp(layer_norm, first_in, norm_gains[0], norm_shifts[0])
    first_low = first_norm.astype(jnp.bfloat16)
    hidden = jnp.dot(first_low, w_up, preferred_element_type=jnp.float32)
    activated, gelu_back = jax.vjp(exact_gelu, hidden)
    act_low = activated.astype(jnp.bfloat16)
    second = jnp.dot(act_low, w_down, preferred_element_type=jnp.float32)
    output, second_back = jax.vjp(layer_norm, first_norm + second, norm_gains[1], norm_shifts[1])
    cotangent = out_grad.astype(jnp.float32) * live
    grad_second_in, grad_gain_two, grad_shift_two = second_back(cotangent)
    grad_second = grad_second_in.astype(jnp.bfloat16)
    grad_down = row_contract(act_low, grad_second)
    grad_act = jnp.dot(grad_second, w_down.T, preferred_element_type=jnp.float32)
    grad_hidden = gelu_back(grad_act)[0].astype(jnp.bfloat16)
    grad_up = row_contract(first_low, grad_hidden)
    grad_first = grad_second_in + jnp.dot(grad_hidden, w_up.T, preferred_element_type=jnp.float32)
    grad_first_in, grad_gain_one, grad_shift_one = first_back(grad_first)
    grad_branch = grad_first_in.astype(jnp.bfloat16)
    grad_wout = row_contract(heads_rows, grad_branch)
    grad_heads = jnp.dot(grad_branch, w_out.T, preferred_element_type=jnp.float32).astype(
        jnp.bfloat16
    )
    heads_grad = lax.all_to_all(
        grad_heads.reshape(tok_rows, quarters, head_width),
        "head",
        split_axis=1,
        concat_axis=0,
        tiled=True,
    ).reshape(group_rows, head_width)
    grad_packed, grad_local_kernels = attention_back(heads_grad.astype(jnp.float32))
    grad_packed_low = grad_packed.astype(jnp.bfloat16).reshape(group_rows, 3, 1, head_width)
    grad_projected = lax.all_to_all(
        grad_packed_low, "head", split_axis=0, concat_axis=2, tiled=True
    ).reshape(tok_rows, 3 * quarters * head_width)
    grad_wqkv = row_contract(tokens, grad_projected)
    input_grad = (
        grad_first_in + jnp.dot(grad_projected, w_qkv.T, preferred_element_type=jnp.float32)
    ).astype(jnp.bfloat16)
    kernel_full = lax.dynamic_update_slice_in_dim(
        jnp.zeros((head_count, kernel_len), jnp.float32),
        grad_local_kernels,
        quarter * local_heads,
        0,
    )
    small_sums = lax.psum(
        (
            jnp.stack([grad_gain_one, grad_gain_two]),
            jnp.stack([grad_shift_one, grad_shift_two]),
            kernel_full,
        ),
        ("dp", "head"),
    )
    blocked_qkv = to_blocks(grad_wqkv, dp_count, quarters)
    blocked_out = to_blocks(grad_wout, dp_count, quarters)
    blocked_up = to_blocks(grad_up, dp_count, quarters)
    blocked_down = to_blocks(grad_down, dp_count, quarters)
    weight_sums = (
        lax.psum_scatter(blocked_qkv, ("dp", "head"), scatter_dimension=0, tiled=True),
        lax.psum_scatter(blocked_out, ("dp", "head"), scatter_dimension=0, tiled=True),
        lax.psum_scatter(blocked_up, ("dp", "head"), scatter_dimension=0, tiled=True),
        lax.psum_scatter(blocked_down, ("dp", "head"), scatter_dimension=0, tiled=True),
    )
    return (
        output.astype(jnp.bfloat16),
        input_grad,
        weight_sums[0],
        weight_sums[1],
        weight_sums[2],
        weight_sums[3],
        small_sums[0],
        small_sums[1],
        small_sums[2],
    )


def solution(mesh):
    placed = (
        P(("dp", "head"), None),
        P(),
        P(),
        P(),
        P(),
        P(),
        P(),
        P(),
        P("dp"),
        P("dp", None),
        P(("dp", "head"), None),
    )
    aligned = mesh.shape["dp"] == 8 and mesh.shape["head"] == 4
    return jax.shard_map(
        per_device_fast if aligned else per_device,
        mesh=mesh,
        in_specs=placed,
        out_specs=(
            P(("dp", "head"), None),
            P(("dp", "head"), None),
            P("dp", "head"),
            P("dp", "head"),
            P("dp", "head"),
            P("dp", "head"),
            P(),
            P(),
            P(),
        ),
        check_vma=False,
    )
```

```python
import jax
import jax.numpy as jnp
from jax import lax
from jax.sharding import PartitionSpec as P
from jax.experimental import pallas as pl
from jax.experimental.pallas import tpu as pltpu

MESH = pl.DeviceIdType.MESH
NEWTON = 6
F32 = jnp.float32
BF16 = jnp.bfloat16
VMEM = pltpu.VMEM
HEADS_HERE = 3
DIM = 64
TAPS = 33


def mm(a, b, ca, cb):
    return lax.dot_general(a, b, (((ca,), (cb,)), ((), ())), preferred_element_type=F32)


def halves(value):
    high = value.astype(BF16)
    return high, (value - high.astype(F32)).astype(BF16)


def cat(parts, axis):
    return jnp.concatenate(parts, axis=axis)


class Packs:
    def __init__(self):
        lane = lax.broadcasted_iota(jnp.int32, (1, HEADS_HERE * DIM), 1)
        self.hit = [(lane // DIM == h).astype(F32) for h in range(HEADS_HERE)]
        self.low_hit = [h.astype(BF16) for h in self.hit]
        rows = lax.broadcasted_iota(jnp.int32, (DIM, HEADS_HERE * DIM), 0)
        cols = lax.broadcasted_iota(jnp.int32, (DIM, HEADS_HERE * DIM), 1)
        self.unit = (rows == cols % DIM).astype(F32)

    def block(self, low):
        return cat([low * h for h in self.low_hit], 0)

    def times(self, lhs, rhs, side=0):
        rows = lhs.shape[0]
        l_high, l_low = halves(lhs)
        r_high, r_low = halves(rhs)
        both = mm(cat([l_high, l_low], 0), self.block(r_high), 1, side)
        return both[:rows] + both[rows:] + mm(l_high, self.block(r_low), 1, side)

    def diagonal(self, full):
        total = full[:DIM] * self.hit[0]
        for h in range(1, HEADS_HERE):
            total = total + full[DIM * h : DIM * (h + 1)] * self.hit[h]
        return total

    def turn(self, value):
        tall = value.T
        return cat([tall[DIM * h : DIM * (h + 1)] for h in range(HEADS_HERE)], 1)

    def each(self, values):
        total = values[0] * self.hit[0]
        for h in range(1, HEADS_HERE):
            total = total + values[h] * self.hit[h]
        return total

    def row_max(self, value):
        return self.each(
            [
                jnp.max(jnp.where(h > 0, value, -jnp.inf), axis=1, keepdims=True)
                for h in self.hit
            ]
        )

    def row_sum(self, value):
        return self.each([jnp.sum(value * h, axis=1, keepdims=True) for h in self.hit])


def expand(block_low, lhs_side, wide):
    return mm(block_low, wide, lhs_side, 0)


def toeplitz(base):
    rows = jnp.broadcast_to(base, (128, base.shape[1]))
    return pltpu.roll(rows, 0, 1, stride=1, stride_axis=0).astype(BF16)


def windows(mat):
    zero = jnp.zeros((mat.shape[0], 128), mat.dtype)
    wide = cat([zero, mat, zero], 1)
    return cat([wide[:, 128 * b : 128 * b + 384] for b in range(mat.shape[1] // 128)], 0)


def unwindow(stacked, rows):
    return cat([stacked[rows * b : rows * (b + 1)] for b in range(stacked.shape[0] // rows)], 1)


def gelu_pair(hidden):
    tail = jnp.exp(-0.5 * hidden * hidden)
    t = 1.0 / (1.0 + 0.23164190 * jnp.abs(hidden))
    poly = 1.330274429
    for term in (-1.821255978, 1.781477937, -0.356563782, 0.319381530):
        poly = poly * t + term
    density = 0.3989422804014327 * tail
    below = density * poly * t
    normal = jnp.where(hidden >= 0.0, 1.0 - below, below)
    return hidden * normal, normal + hidden * density


def norm_forward(values):
    center = jnp.mean(values, axis=-1, keepdims=True)
    centred = values - center
    spread = jnp.mean(centred * centred, axis=-1, keepdims=True)
    root = lax.rsqrt(spread + 1e-5)
    return centred * root, root


def norm_backward(grad, gain, normed, root):
    scaled = grad * gain
    center = jnp.mean(scaled, axis=-1, keepdims=True)
    along = jnp.mean(scaled * normed, axis=-1, keepdims=True)
    return root * (scaled - center - normed * along)


def copy_to(src, dst, sems, index, device):
    return pltpu.make_async_remote_copy(
        src_ref=src,
        dst_ref=dst,
        send_sem=sems.at[0, index],
        recv_sem=sems.at[1, index],
        device_id=device,
        device_id_type=MESH,
    )


def greet(devices):
    barrier = pltpu.get_barrier_semaphore()
    for device in devices:
        pl.semaphore_signal(barrier, inc=1, device_id=device, device_id_type=MESH)
    pl.semaphore_wait(barrier, len(devices))


class Spread:
    def __init__(self, acc, got, bits, sems, base):
        self.acc, self.got, self.bits, self.sems, self.base = acc, got, bits, sems, base
        self.blocks = acc.shape[0]
        self.stage = 0
        self.offset = 0
        self.at = 0
        self.sent = []

    def start(self):
        bit, device = self.bits[self.stage]
        size = self.blocks >> (self.stage + 1)
        self.keep = self.offset + bit * size
        other = self.offset + (1 - bit) * size
        self.flight = copy_to(
            self.acc.at[pl.ds(other, size)], self.got.at[pl.ds(self.at, size)],
            self.sems, self.base + self.stage, device,
        )
        self.flight.start()
        self.size = size

    def take(self):
        self.flight.wait_recv()
        self.sent.append(self.flight)
        mine, new = pl.ds(self.keep, self.size), pl.ds(self.at, self.size)
        self.at += self.size
        self.offset = self.keep
        self.stage += 1
        if self.stage == len(self.bits):
            return self.acc[mine].astype(F32) + self.got[new].astype(F32)
        self.acc[mine] = self.acc[mine] + self.got[new]
        return None

    def step(self):
        self.take()
        self.start()

    def finish(self):
        total = self.take()
        for sent in self.sent:
            sent.wait_send()
        return total[0]


def position(order, values):
    spot = 0
    for name in order:
        spot = 2 * spot + values[name]
    return spot


DOWN_ORDERS = ("lyxh", "lxyh", "yxlh")
UP_ORDERS = ("lyh", "ylh", "ylh")
OUT_ORDER = "xylh"
SUM_ORDER = "hlxyc"
QKV_ORDERS = ("ylh", "ylh", "ylh")
SCHEDULE = (
    "DG", "LF", "FB", "D0", "D2", "GF", "UH", "UG0", "OG", "UG1", "D0", "AV", "S0", "D1",
    "D2", "NB1", "SM", "U0", "S1", "U1", "QG2", "NB2", "D2", "O", "MM", "D0", "S2", "U1",
    "U0", "QG0", "QG1", "D2", "UG2", "P2", "D0", "O", "U1", "D1", "U0", "P0", "P2", "O", "P1",
    "P0", "P2", "IN", "U2", "S3", "O", "P1", "D1", "P0", "S4", "U2", "S5", "P1", "D1", "U2",
    "GQ",
)


def main_kernel(
    tok_hbm, grad_hbm, wqkv_hbm, wout_hbm, wup_hbm, wdown_hbm,
    gain_ref, shift_ref, taps_ref, len_ref, bounds_ref,
    out_hbm, in_hbm, gqkv_hbm, gout_hbm, gup_hbm, gdown_hbm, ggain_hbm, gshift_hbm, gtaps_hbm,
    tok, grad_in, w_qkv, w_out, w_up, w_down, lsem, sems,
    everyone, wt, bases, packed, a1, a3, chain, marks, att, heads, heads_x,
    low_all, g2_all, act, gst, gst_x, slope, gh, gb, gb_x, gatt, g_in, gproj, gp_in,
    first_ref, norm1_ref, gr1_ref, sum_s, sum_r, fin, slots,
    acc_down, got_down, acc_up, got_up, acc_out, got_out, acc_qkv, got_qkv,
    out_v, in_v, gqkv_v, gout_v, gup_v, gdown_v, ggain_v, gshift_v, gtaps_v,
):
    dp = lax.axis_index("dp")
    me = lax.axis_index("head")
    quarters = 4
    rows, width = tok.shape
    slot = rows * quarters
    hidden_width = w_up.shape[1]
    block = hidden_width // quarters
    head_width = width // quarters
    count = DIM
    nh = HEADS_HERE
    band_rows = width // 8
    down_cols = hidden_width // 8
    core = lax.rem(me, 2)
    mate = (dp, me ^ 1)
    bits = {
        "x": (lax.div(me, 2), (dp, me ^ 2)),
        "y": (lax.rem(dp, 2), (dp ^ 1, me)),
        "l": (lax.rem(lax.div(dp, 2), 2), (dp ^ 2, me)),
        "h": (lax.div(dp, 4), (dp ^ 4, me)),
    }
    counter = iter(range(200))
    local = iter(range(40))

    def fetch(src, dst):
        copy = pltpu.make_async_copy(src, dst, lsem.at[next(local)])
        copy.start()
        return copy

    def send(src, dst, device):
        copy = copy_to(src, dst, sems, next(counter), device)
        copy.start()
        return copy

    def reserve(n):
        base = next(counter)
        for _ in range(n - 1):
            next(counter)
        return base

    def spread(acc, got, order):
        return Spread(acc, got, [bits[name] for name in order], sems, reserve(len(order)))

    own_fetch = fetch(tok_hbm, everyone.at[me])
    tok_fetch = fetch(tok_hbm, tok)
    wqkv_fetch = fetch(wqkv_hbm, w_qkv)
    greet([(dp, me ^ k) for k in (1, 2, 3)] + [(dp ^ k, me) for k in (1, 2, 4)])
    half = rows // 2
    far = []
    for piece in range(2):
        part = pl.ds(piece * half, half)
        far.append(send(tok_hbm.at[part], everyone.at[me, part], (dp, me ^ 2)))
    near = send(tok_hbm, everyone.at[me], mate)
    wqkv_fetch.wait()
    wout_fetch = fetch(wout_hbm, w_out)
    wup_fetch = fetch(wup_hbm, w_up)
    wdown_fetch = fetch(wdown_hbm, w_down)
    grad_fetch = fetch(grad_hbm, grad_in)
    odd = lax.rem(me, 2)
    for part in range(3):
        start = pl.multiple_of(part * width + 2 * head_width * lax.div(me, 2) + 128 * odd, 128)
        wt[part] = w_qkv[:, pl.ds(start, 256)].T
    w_own = cat(
        [wt[part, pl.ds(pl.multiple_of(64 * odd, 64), head_width), :] for part in range(3)], 0
    )
    packs = Packs()
    lane = lax.broadcasted_iota(jnp.int32, (TAPS, 384), 1)
    tap = lax.broadcasted_iota(jnp.int32, (TAPS, 384), 0)
    for turn, spots in enumerate((tap + 112, 144 - tap)):
        bases[turn] = mm(taps_ref[...], (lane == spots).astype(F32).astype(BF16), 1, 0)
    bands = [
        [toeplitz(bases[turn, pl.ds(nh * me + h, 1), :]) for h in range(nh)] for turn in range(2)
    ]
    edges = bounds_ref[...].astype(F32)
    low_edge = jnp.broadcast_to(edges[:, :count], (count, count)).T[:, 0:1]
    high_edge = jnp.broadcast_to(edges[:, 1 : count + 1], (count, count)).T[:, 0:1]
    place = lax.broadcasted_iota(jnp.int32, (count, slot), 1).astype(F32)
    member = ((place >= low_edge) & (place < high_edge)).astype(F32).astype(BF16)
    share_of = 1.0 / (high_edge - low_edge)
    length = len_ref[0]
    live = lax.broadcasted_iota(jnp.int32, (1, slot), 1) < length
    scale = DIM ** (-0.25)

    def project(which):
        lanes = pl.ds(pl.multiple_of(rows * which, rows), rows)
        packed[:, lanes] = mm(w_own, everyone[which], 1, 1).astype(BF16)

    own_fetch.wait()
    project(me)
    near.wait()
    project(me ^ 1)
    onward = []
    for piece in range(2):
        part = pl.ds(piece * half, half)
        far[piece].wait()
        onward.append(send(everyone.at[me ^ 2, part], everyone.at[me ^ 2, part], mate))
    project(me ^ 2)
    for copy in onward:
        copy.wait()
    project(me ^ 3)
    queries = packed[:head_width]
    keys = packed[head_width : 2 * head_width]
    q_marks = mm(member, queries, 1, 1) * (scale * share_of)
    k_marks = mm(member, keys, 1, 1) * (scale * share_of)
    marks[0] = q_marks
    marks[1] = k_marks
    scores = packs.times(q_marks, k_marks, 1)
    powers = jnp.exp(scores - packs.row_max(scores))
    middle = powers / packs.row_sum(powers)
    marks[2] = middle
    col_sums = jnp.sum(middle, axis=0, keepdims=True)
    col_top = packs.row_max(col_sums)
    row_top = jnp.max(packs.row_sum(middle), axis=0, keepdims=True)
    inverse_t = middle / (col_top * row_top)
    product = packs.times(inverse_t, middle, 1)
    for step in range(NEWTON):
        second = packs.times(product, product)
        pair = packs.times(cat([product, second], 0), second)
        third, fourth = pair[:count], pair[count:]
        for i, value in enumerate((product, second, third, inverse_t)):
            chain[step, i] = value
        blend = 0.25 * (13.0 * packs.unit - 15.0 * product + 7.0 * second - third)
        product = 0.25 * (13.0 * product - 15.0 * second + 7.0 * third - fourth)
        inverse_t = packs.times(blend, inverse_t)
    marks[3] = inverse_t
    def tall_scores(values, wide):
        high, low = halves(values * scale)
        both = mm(cat([packs.block(high), packs.block(low)], 0), wide, 1, 0)
        return both[:head_width] + both[head_width:]

    def per_head(value):
        return value.reshape(nh, count, slot)

    scores = per_head(tall_scores(k_marks, queries))
    powers = jnp.exp(scores - jnp.max(scores, axis=1, keepdims=True))
    first = (powers * (1.0 / jnp.sum(powers, axis=1, keepdims=True))).reshape(head_width, slot)
    a1[...] = first
    scores = jnp.where(live, tall_scores(q_marks, keys), -1e9)
    powers = jnp.exp(scores - jnp.max(scores, axis=1, keepdims=True))
    third = powers * (1.0 / jnp.sum(powers, axis=1, keepdims=True))
    a3[...] = third
    values = jnp.where(live, packed[2 * head_width :].astype(F32), 0.0).astype(BF16)
    t_high, t_low = halves(third)
    summary_t = packs.diagonal(mm(values, t_high, 1, 1) + mm(values, t_low, 1, 1))
    weights_t = packs.times(summary_t, inverse_t)
    marks[4] = summary_t
    marks[5] = weights_t
    w_high, w_low = halves(weights_t)
    f_high, f_low = halves(first)
    mixed = mm(cat([packs.block(w_high), packs.block(w_low)], 0), f_high, 1, 0)
    mixed = mixed[:head_width] + mixed[head_width:] + mm(packs.block(w_high), f_low, 1, 0)
    for h in range(nh):
        part = slice(DIM * h, DIM * (h + 1))
        conv = unwindow(mm(windows(values[part]), bands[0][h], 1, 1), DIM)
        att[part] = jnp.where(live, mixed[part] + conv, 0.0).astype(BF16)
    mine = pl.ds(pl.multiple_of(rows * me, rows), rows)
    own_rows = pl.ds(pl.multiple_of(head_width * me, 64), head_width)
    att_sent = []
    for k in (2, 3, 1):
        lanes = pl.ds(pl.multiple_of(rows * (me ^ k), rows), rows)
        att_sent.append(send(att.at[:, lanes], heads.at[own_rows], (dp, me ^ k)))
    heads[own_rows] = att[:, mine]
    wout_fetch.wait()
    tok_fetch.wait()
    for copy in att_sent:
        copy.wait()
    heads_sent = send(heads, heads_x, mate)
    branch = mm(heads[...], w_out[...], 0, 0)
    normed, root_one = norm_forward(tok[...].astype(F32) + branch)
    norm1_ref[...] = normed
    first_norm = normed * gain_ref[0:1] + shift_ref[0:1]
    first_ref[...] = first_norm
    low = first_norm.astype(BF16)
    low_all[me] = low
    low_far = send(low_all.at[me], low_all.at[me], (dp, me ^ 2))
    low_near = send(low_all.at[me], low_all.at[me], mate)
    wup_fetch.wait()
    wdown_fetch.wait()
    second_sum = None
    act_sent = []
    for i in range(quarters):
        cols = slice(block * i, block * (i + 1))
        active, slope_part = gelu_pair(mm(low, w_up[:, cols], 1, 0))
        active = active.astype(BF16)
        act[:rows, cols] = active
        act_sent.append(send(act.at[:rows, cols], act.at[rows:, cols], mate))
        slope[:, cols] = slope_part
        part = mm(active, w_down[cols, :], 1, 0)
        second_sum = part if second_sum is None else second_sum + part
    normed_two, root_two = norm_forward(first_ref[...] + second_sum)
    out_v[...] = (normed_two * gain_ref[1:2] + shift_ref[1:2]).astype(BF16)
    stores = [fetch(out_v, out_hbm)]
    grad_fetch.wait()
    spot = me * rows + lax.broadcasted_iota(jnp.int32, (rows, 1), 0)
    cotangent = jnp.where(spot < length, grad_in[...].astype(F32), 0.0)
    sum_s[0] = jnp.zeros(sum_s.shape[1:], F32)
    sum_s[0, 1:2] = jnp.sum(cotangent * normed_two, axis=0, keepdims=True)
    sum_s[0, 3:4] = jnp.sum(cotangent, axis=0, keepdims=True)
    g_two = norm_backward(cotangent, gain_ref[1:2], normed_two, root_two)
    gr1_ref[...] = g_two
    g_low = g_two.astype(BF16)
    g2_all[me] = g_low
    g2_far = send(g2_all.at[me], g2_all.at[me], (dp, me ^ 2))
    g2_near = send(g2_all.at[me], g2_all.at[me], mate)
    gst[...] = g_low.T
    gst_sent = send(gst, gst_x, mate)
    for copy in act_sent:
        copy.wait()
    gst_sent.wait()
    s = {}
    downs = [spread(acc_down.at[q], got_down.at[q], DOWN_ORDERS[q]) for q in range(3)]
    ups = [spread(acc_up.at[q], got_up.at[q], UP_ORDERS[q]) for q in range(3)]
    outs = spread(acc_out, got_out, OUT_ORDER)
    projs = [spread(acc_qkv.at[j], got_qkv.at[j], QKV_ORDERS[j]) for j in range(3)]
    sum_base = reserve(5)
    last = reserve(3)
    band_half = band_rows // 2
    p_sent = []

    def folded(total, d):
        top = band_rows * d
        return cat([total[top : top + band_half], total[top + band_half : top + band_rows]], 1)

    def places(x, d):
        return {"x": x, "y": d % 2, "l": d // 2 % 2, "h": d // 4}

    def down_gradient():
        tops = [pl.ds(pl.multiple_of(head_width * (2 * x + core), 64), head_width) for x in (0, 1)]
        lead = cat([cat([gst[top, :], gst_x[top, :]], 1) for top in tops], 0)
        for pair in range(4):
            total = mm(lead, act[:, 2 * down_cols * pair : 2 * down_cols * (pair + 1)], 1, 0)
            total = total.astype(BF16)
            for x in range(2):
                for inner in range(2):
                    at = places(x, 2 * pair + inner)
                    for q in range(3):
                        top = head_width * x + 64 * q
                        acc_down[q, position(DOWN_ORDERS[q], at)] = total[
                            top : top + 64, down_cols * inner : down_cols * (inner + 1)
                        ]
        for chunk in downs:
            chunk.start()

    def forward_back():
        g_first = gr1_ref[...]
        for i in range(quarters):
            cols = slice(block * i, block * (i + 1))
            part = (slope[:, cols] * mm(g_low, w_down[cols, :], 1, 1)).astype(BF16)
            g_first = g_first + mm(part, w_up[:, cols], 1, 1)
        normed = norm1_ref[...]
        sum_s[0, 0:1] = jnp.sum(g_first * normed, axis=0, keepdims=True)
        sum_s[0, 2:3] = jnp.sum(g_first, axis=0, keepdims=True)
        g_one = norm_backward(g_first, gain_ref[0:1], normed, root_one)
        gr1_ref[...] = g_one
        g_branch = g_one.astype(BF16)
        gb[...] = g_branch
        gatt[...] = mm(w_out[...], g_branch, 1, 1).astype(BF16)
        s["g"] = []
        for k in (2, 3, 1):
            src = gatt.at[pl.ds(pl.multiple_of(head_width * (me ^ k), 64), head_width)]
            s["g"].append(send(src, g_in.at[:, mine], (dp, me ^ k)))
        s["gb"] = send(gb, gb_x, mate)
        g_in[:, mine] = gatt[own_rows]

    own_cols = pl.ds(pl.multiple_of(block * me, 128), block)

    def low_onward():
        low_far.wait()
        s["low"] = send(low_all.at[me ^ 2], low_all.at[me ^ 2], mate)

    def g2_onward():
        g2_far.wait()
        s["g2"] = send(g2_all.at[me ^ 2], g2_all.at[me ^ 2], mate)

    def up_slopes():
        low_near.wait()
        s["low"].wait()
        side = w_up[:, own_cols]
        for b in range(quarters):
            hidden = mm(low_all[b], side, 1, 0)
            slope[:, block * b : block * (b + 1)] = gelu_pair(hidden)[1]
        s["low_t"] = low_all[...].reshape(slot, width).T

    def up_gradient(q):
        if q == 0:
            g2_near.wait()
            s["g2"].wait()
            side = w_down[own_cols, :]
            for b in range(quarters):
                cols = slice(block * b, block * (b + 1))
                gh[:, cols] = (slope[:, cols] * mm(g2_all[b], side, 1, 1)).astype(BF16)
        side = cat([gh[:, block * b + 256 * q : block * b + 256 * (q + 1)] for b in range(4)], 0)
        total = mm(s["low_t"], side, 1, 0).astype(BF16)
        for d in range(8):
            acc_up[q, position(UP_ORDERS[q], places(0, d))] = total[
                band_rows * d : band_rows * (d + 1)
            ]
        ups[q].start()

    def out_gradient():
        heads_sent.wait()
        s["gb"].wait()
        lead = cat([heads[...], heads_x[...]], 1)
        both = cat([gb[...], gb_x[...]], 0)
        for x in range(2):
            left_cols = both[:, 2 * head_width * x : 2 * head_width * x + head_width]
            right_cols = both[:, 2 * head_width * x + head_width : 2 * head_width * (x + 1)]
            total = mm(lead, jnp.where(core == 0, left_cols, right_cols), 1, 0).astype(BF16)
            for d in range(8):
                acc_out[position(OUT_ORDER, places(x, d))] = folded(total, d)
        outs.start()

    def share(part):
        own = gproj.at[head_width * part : head_width * (part + 1)]
        dst = pl.ds(pl.multiple_of(width * part + head_width * me, 64), head_width)
        for k in (2, 3, 1):
            lanes = pl.ds(pl.multiple_of(rows * (me ^ k), rows), rows)
            p_sent.append(send(own.at[:, lanes], gp_in.at[dst], (dp, me ^ k)))
        gp_in[dst] = own[:, mine]

    def values_back():
        s["tokens_t"] = everyone[...].reshape(slot, width).T
        for copy in s["g"]:
            copy.wait()
        grad = jnp.where(live, g_in[...].astype(F32), 0.0).astype(BF16)
        values = jnp.where(live, packed[2 * head_width :].astype(F32), 0.0).astype(BF16)
        f_high, f_low = halves(a1[...])
        t_high, t_low = halves(a3[...])
        g_weights = packs.diagonal(mm(f_high, grad, 1, 1) + mm(f_low, grad, 1, 1))
        s_high, s_low = halves(packs.times(marks[3], g_weights))
        g_values = mm(packs.block(s_high), t_high, 0, 0) + mm(packs.block(s_low), t_high, 0, 0)
        g_values = g_values + mm(packs.block(s_high), t_low, 0, 0)
        flip_rows = lax.broadcasted_iota(jnp.int32, (128, 128), 0)
        flip_cols = lax.broadcasted_iota(jnp.int32, (128, 128), 1)
        flip = (flip_rows + flip_cols == 127).astype(F32).astype(BF16)
        for h in range(nh):
            part = slice(DIM * h, DIM * (h + 1))
            g_wide = windows(grad[part])
            total = g_values[part] + unwindow(mm(g_wide, bands[1][h], 1, 1), DIM)
            gproj[2 * head_width + DIM * h : 2 * head_width + DIM * (h + 1)] = jnp.where(
                live, total, 0.0
            ).astype(BF16)
            turned = mm(g_wide[:, 128:256], flip, 1, 0).astype(BF16)
            gram = mm(turned, windows(values[part]), 0, 0)
            gram = pltpu.roll(gram, 384 - 127, 1, stride=1, stride_axis=0)
            found = pltpu.roll(jnp.sum(gram, axis=0, keepdims=True), 384 - 112, 1)
            at = lax.broadcasted_iota(jnp.int32, (1, 128), 1)
            lanes = pl.ds(pl.multiple_of(128 * me, 128), 128)
            sum_s[0, 4 + h : 5 + h, lanes] = jnp.where(at < TAPS, found[:, :128], 0.0)
        s.update(grad=grad, values=values, s_high=s_high, s_low=s_low)
        s["outer"] = packs.times(g_weights, marks[4])
        s["hold"] = jnp.zeros_like(s["outer"])
        share(2)

    def qkv_gradient(part):
        total = mm(s["tokens_t"], gproj[head_width * part : head_width * (part + 1)], 1, 1)
        total = total.astype(BF16)
        for d in range(8):
            acc_qkv[part, position(QKV_ORDERS[part], places(0, d))] = folded(total, d)
        projs[part].start()

    sums = [mate if name == "c" else bits[name][1] for name in SUM_ORDER]

    def sum_step(k):
        if k:
            s["sum"].wait()
            total = sum_s[k - 1] + sum_r[k - 1]
            if k == 5:
                ggain_v[...] = total[0:2]
                gshift_v[...] = total[2:4]
                for n in range(gtaps_v.shape[0]):
                    at = 128 * (n // nh)
                    row = 4 + n % nh
                    gtaps_v[n : n + 1] = total[row : row + 1, at : at + TAPS]
                stores.append(fetch(ggain_v, ggain_hbm))
                stores.append(fetch(gshift_v, gshift_hbm))
                stores.append(fetch(gtaps_v, gtaps_hbm))
                return
            sum_s[k] = total
        s["sum"] = copy_to(sum_s.at[k], sum_r.at[k], sems, sum_base + k, sums[k])
        s["sum"].start()

    def newton_back(steps):
        outer, hold = s["outer"], s["hold"]
        for step in steps:
            product, second, cube, inverse_t = [chain[step, i] for i in range(4)]
            blend = 0.25 * (13.0 * packs.unit - 15.0 * product + 7.0 * second - cube)
            inner = packs.times(inverse_t, outer)
            by_inner = packs.times(cat([product, second], 0), inner)
            zero_th, once, twice = inner, by_inner[:count], by_inner[count:]
            if step < NEWTON - 1:
                by_hold = packs.times(cat([product, second, cube], 0), hold)
                zero_th = zero_th + by_hold[:count]
                once = once + by_hold[count : 2 * count]
                twice = twice + by_hold[2 * count :]
            rest = packs.times(zero_th, 7.0 * product - second - 15.0 * packs.unit)
            rest = rest + packs.times(once, 7.0 * packs.unit - product) - twice
            pair = packs.times(cat([outer, hold], 0), blend)
            outer, hold = pair[:count], pair[count:] + 0.25 * rest
        s["outer"], s["hold"] = outer, hold

    def softmax_back():
        first, third = a1[...], a3[...]
        w_high, w_low = halves(marks[5])
        g_tall = mm(packs.block(w_high), s["grad"], 0, 0) + mm(packs.block(w_low), s["grad"], 0, 0)
        along = jnp.sum(per_head(g_tall * first), axis=1, keepdims=True)
        g_one = first * (per_head(g_tall) - along).reshape(head_width, slot)
        g_tall = mm(cat([packs.block(s["s_high"]), packs.block(s["s_low"])], 0), s["values"], 1, 0)
        g_tall = g_tall[:head_width] + g_tall[head_width:]
        g_three = third * (g_tall - jnp.sum(g_tall * third, axis=1, keepdims=True))

        def tall_marks(high, low, wide):
            both = mm(cat([high, low], 0), wide, 1, 1)
            return packs.diagonal(both[:head_width] + both[head_width:]) * scale

        one_high, one_low = halves(g_one)
        three_high, three_low = halves(g_three)
        s["g_k"] = tall_marks(one_high, one_low, packed[:head_width])
        s["g_q"] = tall_marks(three_high, three_low, packed[head_width : 2 * head_width])
        s["one"], s["three"] = one_high, three_high

    def middle_back():
        q_marks, k_marks, middle = marks[0], marks[1], marks[2]
        outer, hold = s["outer"], s["hold"]
        inverse_t = chain[0, 3]
        col_sums = jnp.sum(middle, axis=0, keepdims=True)
        row_sums = packs.row_sum(middle)
        col_top = packs.row_max(col_sums)
        row_top = jnp.max(row_sums, axis=0, keepdims=True)
        norm = 1.0 / (col_top * row_top)
        g_start_t = packs.turn(outer) + packs.times(packs.turn(hold), middle)
        g_norm = -packs.row_sum(jnp.sum(g_start_t * inverse_t, axis=0, keepdims=True)) * norm
        col_hit = (col_sums == col_top).astype(F32)
        row_hit = (row_sums == row_top).astype(F32)
        col_hit = col_hit / packs.row_sum(col_hit)
        row_hit = row_hit / jnp.sum(row_hit, axis=0, keepdims=True)
        g_middle = packs.times(hold, inverse_t) + g_start_t * norm
        g_middle = g_middle + g_norm * (row_top * col_hit + col_top * row_hit)
        g_two_s = middle * (g_middle - packs.row_sum(g_middle * middle))
        g_q_marks = s["g_q"] + packs.times(g_two_s, k_marks)
        g_k_marks = s["g_k"] + packs.times(packs.turn(g_two_s), q_marks)
        for part, other, g_own, high in (
            (0, k_marks, g_q_marks, s["one"]),
            (1, q_marks, g_k_marks, s["three"]),
        ):
            m_high, m_low = halves(other)
            l_high, l_low = halves(g_own * share_of)
            total = mm(packs.block(m_high), high, 0, 0) + mm(packs.block(m_low), high, 0, 0)
            total = total + mm(cat([l_high, l_low], 0), cat([member, member], 0), 0, 0)
            gproj[head_width * part : head_width * (part + 1)] = (total * scale).astype(BF16)
            share(part)

    def input_gradient():
        wqkv = w_qkv[...]
        for copy in p_sent:
            copy.wait()
        in_v[...] = (gr1_ref[...] + mm(gp_in[...], wqkv, 0, 1)).astype(BF16)
        stores.append(fetch(in_v, in_hbm))

    def finish_down(q):
        gdown_v[64 * q : 64 * (q + 1)] = downs[q].finish()
        s["downs"] = s.get("downs", 0) + 1
        if s["downs"] == 3:
            stores.append(fetch(gdown_v, gdown_hbm))

    def finish_up(q):
        gup_v[:, 256 * q : 256 * (q + 1)] = ups[q].finish()
        s["ups"] = s.get("ups", 0) + 1
        if s["ups"] == 3:
            stores.append(fetch(gup_v, gup_hbm))

    def finish_out():
        total = outs.finish()
        gout_v[:band_half] = total[:, :head_width]
        gout_v[band_half:] = total[:, head_width:]
        stores.append(fetch(gout_v, gout_hbm))

    def finish_proj(part):
        total = projs[part].finish()
        goal = quarters * part + me
        dest, where = lax.div(goal, 3), lax.rem(goal, 3)

        @pl.when(dest == me)
        def _():
            slots[where] = total

        @pl.when(dest != me)
        def _():
            fin[part] = total
            pltpu.make_async_remote_copy(
                src_ref=fin.at[part], dst_ref=slots.at[where],
                send_sem=sems.at[0, last + part], recv_sem=sems.at[1, last + where],
                device_id=(dp, dest), device_id_type=MESH,
            ).start()

    def collect():
        for index in range(3):
            goal = quarters * index + me
            source = lax.rem(3 * me + index, quarters)

            @pl.when(lax.div(goal, 3) != me)
            def _():
                copy_to(fin.at[index], slots.at[0], sems, last + index, mate).wait_send()

            @pl.when(source != me)
            def _():
                copy_to(fin.at[0], slots.at[index], sems, last + index, mate).wait_recv()

        for index in range(3):
            got = slots[index]
            cols = slice(head_width * index, head_width * (index + 1))
            gqkv_v[:band_half, cols] = got[:, :head_width]
            gqkv_v[band_half:, cols] = got[:, head_width:]
        stores.append(fetch(gqkv_v, gqkv_hbm))

    table = {
        "DG": down_gradient, "FB": forward_back, "OG": out_gradient, "AV": values_back,
        "SM": softmax_back, "MM": middle_back, "IN": input_gradient, "GQ": collect,
        "LF": low_onward, "GF": g2_onward, "UH": up_slopes,
        "NB1": lambda: newton_back((5, 4, 3)), "NB2": lambda: newton_back((2, 1, 0)),
    }
    for q in range(3):
        table["UG%d" % q] = lambda q=q: up_gradient(q)
        table["QG%d" % q] = lambda q=q: qkv_gradient(q)
    for k in range(6):
        table["S%d" % k] = lambda k=k: sum_step(k)
    names = {"O": (outs, finish_out)}
    for q in range(3):
        names["D%d" % q] = (downs[q], lambda q=q: finish_down(q))
        names["U%d" % q] = (ups[q], lambda q=q: finish_up(q))
        names["P%d" % q] = (projs[q], lambda q=q: finish_proj(q))
    for item in SCHEDULE:
        if item in table:
            table[item]()
        else:
            chunk, finish = names[item]
            if chunk.stage == len(chunk.bits) - 1:
                finish()
            else:
                chunk.step()
    for copy in stores:
        copy.wait()


def final_kernel(*refs):
    sem = refs[-1]
    count = (len(refs) - 1) // 3
    inward = [
        pltpu.make_async_copy(refs[i], refs[2 * count + i], sem.at[0, i]) for i in range(count)
    ]
    outward = [
        pltpu.make_async_copy(refs[2 * count + i], refs[count + i], sem.at[1, i])
        for i in range(count)
    ]
    for copy in inward:
        copy.start()
    for got, put in zip(inward, outward):
        got.wait()
        put.start()
    for copy in outward:
        copy.wait()


def per_device_fast(
    tokens, w_qkv, w_out, w_up, w_down, norm_gains, norm_shifts, conv_kernels, seq_lengths,
    seg_bounds, out_grad,
):
    rows, width = tokens.shape
    ff = w_up.shape[1]
    head_width = width // 4
    slot = 4 * rows
    band, down_cols = width // 8, ff // 8
    whole = pl.BlockSpec(memory_space=VMEM)
    anywhere = pl.BlockSpec(memory_space=pl.ANY)
    shape = jax.ShapeDtypeStruct
    outs = (
        shape((rows, width), BF16),
        shape((rows, width), BF16),
        shape((band, w_qkv.shape[1] // 4), F32),
        shape((band, width // 4), F32),
        shape((band, ff // 4), F32),
        shape((width // 4, down_cols), F32),
        shape(norm_gains.shape, F32),
        shape(norm_shifts.shape, F32),
        shape(conv_kernels.shape, F32),
    )
    found = pl.pallas_call(
        main_kernel,
        out_shape=outs,
        in_specs=[anywhere] * 6
        + [whole] * 3
        + [pl.BlockSpec(memory_space=pltpu.SMEM), whole],
        out_specs=[anywhere] * 9,
        scratch_shapes=[
            VMEM((rows, width), BF16), VMEM((rows, width), BF16),
            VMEM(w_qkv.shape, BF16), VMEM(w_out.shape, BF16),
            VMEM(w_up.shape, BF16), VMEM(w_down.shape, BF16),
            pltpu.SemaphoreType.DMA((32,)), pltpu.SemaphoreType.DMA((2, 120)),
            VMEM((4, rows, width), BF16),
            VMEM((3, 256, width), BF16),
            VMEM((2, conv_kernels.shape[0], 384), F32),
            VMEM((3 * head_width, slot), BF16),
            VMEM((head_width, slot), F32), VMEM((head_width, slot), F32),
            VMEM((NEWTON, 4, DIM, head_width), F32),
            VMEM((6, DIM, head_width), F32),
            VMEM((head_width, slot), BF16),
            VMEM((width, rows), BF16), VMEM((width, rows), BF16),
            VMEM((4, rows, width), BF16), VMEM((4, rows, width), BF16),
            VMEM((2 * rows, ff), BF16),
            VMEM((width, rows), BF16), VMEM((width, rows), BF16),
            VMEM((rows, ff), F32),
            VMEM((rows, ff), BF16),
            VMEM((rows, width), BF16), VMEM((rows, width), BF16),
            VMEM((width, rows), BF16),
            VMEM((head_width, slot), BF16),
            VMEM((3 * head_width, slot), BF16),
            VMEM((3 * width, rows), BF16),
            VMEM((rows, width), F32), VMEM((rows, width), F32), VMEM((rows, width), F32),
            VMEM((5, 8, width), F32), VMEM((5, 8, width), F32),
            VMEM((3, band // 2, 2 * head_width), F32),
            VMEM((3, band // 2, 2 * head_width), F32),
            VMEM((3, 16, 64, down_cols), BF16), VMEM((3, 15, 64, down_cols), BF16),
            VMEM((3, 8, band, 256), BF16), VMEM((3, 7, band, 256), BF16),
            VMEM((16, band // 2, 2 * head_width), BF16),
            VMEM((15, band // 2, 2 * head_width), BF16),
            VMEM((3, 8, band // 2, 2 * head_width), BF16),
            VMEM((3, 7, band // 2, 2 * head_width), BF16),
        ]
        + [VMEM(out.shape, out.dtype) for out in outs],
        compiler_params=pltpu.CompilerParams(
            collective_id=0, has_side_effects=True, vmem_limit_bytes=63 * 2**20
        ),
        name="main_kernel",
    )(
        tokens, out_grad, w_qkv, w_out, w_up, w_down, norm_gains, norm_shifts, conv_kernels,
        seq_lengths, seg_bounds,
    )
    copied = pl.pallas_call(
        final_kernel,
        out_shape=outs,
        in_specs=[anywhere] * 9,
        out_specs=[anywhere] * 9,
        scratch_shapes=[VMEM(out.shape, out.dtype) for out in outs]
        + [pltpu.SemaphoreType.DMA((2, 9))],
        name="final_kernel",
    )(*found)
    copied = tuple(copied)
    return copied[:5] + (copied[5].T,) + copied[6:]


highest = lax.Precision.HIGHEST
epsilon = 1e-05


def layer_norm(values, gain, shift):
    center = jnp.mean(values, axis=-1, keepdims=True)
    centred = values - center
    spread_sq = jnp.mean(centred * centred, axis=-1, keepdims=True)
    return centred * lax.rsqrt(spread_sq + epsilon) * gain + shift


def exact_gelu(values):
    return jax.nn.gelu(values, approximate=False)


def shifted_conv(values, kernel):
    slot_len = values.shape[0]
    taps = kernel.shape[0]
    half_width = taps // 2
    padded = jnp.pad(values, ((half_width, half_width), (0, 0)))
    total = jnp.zeros_like(values)
    for offset in range(taps):
        total = total + kernel[offset] * padded[offset : offset + slot_len]
    return total


def nystrom_head(queries, keys, values, kernel, length, bounds):
    slot_len = queries.shape[0]
    mark_count = bounds.shape[0] - 1
    head_dim = queries.shape[1]
    places = jnp.arange(slot_len, dtype=jnp.int32)
    valid = places < length
    weight_mask = valid.astype(jnp.float32)[:, None]
    scaling = head_dim ** (-0.25)
    queries = queries * weight_mask * scaling
    keys = keys * weight_mask * scaling
    values = values * weight_mask
    member = ((places[None, :] >= bounds[:-1, None]) & (places[None, :] < bounds[1:, None])).astype(
        jnp.float32
    )
    counts = (bounds[1:] - bounds[:-1]).astype(jnp.float32)[:, None]
    query_marks = jnp.dot(member, queries, precision=highest) / counts
    key_marks = jnp.dot(member, keys, precision=highest) / counts
    first = jax.nn.softmax(jnp.dot(queries, key_marks.T, precision=highest), axis=-1)
    middle = jax.nn.softmax(jnp.dot(query_marks, key_marks.T, precision=highest), axis=-1)
    third_scores = jnp.dot(query_marks, keys.T, precision=highest)
    third = jax.nn.softmax(jnp.where(valid[None, :], third_scores, -1000000000.0), axis=-1)
    inverse = middle.T / (jnp.max(jnp.sum(middle, axis=0)) * jnp.max(jnp.sum(middle, axis=1)))
    identity = jnp.eye(mark_count, dtype=jnp.float32)
    for _ in range(NEWTON):
        product = jnp.dot(middle, inverse, precision=highest)
        inner = 7.0 * identity - product
        inner = 15.0 * identity - jnp.dot(product, inner, precision=highest)
        inner = 13.0 * identity - jnp.dot(product, inner, precision=highest)
        inverse = 0.25 * jnp.dot(inverse, inner, precision=highest)
    summary = jnp.dot(third, values, precision=highest)
    mixed = jnp.dot(first, jnp.dot(inverse, summary, precision=highest), precision=highest)
    return (mixed + shifted_conv(values, kernel)) * weight_mask


def attend(packed, kernels, lengths, bounds):
    seq_count = lengths.shape[0]
    head_count = kernels.shape[0]
    head_dim = packed.shape[-1] // (3 * head_count)
    grouped = packed.reshape(seq_count, -1, 3, head_count, head_dim)
    over_heads = jax.vmap(nystrom_head, in_axes=(1, 1, 1, 0, None, None), out_axes=1)
    over_seqs = jax.vmap(over_heads, in_axes=(0, 0, 0, None, 0, 0))
    result = over_seqs(
        grouped[:, :, 0], grouped[:, :, 1], grouped[:, :, 2], kernels, lengths, bounds
    )
    return result.reshape(seq_count * grouped.shape[1], head_count * head_dim)


def row_contract(left, right):
    return lax.dot_general(
        left, right, (((0,), (0,)), ((), ())), preferred_element_type=jnp.float32
    )


def to_blocks(matrix, dp_count, quarters):
    total_rows, total_cols = matrix.shape
    shaped = matrix.reshape(dp_count, total_rows // dp_count, quarters, total_cols // quarters)
    return shaped.transpose(0, 2, 1, 3).reshape(total_rows * quarters, total_cols // quarters)


def per_device(
    tokens,
    w_qkv,
    w_out,
    w_up,
    w_down,
    norm_gains,
    norm_shifts,
    conv_kernels,
    seq_lengths,
    seg_bounds,
    out_grad,
):
    quarters = lax.axis_size("head")
    quarter = lax.axis_index("head")
    dp_count = lax.axis_size("dp")
    tok_rows, width = tokens.shape
    seq_count = seq_lengths.shape[0]
    group_rows = tok_rows * quarters
    slot_len = group_rows // seq_count
    head_count, kernel_len = conv_kernels.shape
    local_heads = head_count // quarters
    head_width = w_qkv.shape[1] // (3 * quarters)
    places = quarter * tok_rows + jnp.arange(tok_rows, dtype=jnp.int32)
    owners = places // slot_len
    within = places % slot_len
    limits = jnp.sum(
        jnp.where(
            owners[:, None] == jnp.arange(seq_count, dtype=jnp.int32)[None, :],
            seq_lengths[None, :],
            0,
        ),
        axis=1,
    )
    live = (within < limits).astype(jnp.float32)[:, None]
    local_kernels = lax.dynamic_slice_in_dim(
        conv_kernels.astype(jnp.float32), quarter * local_heads, local_heads, 0
    )
    projected = jnp.dot(tokens, w_qkv, preferred_element_type=jnp.float32).astype(jnp.bfloat16)
    packed = lax.all_to_all(
        projected.reshape(tok_rows, 3, quarters, head_width),
        "head",
        split_axis=2,
        concat_axis=0,
        tiled=True,
    )
    packed_rows = packed.reshape(group_rows, 3 * head_width)

    def attention_piece(packed_in, kernel_in):
        return attend(packed_in, kernel_in, seq_lengths, seg_bounds)

    attended, attention_back = jax.vjp(
        attention_piece, packed_rows.astype(jnp.float32), local_kernels
    )
    attended_low = attended.astype(jnp.bfloat16)
    heads_rows = lax.all_to_all(
        attended_low.reshape(group_rows, 1, head_width),
        "head",
        split_axis=0,
        concat_axis=1,
        tiled=True,
    ).reshape(tok_rows, width)
    branch = jnp.dot(heads_rows, w_out, preferred_element_type=jnp.float32)
    first_in = tokens.astype(jnp.float32) + branch
    first_norm, first_back = jax.vjp(layer_norm, first_in, norm_gains[0], norm_shifts[0])
    first_low = first_norm.astype(jnp.bfloat16)
    hidden = jnp.dot(first_low, w_up, preferred_element_type=jnp.float32)
    activated, gelu_back = jax.vjp(exact_gelu, hidden)
    act_low = activated.astype(jnp.bfloat16)
    second = jnp.dot(act_low, w_down, preferred_element_type=jnp.float32)
    output, second_back = jax.vjp(layer_norm, first_norm + second, norm_gains[1], norm_shifts[1])
    cotangent = out_grad.astype(jnp.float32) * live
    grad_second_in, grad_gain_two, grad_shift_two = second_back(cotangent)
    grad_second = grad_second_in.astype(jnp.bfloat16)
    grad_down = row_contract(act_low, grad_second)
    grad_act = jnp.dot(grad_second, w_down.T, preferred_element_type=jnp.float32)
    grad_hidden = gelu_back(grad_act)[0].astype(jnp.bfloat16)
    grad_up = row_contract(first_low, grad_hidden)
    grad_first = grad_second_in + jnp.dot(grad_hidden, w_up.T, preferred_element_type=jnp.float32)
    grad_first_in, grad_gain_one, grad_shift_one = first_back(grad_first)
    grad_branch = grad_first_in.astype(jnp.bfloat16)
    grad_wout = row_contract(heads_rows, grad_branch)
    grad_heads = jnp.dot(grad_branch, w_out.T, preferred_element_type=jnp.float32).astype(
        jnp.bfloat16
    )
    heads_grad = lax.all_to_all(
        grad_heads.reshape(tok_rows, quarters, head_width),
        "head",
        split_axis=1,
        concat_axis=0,
        tiled=True,
    ).reshape(group_rows, head_width)
    grad_packed, grad_local_kernels = attention_back(heads_grad.astype(jnp.float32))
    grad_packed_low = grad_packed.astype(jnp.bfloat16).reshape(group_rows, 3, 1, head_width)
    grad_projected = lax.all_to_all(
        grad_packed_low, "head", split_axis=0, concat_axis=2, tiled=True
    ).reshape(tok_rows, 3 * quarters * head_width)
    grad_wqkv = row_contract(tokens, grad_projected)
    input_grad = (
        grad_first_in + jnp.dot(grad_projected, w_qkv.T, preferred_element_type=jnp.float32)
    ).astype(jnp.bfloat16)
    kernel_full = lax.dynamic_update_slice_in_dim(
        jnp.zeros((head_count, kernel_len), jnp.float32),
        grad_local_kernels,
        quarter * local_heads,
        0,
    )
    small_sums = lax.psum(
        (
            jnp.stack([grad_gain_one, grad_gain_two]),
            jnp.stack([grad_shift_one, grad_shift_two]),
            kernel_full,
        ),
        ("dp", "head"),
    )
    blocked_qkv = to_blocks(grad_wqkv, dp_count, quarters)
    blocked_out = to_blocks(grad_wout, dp_count, quarters)
    blocked_up = to_blocks(grad_up, dp_count, quarters)
    blocked_down = to_blocks(grad_down, dp_count, quarters)
    weight_sums = (
        lax.psum_scatter(blocked_qkv, ("dp", "head"), scatter_dimension=0, tiled=True),
        lax.psum_scatter(blocked_out, ("dp", "head"), scatter_dimension=0, tiled=True),
        lax.psum_scatter(blocked_up, ("dp", "head"), scatter_dimension=0, tiled=True),
        lax.psum_scatter(blocked_down, ("dp", "head"), scatter_dimension=0, tiled=True),
    )
    return (
        output.astype(jnp.bfloat16),
        input_grad,
        weight_sums[0],
        weight_sums[1],
        weight_sums[2],
        weight_sums[3],
        small_sums[0],
        small_sums[1],
        small_sums[2],
    )


def solution(mesh):
    placed = (
        P(("dp", "head"), None),
        P(),
        P(),
        P(),
        P(),
        P(),
        P(),
        P(),
        P("dp"),
        P("dp", None),
        P(("dp", "head"), None),
    )
    aligned = mesh.shape["dp"] == 8 and mesh.shape["head"] == 4
    return jax.shard_map(
        per_device_fast if aligned else per_device,
        mesh=mesh,
        in_specs=placed,
        out_specs=(
            P(("dp", "head"), None),
            P(("dp", "head"), None),
            P("dp", "head"),
            P("dp", "head"),
            P("dp", "head"),
            P("dp", "head"),
            P(),
            P(),
            P(),
        ),
        check_vma=False,
    )
```

```python
import jax
import jax.numpy as jnp
from jax import lax
from jax.sharding import PartitionSpec as P
from jax.experimental import pallas as pl
from jax.experimental.pallas import tpu as pltpu

MESH = pl.DeviceIdType.MESH
NEWTON = 6
F32 = jnp.float32
BF16 = jnp.bfloat16
VMEM = pltpu.VMEM
HEADS_HERE = 3
DIM = 64
TAPS = 33


def mm(a, b, ca, cb):
    return lax.dot_general(a, b, (((ca,), (cb,)), ((), ())), preferred_element_type=F32)


def halves(value):
    high = value.astype(BF16)
    return high, (value - high.astype(F32)).astype(BF16)


def cat(parts, axis):
    return jnp.concatenate(parts, axis=axis)


class Packs:
    def __init__(self):
        lane = lax.broadcasted_iota(jnp.int32, (1, HEADS_HERE * DIM), 1)
        self.hit = [(lane // DIM == h).astype(F32) for h in range(HEADS_HERE)]
        self.low_hit = [h.astype(BF16) for h in self.hit]
        rows = lax.broadcasted_iota(jnp.int32, (DIM, HEADS_HERE * DIM), 0)
        cols = lax.broadcasted_iota(jnp.int32, (DIM, HEADS_HERE * DIM), 1)
        self.unit = (rows == cols % DIM).astype(F32)

    def block(self, low):
        return cat([low * h for h in self.low_hit], 0)

    def times(self, lhs, rhs, side=0):
        rows = lhs.shape[0]
        l_high, l_low = halves(lhs)
        r_high, r_low = halves(rhs)
        both = mm(cat([l_high, l_low], 0), self.block(r_high), 1, side)
        return both[:rows] + both[rows:] + mm(l_high, self.block(r_low), 1, side)

    def diagonal(self, full):
        total = full[:DIM] * self.hit[0]
        for h in range(1, HEADS_HERE):
            total = total + full[DIM * h : DIM * (h + 1)] * self.hit[h]
        return total

    def turn(self, value):
        tall = value.T
        return cat([tall[DIM * h : DIM * (h + 1)] for h in range(HEADS_HERE)], 1)

    def each(self, values):
        total = values[0] * self.hit[0]
        for h in range(1, HEADS_HERE):
            total = total + values[h] * self.hit[h]
        return total

    def row_max(self, value):
        return self.each(
            [
                jnp.max(jnp.where(h > 0, value, -jnp.inf), axis=1, keepdims=True)
                for h in self.hit
            ]
        )

    def row_sum(self, value):
        return self.each([jnp.sum(value * h, axis=1, keepdims=True) for h in self.hit])


def expand(block_low, lhs_side, wide):
    return mm(block_low, wide, lhs_side, 0)


def toeplitz(base):
    rows = jnp.broadcast_to(base, (128, base.shape[1]))
    return pltpu.roll(rows, 0, 1, stride=1, stride_axis=0).astype(BF16)


def windows(mat):
    zero = jnp.zeros((mat.shape[0], 128), mat.dtype)
    wide = cat([zero, mat, zero], 1)
    return cat([wide[:, 128 * b : 128 * b + 384] for b in range(mat.shape[1] // 128)], 0)


def unwindow(stacked, rows):
    return cat([stacked[rows * b : rows * (b + 1)] for b in range(stacked.shape[0] // rows)], 1)


def gelu_pair(hidden):
    tail = jnp.exp(-0.5 * hidden * hidden)
    t = 1.0 / (1.0 + 0.23164190 * jnp.abs(hidden))
    poly = 1.330274429
    for term in (-1.821255978, 1.781477937, -0.356563782, 0.319381530):
        poly = poly * t + term
    density = 0.3989422804014327 * tail
    below = density * poly * t
    normal = jnp.where(hidden >= 0.0, 1.0 - below, below)
    return hidden * normal, normal + hidden * density


def norm_forward(values):
    center = jnp.mean(values, axis=-1, keepdims=True)
    centred = values - center
    spread = jnp.mean(centred * centred, axis=-1, keepdims=True)
    root = lax.rsqrt(spread + 1e-5)
    return centred * root, root


def norm_backward(grad, gain, normed, root):
    scaled = grad * gain
    center = jnp.mean(scaled, axis=-1, keepdims=True)
    along = jnp.mean(scaled * normed, axis=-1, keepdims=True)
    return root * (scaled - center - normed * along)


def copy_to(src, dst, sems, index, device):
    return pltpu.make_async_remote_copy(
        src_ref=src,
        dst_ref=dst,
        send_sem=sems.at[0, index],
        recv_sem=sems.at[1, index],
        device_id=device,
        device_id_type=MESH,
    )


def greet(devices):
    barrier = pltpu.get_barrier_semaphore()
    for device in devices:
        pl.semaphore_signal(barrier, inc=1, device_id=device, device_id_type=MESH)
    return lambda: pl.semaphore_wait(barrier, len(devices))


class Spread:
    def __init__(self, acc, got, bits, sems, base):
        self.acc, self.got, self.bits, self.sems, self.base = acc, got, bits, sems, base
        self.blocks = acc.shape[0]
        self.stage = 0
        self.offset = 0
        self.at = 0
        self.sent = []

    def start(self):
        bit, device = self.bits[self.stage]
        size = self.blocks >> (self.stage + 1)
        self.keep = self.offset + bit * size
        other = self.offset + (1 - bit) * size
        self.flight = copy_to(
            self.acc.at[pl.ds(other, size)], self.got.at[pl.ds(self.at, size)],
            self.sems, self.base + self.stage, device,
        )
        self.flight.start()
        self.size = size

    def take(self):
        self.flight.wait_recv()
        self.sent.append(self.flight)
        mine, new = pl.ds(self.keep, self.size), pl.ds(self.at, self.size)
        self.at += self.size
        self.offset = self.keep
        self.stage += 1
        if self.stage == len(self.bits):
            return self.acc[mine].astype(F32) + self.got[new].astype(F32)
        self.acc[mine] = self.acc[mine] + self.got[new]
        return None

    def step(self):
        self.take()
        self.start()

    def finish(self):
        total = self.take()
        for sent in self.sent:
            sent.wait_send()
        return total[0]


def position(order, values):
    spot = 0
    for name in order:
        spot = 2 * spot + values[name]
    return spot


DOWN_ORDERS = ("yxlh", "lyxh", "lxyh")
UP_ORDERS = ("lyh", "ylh", "ylh")
OUT_ORDER = "yxlh"
SUM_ORDER = "hycxl"
QKV_ORDERS = ("ylh", "ylh", "ylh")
SCHEDULE = (
    "HB0", "DG", "LF", "HB1", "FB", "OG", "D1", "D0", "GF", "UH", "UG0", "UG1", "O", "AV",
    "S0", "D2", "D0", "SM", "D1", "NB1", "O", "U0", "S1", "QG2", "U1", "NB2", "D0", "MM", "O",
    "U0", "QG0", "S2", "U1", "QG1", "UG2", "S3", "D2", "D0", "P2", "D1", "O", "P0", "U0",
    "U1", "P1", "P2", "D1", "IN", "S4", "U2", "P0", "P1", "D2", "P2", "S5", "U2", "P0", "P1",
    "D2", "U2", "GQ",
)


def main_kernel(
    tok_hbm, grad_hbm, wqkv_hbm, wout_hbm, wup_hbm, wdown_hbm,
    gain_ref, shift_ref, taps_ref, len_ref, bounds_ref,
    out_hbm, in_hbm, gqkv_hbm, gout_hbm, gup_hbm, gdown_hbm, ggain_hbm, gshift_hbm, gtaps_hbm,
    tok, grad_in, w_qkv, w_out, w_up, w_down, lsem, sems,
    everyone, wt, bases, packed, a1, a3, chain, marks, att, heads, heads_x,
    low_all, g2_all, act, gst, gst_x, slope, gh, gb, gb_x, gatt, g_in, gproj, gp_in,
    first_ref, norm1_ref, gr1_ref, sum_s, sum_r, fin, slots,
    acc_down, got_down, acc_up, got_up, acc_out, got_out, acc_qkv, got_qkv,
    out_v, in_v, gqkv_v, gout_v, gup_v, gdown_v, ggain_v, gshift_v, gtaps_v,
):
    dp = lax.axis_index("dp")
    me = lax.axis_index("head")
    quarters = 4
    rows, width = tok.shape
    slot = rows * quarters
    hidden_width = w_up.shape[1]
    block = hidden_width // quarters
    head_width = width // quarters
    count = DIM
    nh = HEADS_HERE
    band_rows = width // 8
    down_cols = hidden_width // 8
    core = lax.rem(me, 2)
    mate = (dp, me ^ 1)
    bits = {
        "x": (lax.div(me, 2), (dp, me ^ 2)),
        "y": (lax.rem(dp, 2), (dp ^ 1, me)),
        "l": (lax.rem(lax.div(dp, 2), 2), (dp ^ 2, me)),
        "h": (lax.div(dp, 4), (dp ^ 4, me)),
    }
    counter = iter(range(200))
    local = iter(range(40))

    def fetch(src, dst):
        copy = pltpu.make_async_copy(src, dst, lsem.at[next(local)])
        copy.start()
        return copy

    def send(src, dst, device):
        copy = copy_to(src, dst, sems, next(counter), device)
        copy.start()
        return copy

    def reserve(n):
        base = next(counter)
        for _ in range(n - 1):
            next(counter)
        return base

    def spread(acc, got, order):
        return Spread(acc, got, [bits[name] for name in order], sems, reserve(len(order)))

    all_here = greet([(dp, me ^ k) for k in (1, 2, 3)] + [(dp ^ k, me) for k in (1, 2, 4)])
    own_fetch = fetch(tok_hbm, everyone.at[me])
    tok_fetch = fetch(tok_hbm, tok)
    wqkv_fetch = fetch(wqkv_hbm, w_qkv)
    all_here()
    half = rows // 2
    far = []
    for piece in range(2):
        part = pl.ds(piece * half, half)
        far.append(send(tok_hbm.at[part], everyone.at[me, part], (dp, me ^ 2)))
    near = send(tok_hbm, everyone.at[me], mate)
    wqkv_fetch.wait()
    wout_fetch = fetch(wout_hbm, w_out)
    wup_fetch = fetch(wup_hbm, w_up)
    wdown_fetch = fetch(wdown_hbm, w_down)
    grad_fetch = fetch(grad_hbm, grad_in)
    odd = lax.rem(me, 2)
    for part in range(3):
        start = pl.multiple_of(part * width + 2 * head_width * lax.div(me, 2) + 128 * odd, 128)
        wt[part] = w_qkv[:, pl.ds(start, 256)].T
    w_own = cat(
        [wt[part, pl.ds(pl.multiple_of(64 * odd, 64), head_width), :] for part in range(3)], 0
    )
    packs = Packs()
    lane = lax.broadcasted_iota(jnp.int32, (TAPS, 384), 1)
    tap = lax.broadcasted_iota(jnp.int32, (TAPS, 384), 0)
    for turn, spots in enumerate((tap + 112, 144 - tap)):
        bases[turn] = mm(taps_ref[...], (lane == spots).astype(F32).astype(BF16), 1, 0)
    bands = [
        [toeplitz(bases[turn, pl.ds(nh * me + h, 1), :]) for h in range(nh)] for turn in range(2)
    ]
    edges = bounds_ref[...].astype(F32)
    low_edge = jnp.broadcast_to(edges[:, :count], (count, count)).T[:, 0:1]
    high_edge = jnp.broadcast_to(edges[:, 1 : count + 1], (count, count)).T[:, 0:1]
    place = lax.broadcasted_iota(jnp.int32, (count, slot), 1).astype(F32)
    member = ((place >= low_edge) & (place < high_edge)).astype(F32).astype(BF16)
    share_of = 1.0 / (high_edge - low_edge)
    length = len_ref[0]
    live = lax.broadcasted_iota(jnp.int32, (1, slot), 1) < length
    scale = DIM ** (-0.25)

    def project(which):
        lanes = pl.ds(pl.multiple_of(rows * which, rows), rows)
        packed[:, lanes] = mm(w_own, everyone[which], 1, 1).astype(BF16)

    own_fetch.wait()
    project(me)
    near.wait()
    project(me ^ 1)
    onward = []
    for piece in range(2):
        part = pl.ds(piece * half, half)
        far[piece].wait()
        onward.append(send(everyone.at[me ^ 2, part], everyone.at[me ^ 2, part], mate))
    project(me ^ 2)
    for copy in onward:
        copy.wait()
    project(me ^ 3)
    queries = packed[:head_width]
    keys = packed[head_width : 2 * head_width]
    q_marks = mm(member, queries, 1, 1) * (scale * share_of)
    k_marks = mm(member, keys, 1, 1) * (scale * share_of)
    marks[0] = q_marks
    marks[1] = k_marks
    scores = packs.times(q_marks, k_marks, 1)
    powers = jnp.exp(scores - packs.row_max(scores))
    middle = powers / packs.row_sum(powers)
    marks[2] = middle
    col_sums = jnp.sum(middle, axis=0, keepdims=True)
    col_top = packs.row_max(col_sums)
    row_top = jnp.max(packs.row_sum(middle), axis=0, keepdims=True)
    inverse_t = middle / (col_top * row_top)
    product = packs.times(inverse_t, middle, 1)
    for step in range(NEWTON):
        second = packs.times(product, product)
        pair = packs.times(cat([product, second], 0), second)
        third, fourth = pair[:count], pair[count:]
        for i, value in enumerate((product, second, third, inverse_t)):
            chain[step, i] = value
        blend = 0.25 * (13.0 * packs.unit - 15.0 * product + 7.0 * second - third)
        product = 0.25 * (13.0 * product - 15.0 * second + 7.0 * third - fourth)
        inverse_t = packs.times(blend, inverse_t)
    marks[3] = inverse_t
    def tall_scores(values, wide):
        high, low = halves(values * scale)
        both = mm(cat([packs.block(high), packs.block(low)], 0), wide, 1, 0)
        return both[:head_width] + both[head_width:]

    def per_head(value):
        return value.reshape(nh, count, slot)

    scores = per_head(tall_scores(k_marks, queries))
    powers = jnp.exp(scores - jnp.max(scores, axis=1, keepdims=True))
    first = (powers * (1.0 / jnp.sum(powers, axis=1, keepdims=True))).reshape(head_width, slot)
    a1[...] = first
    scores = jnp.where(live, tall_scores(q_marks, keys), -1e9)
    powers = jnp.exp(scores - jnp.max(scores, axis=1, keepdims=True))
    third = powers * (1.0 / jnp.sum(powers, axis=1, keepdims=True))
    a3[...] = third
    values = jnp.where(live, packed[2 * head_width :].astype(F32), 0.0).astype(BF16)
    t_high, t_low = halves(third)
    summary_t = packs.diagonal(mm(values, t_high, 1, 1) + mm(values, t_low, 1, 1))
    weights_t = packs.times(summary_t, inverse_t)
    marks[4] = summary_t
    marks[5] = weights_t
    w_high, w_low = halves(weights_t)
    f_high, f_low = halves(first)
    mixed = mm(cat([packs.block(w_high), packs.block(w_low)], 0), f_high, 1, 0)
    mixed = mixed[:head_width] + mixed[head_width:] + mm(packs.block(w_high), f_low, 1, 0)
    mine = pl.ds(pl.multiple_of(rows * me, rows), rows)
    own_rows = pl.ds(pl.multiple_of(head_width * me, 64), head_width)
    att_sent = []
    for h in range(nh):
        part = slice(DIM * h, DIM * (h + 1))
        conv = unwindow(mm(windows(values[part]), bands[0][h], 1, 1), DIM)
        att[part] = jnp.where(live, mixed[part] + conv, 0.0).astype(BF16)
        goal = pl.ds(pl.multiple_of(head_width * me + DIM * h, 64), DIM)
        for k in (2, 3, 1):
            lanes = pl.ds(pl.multiple_of(rows * (me ^ k), rows), rows)
            att_sent.append(send(att.at[part, lanes], heads.at[goal], (dp, me ^ k)))
    heads[own_rows] = att[:, mine]
    wout_fetch.wait()
    tok_fetch.wait()
    for copy in att_sent:
        copy.wait()
    heads_sent = send(heads, heads_x, mate)
    branch = mm(heads[...], w_out[...], 0, 0)
    normed, root_one = norm_forward(tok[...].astype(F32) + branch)
    norm1_ref[...] = normed
    first_norm = normed * gain_ref[0:1] + shift_ref[0:1]
    first_ref[...] = first_norm
    low = first_norm.astype(BF16)
    low_all[me] = low
    low_far = send(low_all.at[me], low_all.at[me], (dp, me ^ 2))
    low_near = send(low_all.at[me], low_all.at[me], mate)
    wup_fetch.wait()
    wdown_fetch.wait()
    second_sum = None
    act_sent = []
    for i in range(quarters):
        cols = slice(block * i, block * (i + 1))
        active, slope_part = gelu_pair(mm(low, w_up[:, cols], 1, 0))
        active = active.astype(BF16)
        act[:rows, cols] = active
        act_sent.append(send(act.at[:rows, cols], act.at[rows:, cols], mate))
        slope[:, cols] = slope_part
        part = mm(active, w_down[cols, :], 1, 0)
        second_sum = part if second_sum is None else second_sum + part
    normed_two, root_two = norm_forward(first_ref[...] + second_sum)
    grad_fetch.wait()
    spot = me * rows + lax.broadcasted_iota(jnp.int32, (rows, 1), 0)
    cotangent = jnp.where(spot < length, grad_in[...].astype(F32), 0.0)
    g_two = norm_backward(cotangent, gain_ref[1:2], normed_two, root_two)
    g_low = g_two.astype(BF16)
    g2_all[me] = g_low
    g2_far = send(g2_all.at[me], g2_all.at[me], (dp, me ^ 2))
    gst[...] = g_low.T
    gst_sent = send(gst, gst_x, mate)
    g2_near = send(g2_all.at[me], g2_all.at[me], mate)
    gr1_ref[...] = g_two
    out_v[...] = (normed_two * gain_ref[1:2] + shift_ref[1:2]).astype(BF16)
    stores = [fetch(out_v, out_hbm)]
    sum_s[0] = jnp.zeros(sum_s.shape[1:], F32)
    sum_s[0, 1:2] = jnp.sum(cotangent * normed_two, axis=0, keepdims=True)
    sum_s[0, 3:4] = jnp.sum(cotangent, axis=0, keepdims=True)
    s = {}
    downs = [spread(acc_down.at[q], got_down.at[q], DOWN_ORDERS[q]) for q in range(3)]
    ups = [spread(acc_up.at[q], got_up.at[q], UP_ORDERS[q]) for q in range(3)]
    outs = spread(acc_out, got_out, OUT_ORDER)
    projs = [spread(acc_qkv.at[j], got_qkv.at[j], QKV_ORDERS[j]) for j in range(3)]
    sum_base = reserve(5)
    last = reserve(3)
    band_half = band_rows // 2
    p_sent = []

    def folded(total, d):
        top = band_rows * d
        return cat([total[top : top + band_half], total[top + band_half : top + band_rows]], 1)

    def places(x, d):
        return {"x": x, "y": d % 2, "l": d // 2 % 2, "h": d // 4}

    def down_gradient():
        for copy in act_sent:
            copy.wait()
        gst_sent.wait()
        tops = [pl.ds(pl.multiple_of(head_width * (2 * x + core), 64), head_width) for x in (0, 1)]
        lead = cat([cat([gst[top, :], gst_x[top, :]], 1) for top in tops], 0)
        for pair in range(4):
            total = mm(lead, act[:, 2 * down_cols * pair : 2 * down_cols * (pair + 1)], 1, 0)
            total = total.astype(BF16)
            for x in range(2):
                for inner in range(2):
                    at = places(x, 2 * pair + inner)
                    for q in range(3):
                        top = head_width * x + 64 * q
                        acc_down[q, position(DOWN_ORDERS[q], at)] = total[
                            top : top + 64, down_cols * inner : down_cols * (inner + 1)
                        ]
        for chunk in downs:
            chunk.start()

    def hidden_back(turns):
        g_first = s.get("g_first", g_two)
        for i in turns:
            cols = slice(block * i, block * (i + 1))
            part = (slope[:, cols] * mm(g_low, w_down[cols, :], 1, 1)).astype(BF16)
            g_first = g_first + mm(part, w_up[:, cols], 1, 1)
        s["g_first"] = g_first

    def branch_back():
        g_first = s["g_first"]
        normed = norm1_ref[...]
        sum_s[0, 0:1] = jnp.sum(g_first * normed, axis=0, keepdims=True)
        sum_s[0, 2:3] = jnp.sum(g_first, axis=0, keepdims=True)
        g_one = norm_backward(g_first, gain_ref[0:1], normed, root_one)
        gr1_ref[...] = g_one
        g_branch = g_one.astype(BF16)
        gb[...] = g_branch
        gatt[...] = mm(w_out[...], g_branch, 1, 1).astype(BF16)
        s["g"] = []
        for k in (2, 3, 1):
            src = gatt.at[pl.ds(pl.multiple_of(head_width * (me ^ k), 64), head_width)]
            s["g"].append(send(src, g_in.at[:, mine], (dp, me ^ k)))
        s["gb"] = send(gb, gb_x, mate)
        g_in[:, mine] = gatt[own_rows]

    own_cols = pl.ds(pl.multiple_of(block * me, 128), block)

    def low_onward():
        low_far.wait()
        s["low"] = send(low_all.at[me ^ 2], low_all.at[me ^ 2], mate)

    def g2_onward():
        g2_far.wait()
        s["g2"] = send(g2_all.at[me ^ 2], g2_all.at[me ^ 2], mate)

    def up_slopes():
        low_near.wait()
        s["low"].wait()
        side = w_up[:, own_cols]
        for b in range(quarters):
            hidden = mm(low_all[b], side, 1, 0)
            slope[:, block * b : block * (b + 1)] = gelu_pair(hidden)[1]
        s["low_t"] = low_all[...].reshape(slot, width).T

    def up_gradient(q):
        if q == 0:
            g2_near.wait()
            s["g2"].wait()
            side = w_down[own_cols, :]
            for b in range(quarters):
                cols = slice(block * b, block * (b + 1))
                gh[:, cols] = (slope[:, cols] * mm(g2_all[b], side, 1, 1)).astype(BF16)
        side = cat([gh[:, block * b + 256 * q : block * b + 256 * (q + 1)] for b in range(4)], 0)
        total = mm(s["low_t"], side, 1, 0).astype(BF16)
        for d in range(8):
            acc_up[q, position(UP_ORDERS[q], places(0, d))] = total[
                band_rows * d : band_rows * (d + 1)
            ]
        ups[q].start()

    def out_gradient():
        heads_sent.wait()
        s["gb"].wait()
        lead = cat([heads[...], heads_x[...]], 1)
        both = cat([gb[...], gb_x[...]], 0)
        for x in range(2):
            left_cols = both[:, 2 * head_width * x : 2 * head_width * x + head_width]
            right_cols = both[:, 2 * head_width * x + head_width : 2 * head_width * (x + 1)]
            total = mm(lead, jnp.where(core == 0, left_cols, right_cols), 1, 0).astype(BF16)
            for d in range(8):
                acc_out[position(OUT_ORDER, places(x, d))] = folded(total, d)
        outs.start()

    def share(part):
        own = gproj.at[head_width * part : head_width * (part + 1)]
        dst = pl.ds(pl.multiple_of(width * part + head_width * me, 64), head_width)
        for k in (2, 3, 1):
            lanes = pl.ds(pl.multiple_of(rows * (me ^ k), rows), rows)
            p_sent.append(send(own.at[:, lanes], gp_in.at[dst], (dp, me ^ k)))
        gp_in[dst] = own[:, mine]

    def values_back():
        s["tokens_t"] = everyone[...].reshape(slot, width).T
        for copy in s["g"]:
            copy.wait()
        grad = jnp.where(live, g_in[...].astype(F32), 0.0).astype(BF16)
        values = jnp.where(live, packed[2 * head_width :].astype(F32), 0.0).astype(BF16)
        f_high, f_low = halves(a1[...])
        t_high, t_low = halves(a3[...])
        g_weights = packs.diagonal(mm(f_high, grad, 1, 1) + mm(f_low, grad, 1, 1))
        s_high, s_low = halves(packs.times(marks[3], g_weights))
        g_values = mm(packs.block(s_high), t_high, 0, 0) + mm(packs.block(s_low), t_high, 0, 0)
        g_values = g_values + mm(packs.block(s_high), t_low, 0, 0)
        flip_rows = lax.broadcasted_iota(jnp.int32, (128, 128), 0)
        flip_cols = lax.broadcasted_iota(jnp.int32, (128, 128), 1)
        flip = (flip_rows + flip_cols == 127).astype(F32).astype(BF16)
        for h in range(nh):
            part = slice(DIM * h, DIM * (h + 1))
            g_wide = windows(grad[part])
            total = g_values[part] + unwindow(mm(g_wide, bands[1][h], 1, 1), DIM)
            gproj[2 * head_width + DIM * h : 2 * head_width + DIM * (h + 1)] = jnp.where(
                live, total, 0.0
            ).astype(BF16)
            turned = mm(g_wide[:, 128:256], flip, 1, 0).astype(BF16)
            gram = mm(turned, windows(values[part]), 0, 0)
            gram = pltpu.roll(gram, 384 - 127, 1, stride=1, stride_axis=0)
            found = pltpu.roll(jnp.sum(gram, axis=0, keepdims=True), 384 - 112, 1)
            at = lax.broadcasted_iota(jnp.int32, (1, 128), 1)
            lanes = pl.ds(pl.multiple_of(128 * me, 128), 128)
            sum_s[0, 4 + h : 5 + h, lanes] = jnp.where(at < TAPS, found[:, :128], 0.0)
        s.update(grad=grad, values=values, s_high=s_high, s_low=s_low)
        s["outer"] = packs.times(g_weights, marks[4])
        s["hold"] = jnp.zeros_like(s["outer"])
        share(2)

    def qkv_gradient(part):
        total = mm(s["tokens_t"], gproj[head_width * part : head_width * (part + 1)], 1, 1)
        total = total.astype(BF16)
        for d in range(8):
            acc_qkv[part, position(QKV_ORDERS[part], places(0, d))] = folded(total, d)
        projs[part].start()

    sums = [mate if name == "c" else bits[name][1] for name in SUM_ORDER]

    def sum_step(k):
        if k:
            s["sum"].wait()
            total = sum_s[k - 1] + sum_r[k - 1]
            if k == 5:
                ggain_v[...] = total[0:2]
                gshift_v[...] = total[2:4]
                for n in range(gtaps_v.shape[0]):
                    at = 128 * (n // nh)
                    row = 4 + n % nh
                    gtaps_v[n : n + 1] = total[row : row + 1, at : at + TAPS]
                stores.append(fetch(ggain_v, ggain_hbm))
                stores.append(fetch(gshift_v, gshift_hbm))
                stores.append(fetch(gtaps_v, gtaps_hbm))
                return
            sum_s[k] = total
        s["sum"] = copy_to(sum_s.at[k], sum_r.at[k], sems, sum_base + k, sums[k])
        s["sum"].start()

    def newton_back(steps):
        outer, hold = s["outer"], s["hold"]
        for step in steps:
            product, second, cube, inverse_t = [chain[step, i] for i in range(4)]
            blend = 0.25 * (13.0 * packs.unit - 15.0 * product + 7.0 * second - cube)
            inner = packs.times(inverse_t, outer)
            by_inner = packs.times(cat([product, second], 0), inner)
            zero_th, once, twice = inner, by_inner[:count], by_inner[count:]
            if step < NEWTON - 1:
                by_hold = packs.times(cat([product, second, cube], 0), hold)
                zero_th = zero_th + by_hold[:count]
                once = once + by_hold[count : 2 * count]
                twice = twice + by_hold[2 * count :]
            rest = packs.times(zero_th, 7.0 * product - second - 15.0 * packs.unit)
            rest = rest + packs.times(once, 7.0 * packs.unit - product) - twice
            pair = packs.times(cat([outer, hold], 0), blend)
            outer, hold = pair[:count], pair[count:] + 0.25 * rest
        s["outer"], s["hold"] = outer, hold

    def softmax_back():
        first, third = a1[...], a3[...]
        w_high, w_low = halves(marks[5])
        g_tall = mm(packs.block(w_high), s["grad"], 0, 0) + mm(packs.block(w_low), s["grad"], 0, 0)
        along = jnp.sum(per_head(g_tall * first), axis=1, keepdims=True)
        g_one = first * (per_head(g_tall) - along).reshape(head_width, slot)
        g_tall = mm(cat([packs.block(s["s_high"]), packs.block(s["s_low"])], 0), s["values"], 1, 0)
        g_tall = g_tall[:head_width] + g_tall[head_width:]
        g_three = third * (g_tall - jnp.sum(g_tall * third, axis=1, keepdims=True))

        def tall_marks(high, low, wide):
            both = mm(cat([high, low], 0), wide, 1, 1)
            return packs.diagonal(both[:head_width] + both[head_width:]) * scale

        one_high, one_low = halves(g_one)
        three_high, three_low = halves(g_three)
        s["g_k"] = tall_marks(one_high, one_low, packed[:head_width])
        s["g_q"] = tall_marks(three_high, three_low, packed[head_width : 2 * head_width])
        s["one"], s["three"] = one_high, three_high

    def middle_back():
        q_marks, k_marks, middle = marks[0], marks[1], marks[2]
        outer, hold = s["outer"], s["hold"]
        inverse_t = chain[0, 3]
        col_sums = jnp.sum(middle, axis=0, keepdims=True)
        row_sums = packs.row_sum(middle)
        col_top = packs.row_max(col_sums)
        row_top = jnp.max(row_sums, axis=0, keepdims=True)
        norm = 1.0 / (col_top * row_top)
        g_start_t = packs.turn(outer) + packs.times(packs.turn(hold), middle)
        g_norm = -packs.row_sum(jnp.sum(g_start_t * inverse_t, axis=0, keepdims=True)) * norm
        col_hit = (col_sums == col_top).astype(F32)
        row_hit = (row_sums == row_top).astype(F32)
        col_hit = col_hit / packs.row_sum(col_hit)
        row_hit = row_hit / jnp.sum(row_hit, axis=0, keepdims=True)
        g_middle = packs.times(hold, inverse_t) + g_start_t * norm
        g_middle = g_middle + g_norm * (row_top * col_hit + col_top * row_hit)
        g_two_s = middle * (g_middle - packs.row_sum(g_middle * middle))
        g_q_marks = s["g_q"] + packs.times(g_two_s, k_marks)
        g_k_marks = s["g_k"] + packs.times(packs.turn(g_two_s), q_marks)
        for part, other, g_own, high in (
            (0, k_marks, g_q_marks, s["one"]),
            (1, q_marks, g_k_marks, s["three"]),
        ):
            m_high, m_low = halves(other)
            l_high, l_low = halves(g_own * share_of)
            total = mm(packs.block(m_high), high, 0, 0) + mm(packs.block(m_low), high, 0, 0)
            total = total + mm(cat([l_high, l_low], 0), cat([member, member], 0), 0, 0)
            gproj[head_width * part : head_width * (part + 1)] = (total * scale).astype(BF16)
            share(part)

    def input_gradient():
        wqkv = w_qkv[...]
        for copy in p_sent:
            copy.wait()
        in_v[...] = (gr1_ref[...] + mm(gp_in[...], wqkv, 0, 1)).astype(BF16)
        stores.append(fetch(in_v, in_hbm))

    def finish_down(q):
        gdown_v[64 * q : 64 * (q + 1)] = downs[q].finish()
        s["downs"] = s.get("downs", 0) + 1
        if s["downs"] == 3:
            stores.append(fetch(gdown_v, gdown_hbm))

    def finish_up(q):
        gup_v[:, 256 * q : 256 * (q + 1)] = ups[q].finish()
        s["ups"] = s.get("ups", 0) + 1
        if s["ups"] == 3:
            stores.append(fetch(gup_v, gup_hbm))

    def finish_out():
        total = outs.finish()
        gout_v[:band_half] = total[:, :head_width]
        gout_v[band_half:] = total[:, head_width:]
        stores.append(fetch(gout_v, gout_hbm))

    def finish_proj(part):
        total = projs[part].finish()
        goal = quarters * part + me
        dest, where = lax.div(goal, 3), lax.rem(goal, 3)

        @pl.when(dest == me)
        def _():
            slots[where] = total

        @pl.when(dest != me)
        def _():
            fin[part] = total
            pltpu.make_async_remote_copy(
                src_ref=fin.at[part], dst_ref=slots.at[where],
                send_sem=sems.at[0, last + part], recv_sem=sems.at[1, last + where],
                device_id=(dp, dest), device_id_type=MESH,
            ).start()

    def collect():
        for index in range(3):
            goal = quarters * index + me
            source = lax.rem(3 * me + index, quarters)

            @pl.when(lax.div(goal, 3) != me)
            def _():
                copy_to(fin.at[index], slots.at[0], sems, last + index, mate).wait_send()

            @pl.when(source != me)
            def _():
                copy_to(fin.at[0], slots.at[index], sems, last + index, mate).wait_recv()

        for index in range(3):
            got = slots[index]
            cols = slice(head_width * index, head_width * (index + 1))
            gqkv_v[:band_half, cols] = got[:, :head_width]
            gqkv_v[band_half:, cols] = got[:, head_width:]
        stores.append(fetch(gqkv_v, gqkv_hbm))

    table = {
        "DG": down_gradient, "FB": branch_back,
        "HB0": lambda: hidden_back((0,)), "HB1": lambda: hidden_back((1, 2, 3)),
        "HB2": lambda: hidden_back((0, 1)), "HB3": lambda: hidden_back((2, 3)),
        "OG": out_gradient, "AV": values_back,
        "SM": softmax_back, "MM": middle_back, "IN": input_gradient, "GQ": collect,
        "LF": low_onward, "GF": g2_onward, "UH": up_slopes,
        "NB1": lambda: newton_back((5, 4, 3)), "NB2": lambda: newton_back((2, 1, 0)),
    }
    for q in range(3):
        table["UG%d" % q] = lambda q=q: up_gradient(q)
        table["QG%d" % q] = lambda q=q: qkv_gradient(q)
    for k in range(6):
        table["S%d" % k] = lambda k=k: sum_step(k)
    names = {"O": (outs, finish_out)}
    for q in range(3):
        names["D%d" % q] = (downs[q], lambda q=q: finish_down(q))
        names["U%d" % q] = (ups[q], lambda q=q: finish_up(q))
        names["P%d" % q] = (projs[q], lambda q=q: finish_proj(q))
    for item in SCHEDULE:
        if item in table:
            table[item]()
        else:
            chunk, finish = names[item]
            if chunk.stage == len(chunk.bits) - 1:
                finish()
            else:
                chunk.step()
    for copy in stores:
        copy.wait()


def final_kernel(*refs):
    sem = refs[-1]
    count = (len(refs) - 1) // 3
    inward = [
        pltpu.make_async_copy(refs[i], refs[2 * count + i], sem.at[0, i]) for i in range(count)
    ]
    outward = [
        pltpu.make_async_copy(refs[2 * count + i], refs[count + i], sem.at[1, i])
        for i in range(count)
    ]
    for copy in inward:
        copy.start()
    for got, put in zip(inward, outward):
        got.wait()
        put.start()
    for copy in outward:
        copy.wait()


def per_device_fast(
    tokens, w_qkv, w_out, w_up, w_down, norm_gains, norm_shifts, conv_kernels, seq_lengths,
    seg_bounds, out_grad,
):
    rows, width = tokens.shape
    ff = w_up.shape[1]
    head_width = width // 4
    slot = 4 * rows
    band, down_cols = width // 8, ff // 8
    whole = pl.BlockSpec(memory_space=VMEM)
    anywhere = pl.BlockSpec(memory_space=pl.ANY)
    shape = jax.ShapeDtypeStruct
    outs = (
        shape((rows, width), BF16),
        shape((rows, width), BF16),
        shape((band, w_qkv.shape[1] // 4), F32),
        shape((band, width // 4), F32),
        shape((band, ff // 4), F32),
        shape((width // 4, down_cols), F32),
        shape(norm_gains.shape, F32),
        shape(norm_shifts.shape, F32),
        shape(conv_kernels.shape, F32),
    )
    found = pl.pallas_call(
        main_kernel,
        out_shape=outs,
        in_specs=[anywhere] * 6
        + [whole] * 3
        + [pl.BlockSpec(memory_space=pltpu.SMEM), whole],
        out_specs=[anywhere] * 9,
        scratch_shapes=[
            VMEM((rows, width), BF16), VMEM((rows, width), BF16),
            VMEM(w_qkv.shape, BF16), VMEM(w_out.shape, BF16),
            VMEM(w_up.shape, BF16), VMEM(w_down.shape, BF16),
            pltpu.SemaphoreType.DMA((32,)), pltpu.SemaphoreType.DMA((2, 120)),
            VMEM((4, rows, width), BF16),
            VMEM((3, 256, width), BF16),
            VMEM((2, conv_kernels.shape[0], 384), F32),
            VMEM((3 * head_width, slot), BF16),
            VMEM((head_width, slot), F32), VMEM((head_width, slot), F32),
            VMEM((NEWTON, 4, DIM, head_width), F32),
            VMEM((6, DIM, head_width), F32),
            VMEM((head_width, slot), BF16),
            VMEM((width, rows), BF16), VMEM((width, rows), BF16),
            VMEM((4, rows, width), BF16), VMEM((4, rows, width), BF16),
            VMEM((2 * rows, ff), BF16),
            VMEM((width, rows), BF16), VMEM((width, rows), BF16),
            VMEM((rows, ff), F32),
            VMEM((rows, ff), BF16),
            VMEM((rows, width), BF16), VMEM((rows, width), BF16),
            VMEM((width, rows), BF16),
            VMEM((head_width, slot), BF16),
            VMEM((3 * head_width, slot), BF16),
            VMEM((3 * width, rows), BF16),
            VMEM((rows, width), F32), VMEM((rows, width), F32), VMEM((rows, width), F32),
            VMEM((5, 8, width), F32), VMEM((5, 8, width), F32),
            VMEM((3, band // 2, 2 * head_width), F32),
            VMEM((3, band // 2, 2 * head_width), F32),
            VMEM((3, 16, 64, down_cols), BF16), VMEM((3, 15, 64, down_cols), BF16),
            VMEM((3, 8, band, 256), BF16), VMEM((3, 7, band, 256), BF16),
            VMEM((16, band // 2, 2 * head_width), BF16),
            VMEM((15, band // 2, 2 * head_width), BF16),
            VMEM((3, 8, band // 2, 2 * head_width), BF16),
            VMEM((3, 7, band // 2, 2 * head_width), BF16),
        ]
        + [VMEM(out.shape, out.dtype) for out in outs],
        compiler_params=pltpu.CompilerParams(
            collective_id=0, has_side_effects=True, vmem_limit_bytes=63 * 2**20
        ),
        name="main_kernel",
    )(
        tokens, out_grad, w_qkv, w_out, w_up, w_down, norm_gains, norm_shifts, conv_kernels,
        seq_lengths, seg_bounds,
    )
    copied = pl.pallas_call(
        final_kernel,
        out_shape=outs,
        in_specs=[anywhere] * 9,
        out_specs=[anywhere] * 9,
        scratch_shapes=[VMEM(out.shape, out.dtype) for out in outs]
        + [pltpu.SemaphoreType.DMA((2, 9))],
        name="final_kernel",
    )(*found)
    copied = tuple(copied)
    return copied[:5] + (copied[5].T,) + copied[6:]


highest = lax.Precision.HIGHEST
epsilon = 1e-05


def layer_norm(values, gain, shift):
    center = jnp.mean(values, axis=-1, keepdims=True)
    centred = values - center
    spread_sq = jnp.mean(centred * centred, axis=-1, keepdims=True)
    return centred * lax.rsqrt(spread_sq + epsilon) * gain + shift


def exact_gelu(values):
    return jax.nn.gelu(values, approximate=False)


def shifted_conv(values, kernel):
    slot_len = values.shape[0]
    taps = kernel.shape[0]
    half_width = taps // 2
    padded = jnp.pad(values, ((half_width, half_width), (0, 0)))
    total = jnp.zeros_like(values)
    for offset in range(taps):
        total = total + kernel[offset] * padded[offset : offset + slot_len]
    return total


def nystrom_head(queries, keys, values, kernel, length, bounds):
    slot_len = queries.shape[0]
    mark_count = bounds.shape[0] - 1
    head_dim = queries.shape[1]
    places = jnp.arange(slot_len, dtype=jnp.int32)
    valid = places < length
    weight_mask = valid.astype(jnp.float32)[:, None]
    scaling = head_dim ** (-0.25)
    queries = queries * weight_mask * scaling
    keys = keys * weight_mask * scaling
    values = values * weight_mask
    member = ((places[None, :] >= bounds[:-1, None]) & (places[None, :] < bounds[1:, None])).astype(
        jnp.float32
    )
    counts = (bounds[1:] - bounds[:-1]).astype(jnp.float32)[:, None]
    query_marks = jnp.dot(member, queries, precision=highest) / counts
    key_marks = jnp.dot(member, keys, precision=highest) / counts
    first = jax.nn.softmax(jnp.dot(queries, key_marks.T, precision=highest), axis=-1)
    middle = jax.nn.softmax(jnp.dot(query_marks, key_marks.T, precision=highest), axis=-1)
    third_scores = jnp.dot(query_marks, keys.T, precision=highest)
    third = jax.nn.softmax(jnp.where(valid[None, :], third_scores, -1000000000.0), axis=-1)
    inverse = middle.T / (jnp.max(jnp.sum(middle, axis=0)) * jnp.max(jnp.sum(middle, axis=1)))
    identity = jnp.eye(mark_count, dtype=jnp.float32)
    for _ in range(NEWTON):
        product = jnp.dot(middle, inverse, precision=highest)
        inner = 7.0 * identity - product
        inner = 15.0 * identity - jnp.dot(product, inner, precision=highest)
        inner = 13.0 * identity - jnp.dot(product, inner, precision=highest)
        inverse = 0.25 * jnp.dot(inverse, inner, precision=highest)
    summary = jnp.dot(third, values, precision=highest)
    mixed = jnp.dot(first, jnp.dot(inverse, summary, precision=highest), precision=highest)
    return (mixed + shifted_conv(values, kernel)) * weight_mask


def attend(packed, kernels, lengths, bounds):
    seq_count = lengths.shape[0]
    head_count = kernels.shape[0]
    head_dim = packed.shape[-1] // (3 * head_count)
    grouped = packed.reshape(seq_count, -1, 3, head_count, head_dim)
    over_heads = jax.vmap(nystrom_head, in_axes=(1, 1, 1, 0, None, None), out_axes=1)
    over_seqs = jax.vmap(over_heads, in_axes=(0, 0, 0, None, 0, 0))
    result = over_seqs(
        grouped[:, :, 0], grouped[:, :, 1], grouped[:, :, 2], kernels, lengths, bounds
    )
    return result.reshape(seq_count * grouped.shape[1], head_count * head_dim)


def row_contract(left, right):
    return lax.dot_general(
        left, right, (((0,), (0,)), ((), ())), preferred_element_type=jnp.float32
    )


def to_blocks(matrix, dp_count, quarters):
    total_rows, total_cols = matrix.shape
    shaped = matrix.reshape(dp_count, total_rows // dp_count, quarters, total_cols // quarters)
    return shaped.transpose(0, 2, 1, 3).reshape(total_rows * quarters, total_cols // quarters)


def per_device(
    tokens,
    w_qkv,
    w_out,
    w_up,
    w_down,
    norm_gains,
    norm_shifts,
    conv_kernels,
    seq_lengths,
    seg_bounds,
    out_grad,
):
    quarters = lax.axis_size("head")
    quarter = lax.axis_index("head")
    dp_count = lax.axis_size("dp")
    tok_rows, width = tokens.shape
    seq_count = seq_lengths.shape[0]
    group_rows = tok_rows * quarters
    slot_len = group_rows // seq_count
    head_count, kernel_len = conv_kernels.shape
    local_heads = head_count // quarters
    head_width = w_qkv.shape[1] // (3 * quarters)
    places = quarter * tok_rows + jnp.arange(tok_rows, dtype=jnp.int32)
    owners = places // slot_len
    within = places % slot_len
    limits = jnp.sum(
        jnp.where(
            owners[:, None] == jnp.arange(seq_count, dtype=jnp.int32)[None, :],
            seq_lengths[None, :],
            0,
        ),
        axis=1,
    )
    live = (within < limits).astype(jnp.float32)[:, None]
    local_kernels = lax.dynamic_slice_in_dim(
        conv_kernels.astype(jnp.float32), quarter * local_heads, local_heads, 0
    )
    projected = jnp.dot(tokens, w_qkv, preferred_element_type=jnp.float32).astype(jnp.bfloat16)
    packed = lax.all_to_all(
        projected.reshape(tok_rows, 3, quarters, head_width),
        "head",
        split_axis=2,
        concat_axis=0,
        tiled=True,
    )
    packed_rows = packed.reshape(group_rows, 3 * head_width)

    def attention_piece(packed_in, kernel_in):
        return attend(packed_in, kernel_in, seq_lengths, seg_bounds)

    attended, attention_back = jax.vjp(
        attention_piece, packed_rows.astype(jnp.float32), local_kernels
    )
    attended_low = attended.astype(jnp.bfloat16)
    heads_rows = lax.all_to_all(
        attended_low.reshape(group_rows, 1, head_width),
        "head",
        split_axis=0,
        concat_axis=1,
        tiled=True,
    ).reshape(tok_rows, width)
    branch = jnp.dot(heads_rows, w_out, preferred_element_type=jnp.float32)
    first_in = tokens.astype(jnp.float32) + branch
    first_norm, first_back = jax.vjp(layer_norm, first_in, norm_gains[0], norm_shifts[0])
    first_low = first_norm.astype(jnp.bfloat16)
    hidden = jnp.dot(first_low, w_up, preferred_element_type=jnp.float32)
    activated, gelu_back = jax.vjp(exact_gelu, hidden)
    act_low = activated.astype(jnp.bfloat16)
    second = jnp.dot(act_low, w_down, preferred_element_type=jnp.float32)
    output, second_back = jax.vjp(layer_norm, first_norm + second, norm_gains[1], norm_shifts[1])
    cotangent = out_grad.astype(jnp.float32) * live
    grad_second_in, grad_gain_two, grad_shift_two = second_back(cotangent)
    grad_second = grad_second_in.astype(jnp.bfloat16)
    grad_down = row_contract(act_low, grad_second)
    grad_act = jnp.dot(grad_second, w_down.T, preferred_element_type=jnp.float32)
    grad_hidden = gelu_back(grad_act)[0].astype(jnp.bfloat16)
    grad_up = row_contract(first_low, grad_hidden)
    grad_first = grad_second_in + jnp.dot(grad_hidden, w_up.T, preferred_element_type=jnp.float32)
    grad_first_in, grad_gain_one, grad_shift_one = first_back(grad_first)
    grad_branch = grad_first_in.astype(jnp.bfloat16)
    grad_wout = row_contract(heads_rows, grad_branch)
    grad_heads = jnp.dot(grad_branch, w_out.T, preferred_element_type=jnp.float32).astype(
        jnp.bfloat16
    )
    heads_grad = lax.all_to_all(
        grad_heads.reshape(tok_rows, quarters, head_width),
        "head",
        split_axis=1,
        concat_axis=0,
        tiled=True,
    ).reshape(group_rows, head_width)
    grad_packed, grad_local_kernels = attention_back(heads_grad.astype(jnp.float32))
    grad_packed_low = grad_packed.astype(jnp.bfloat16).reshape(group_rows, 3, 1, head_width)
    grad_projected = lax.all_to_all(
        grad_packed_low, "head", split_axis=0, concat_axis=2, tiled=True
    ).reshape(tok_rows, 3 * quarters * head_width)
    grad_wqkv = row_contract(tokens, grad_projected)
    input_grad = (
        grad_first_in + jnp.dot(grad_projected, w_qkv.T, preferred_element_type=jnp.float32)
    ).astype(jnp.bfloat16)
    kernel_full = lax.dynamic_update_slice_in_dim(
        jnp.zeros((head_count, kernel_len), jnp.float32),
        grad_local_kernels,
        quarter * local_heads,
        0,
    )
    small_sums = lax.psum(
        (
            jnp.stack([grad_gain_one, grad_gain_two]),
            jnp.stack([grad_shift_one, grad_shift_two]),
            kernel_full,
        ),
        ("dp", "head"),
    )
    blocked_qkv = to_blocks(grad_wqkv, dp_count, quarters)
    blocked_out = to_blocks(grad_wout, dp_count, quarters)
    blocked_up = to_blocks(grad_up, dp_count, quarters)
    blocked_down = to_blocks(grad_down, dp_count, quarters)
    weight_sums = (
        lax.psum_scatter(blocked_qkv, ("dp", "head"), scatter_dimension=0, tiled=True),
        lax.psum_scatter(blocked_out, ("dp", "head"), scatter_dimension=0, tiled=True),
        lax.psum_scatter(blocked_up, ("dp", "head"), scatter_dimension=0, tiled=True),
        lax.psum_scatter(blocked_down, ("dp", "head"), scatter_dimension=0, tiled=True),
    )
    return (
        output.astype(jnp.bfloat16),
        input_grad,
        weight_sums[0],
        weight_sums[1],
        weight_sums[2],
        weight_sums[3],
        small_sums[0],
        small_sums[1],
        small_sums[2],
    )


def solution(mesh):
    placed = (
        P(("dp", "head"), None),
        P(),
        P(),
        P(),
        P(),
        P(),
        P(),
        P(),
        P("dp"),
        P("dp", None),
        P(("dp", "head"), None),
    )
    aligned = mesh.shape["dp"] == 8 and mesh.shape["head"] == 4
    return jax.shard_map(
        per_device_fast if aligned else per_device,
        mesh=mesh,
        in_specs=placed,
        out_specs=(
            P(("dp", "head"), None),
            P(("dp", "head"), None),
            P("dp", "head"),
            P("dp", "head"),
            P("dp", "head"),
            P("dp", "head"),
            P(),
            P(),
            P(),
        ),
        check_vma=False,
    )
```

```python
import jax
import jax.numpy as jnp
from jax import lax
from jax.sharding import PartitionSpec as P
from jax.experimental import pallas as pl
from jax.experimental.pallas import tpu as pltpu

MESH = pl.DeviceIdType.MESH
NEWTON = 6
F32 = jnp.float32
BF16 = jnp.bfloat16
VMEM = pltpu.VMEM
HEADS_HERE = 3
DIM = 64
TAPS = 33


def mm(a, b, ca, cb):
    return lax.dot_general(a, b, (((ca,), (cb,)), ((), ())), preferred_element_type=F32)


def halves(value):
    high = value.astype(BF16)
    return high, (value - high.astype(F32)).astype(BF16)


def cat(parts, axis):
    return jnp.concatenate(parts, axis=axis)


class Packs:
    def __init__(self):
        lane = lax.broadcasted_iota(jnp.int32, (1, HEADS_HERE * DIM), 1)
        self.hit = [(lane // DIM == h).astype(F32) for h in range(HEADS_HERE)]
        self.low_hit = [h.astype(BF16) for h in self.hit]
        rows = lax.broadcasted_iota(jnp.int32, (DIM, HEADS_HERE * DIM), 0)
        cols = lax.broadcasted_iota(jnp.int32, (DIM, HEADS_HERE * DIM), 1)
        self.unit = (rows == cols % DIM).astype(F32)

    def block(self, low):
        return cat([low * h for h in self.low_hit], 0)

    def times(self, lhs, rhs, side=0):
        rows = lhs.shape[0]
        l_high, l_low = halves(lhs)
        r_high, r_low = halves(rhs)
        both = mm(cat([l_high, l_low], 0), self.block(r_high), 1, side)
        return both[:rows] + both[rows:] + mm(l_high, self.block(r_low), 1, side)

    def diagonal(self, full):
        total = full[:DIM] * self.hit[0]
        for h in range(1, HEADS_HERE):
            total = total + full[DIM * h : DIM * (h + 1)] * self.hit[h]
        return total

    def turn(self, value):
        tall = value.T
        return cat([tall[DIM * h : DIM * (h + 1)] for h in range(HEADS_HERE)], 1)

    def each(self, values):
        total = values[0] * self.hit[0]
        for h in range(1, HEADS_HERE):
            total = total + values[h] * self.hit[h]
        return total

    def row_max(self, value):
        return self.each(
            [
                jnp.max(jnp.where(h > 0, value, -jnp.inf), axis=1, keepdims=True)
                for h in self.hit
            ]
        )

    def row_sum(self, value):
        return self.each([jnp.sum(value * h, axis=1, keepdims=True) for h in self.hit])


def expand(block_low, lhs_side, wide):
    return mm(block_low, wide, lhs_side, 0)


def toeplitz(base):
    rows = jnp.broadcast_to(base, (128, base.shape[1]))
    return pltpu.roll(rows, 0, 1, stride=1, stride_axis=0).astype(BF16)


def windows(mat):
    zero = jnp.zeros((mat.shape[0], 128), mat.dtype)
    wide = cat([zero, mat, zero], 1)
    return cat([wide[:, 128 * b : 128 * b + 384] for b in range(mat.shape[1] // 128)], 0)


def unwindow(stacked, rows):
    return cat([stacked[rows * b : rows * (b + 1)] for b in range(stacked.shape[0] // rows)], 1)


def gelu_pair(hidden):
    tail = jnp.exp(-0.5 * hidden * hidden)
    t = 1.0 / (1.0 + 0.23164190 * jnp.abs(hidden))
    poly = 1.330274429
    for term in (-1.821255978, 1.781477937, -0.356563782, 0.319381530):
        poly = poly * t + term
    density = 0.3989422804014327 * tail
    below = density * poly * t
    normal = jnp.where(hidden >= 0.0, 1.0 - below, below)
    return hidden * normal, normal + hidden * density


def norm_forward(values):
    center = jnp.mean(values, axis=-1, keepdims=True)
    centred = values - center
    spread = jnp.mean(centred * centred, axis=-1, keepdims=True)
    root = lax.rsqrt(spread + 1e-5)
    return centred * root, root


def norm_backward(grad, gain, normed, root):
    scaled = grad * gain
    center = jnp.mean(scaled, axis=-1, keepdims=True)
    along = jnp.mean(scaled * normed, axis=-1, keepdims=True)
    return root * (scaled - center - normed * along)


def copy_to(src, dst, sems, index, device):
    return pltpu.make_async_remote_copy(
        src_ref=src,
        dst_ref=dst,
        send_sem=sems.at[0, index],
        recv_sem=sems.at[1, index],
        device_id=device,
        device_id_type=MESH,
    )


def greet(devices):
    barrier = pltpu.get_barrier_semaphore()
    for device in devices:
        pl.semaphore_signal(barrier, inc=1, device_id=device, device_id_type=MESH)
    return lambda: pl.semaphore_wait(barrier, len(devices))


class Spread:
    def __init__(self, acc, got, bits, sems, base):
        self.acc, self.got, self.bits, self.sems, self.base = acc, got, bits, sems, base
        self.blocks = acc.shape[0]
        self.stage = 0
        self.offset = 0
        self.at = 0
        self.sent = []

    def start(self):
        bit, device = self.bits[self.stage]
        size = self.blocks >> (self.stage + 1)
        self.keep = self.offset + bit * size
        other = self.offset + (1 - bit) * size
        self.flight = copy_to(
            self.acc.at[pl.ds(other, size)], self.got.at[pl.ds(self.at, size)],
            self.sems, self.base + self.stage, device,
        )
        self.flight.start()
        self.size = size

    def take(self):
        self.flight.wait_recv()
        self.sent.append(self.flight)
        mine, new = pl.ds(self.keep, self.size), pl.ds(self.at, self.size)
        self.at += self.size
        self.offset = self.keep
        self.stage += 1
        if self.stage == len(self.bits):
            return self.acc[mine].astype(F32) + self.got[new].astype(F32)
        self.acc[mine] = self.acc[mine] + self.got[new]
        return None

    def step(self):
        self.take()
        self.start()

    def finish(self):
        total = self.take()
        for sent in self.sent:
            sent.wait_send()
        return total[0]


def position(order, values):
    spot = 0
    for name in order:
        spot = 2 * spot + values[name]
    return spot


DOWN_ORDERS = ("lxyh", "lxyh", "yxlh")
UP_ORDERS = ("lyh", "ylh", "ylh")
OUT_ORDER = "xylh"
SUM_ORDER = "lhcyx"
QKV_ORDERS = ("ylh", "ylh", "ylh")
SCHEDULE = (
    "HB0", "DG", "HB1", "FB", "UH0", "LF", "UGA", "D2", "D0", "GF", "OG", "UH1", "UGB", "UG0",
    "UG1", "AV", "S0", "QG2", "D1", "NB1", "D2", "UG2", "SN", "U1", "SM", "U0", "D0", "S1",
    "NB2", "P2", "D2", "MM", "U1", "QG0", "S2", "QG1", "U2", "O", "P2", "S3", "D2", "U0",
    "U1", "D0", "U2", "P2", "P0", "U0", "D1", "D0", "P1", "U2", "P0", "O", "S4", "P1", "P0",
    "D1", "IN", "P1", "O", "S5", "D1", "O", "GQ",
)


def main_kernel(
    tok_hbm, grad_hbm, wqkv_hbm, wout_hbm, wup_hbm, wdown_hbm,
    gain_ref, shift_ref, taps_ref, len_ref, bounds_ref,
    out_hbm, in_hbm, gqkv_hbm, gout_hbm, gup_hbm, gdown_hbm, ggain_hbm, gshift_hbm, gtaps_hbm,
    tok, grad_in, w_qkv, w_out, w_up, w_down, lsem, sems,
    everyone, wt, bases, packed, a1, a3, chain, marks, att, heads, heads_x,
    low_all, g2_all, act, gst, gst_x, slope, gh, gb, gb_x, gatt, g_in, gproj, gp_in,
    first_ref, norm1_ref, gr1_ref, sum_s, sum_r, fin, slots,
    acc_down, got_down, acc_up, got_up, acc_out, got_out, acc_qkv, got_qkv,
    out_v, in_v, gqkv_v, gout_v, gup_v, gdown_v, ggain_v, gshift_v, gtaps_v,
):
    dp = lax.axis_index("dp")
    me = lax.axis_index("head")
    quarters = 4
    rows, width = tok.shape
    slot = rows * quarters
    hidden_width = w_up.shape[1]
    block = hidden_width // quarters
    head_width = width // quarters
    count = DIM
    nh = HEADS_HERE
    band_rows = width // 8
    down_cols = hidden_width // 8
    core = lax.rem(me, 2)
    mate = (dp, me ^ 1)
    bits = {
        "x": (lax.div(me, 2), (dp, me ^ 2)),
        "y": (lax.rem(dp, 2), (dp ^ 1, me)),
        "l": (lax.rem(lax.div(dp, 2), 2), (dp ^ 2, me)),
        "h": (lax.div(dp, 4), (dp ^ 4, me)),
    }
    counter = iter(range(200))
    local = iter(range(40))

    def fetch(src, dst):
        copy = pltpu.make_async_copy(src, dst, lsem.at[next(local)])
        copy.start()
        return copy

    def send(src, dst, device):
        copy = copy_to(src, dst, sems, next(counter), device)
        copy.start()
        return copy

    def reserve(n):
        base = next(counter)
        for _ in range(n - 1):
            next(counter)
        return base

    def spread(acc, got, order):
        return Spread(acc, got, [bits[name] for name in order], sems, reserve(len(order)))

    all_here = greet([(dp, me ^ k) for k in (1, 2, 3)] + [(dp ^ k, me) for k in (1, 2, 4)])
    own_fetch = fetch(tok_hbm, everyone.at[me])
    tok_fetch = fetch(tok_hbm, tok)
    wqkv_fetch = fetch(wqkv_hbm, w_qkv)
    all_here()
    half = rows // 4
    far = []
    for piece in range(4):
        part = pl.ds(piece * half, half)
        far.append(send(tok_hbm.at[part], everyone.at[me, part], (dp, me ^ 2)))
    near = send(tok_hbm, everyone.at[me], mate)
    wqkv_fetch.wait()
    wout_fetch = fetch(wout_hbm, w_out)
    wup_fetch = fetch(wup_hbm, w_up)
    wdown_fetch = fetch(wdown_hbm, w_down)
    grad_fetch = fetch(grad_hbm, grad_in)
    odd = lax.rem(me, 2)
    for part in range(3):
        start = pl.multiple_of(part * width + 2 * head_width * lax.div(me, 2) + 128 * odd, 128)
        wt[part] = w_qkv[:, pl.ds(start, 256)].T
    w_own = cat(
        [wt[part, pl.ds(pl.multiple_of(64 * odd, 64), head_width), :] for part in range(3)], 0
    )
    packs = Packs()
    lane = lax.broadcasted_iota(jnp.int32, (TAPS, 384), 1)
    tap = lax.broadcasted_iota(jnp.int32, (TAPS, 384), 0)
    for turn, spots in enumerate((tap + 112, 144 - tap)):
        bases[turn] = mm(taps_ref[...], (lane == spots).astype(F32).astype(BF16), 1, 0)
    bands = [
        [toeplitz(bases[turn, pl.ds(nh * me + h, 1), :]) for h in range(nh)] for turn in range(2)
    ]
    edges = bounds_ref[...].astype(F32)
    low_edge = jnp.broadcast_to(edges[:, :count], (count, count)).T[:, 0:1]
    high_edge = jnp.broadcast_to(edges[:, 1 : count + 1], (count, count)).T[:, 0:1]
    place = lax.broadcasted_iota(jnp.int32, (count, slot), 1).astype(F32)
    member = ((place >= low_edge) & (place < high_edge)).astype(F32).astype(BF16)
    share_of = 1.0 / (high_edge - low_edge)
    length = len_ref[0]
    live = lax.broadcasted_iota(jnp.int32, (1, slot), 1) < length
    scale = DIM ** (-0.25)

    def project(which):
        lanes = pl.ds(pl.multiple_of(rows * which, rows), rows)
        packed[:, lanes] = mm(w_own, everyone[which], 1, 1).astype(BF16)

    own_fetch.wait()
    project(me)
    near.wait()
    project(me ^ 1)
    onward = []
    for piece in range(4):
        part = pl.ds(piece * half, half)
        far[piece].wait()
        onward.append(send(everyone.at[me ^ 2, part], everyone.at[me ^ 2, part], mate))
    project(me ^ 2)
    for copy in onward:
        copy.wait()
    project(me ^ 3)
    queries = packed[:head_width]
    keys = packed[head_width : 2 * head_width]
    q_marks = mm(member, queries, 1, 1) * (scale * share_of)
    k_marks = mm(member, keys, 1, 1) * (scale * share_of)
    marks[0] = q_marks
    marks[1] = k_marks
    scores = packs.times(q_marks, k_marks, 1)
    powers = jnp.exp(scores - packs.row_max(scores))
    middle = powers / packs.row_sum(powers)
    marks[2] = middle
    col_sums = jnp.sum(middle, axis=0, keepdims=True)
    col_top = packs.row_max(col_sums)
    row_top = jnp.max(packs.row_sum(middle), axis=0, keepdims=True)
    inverse_t = middle / (col_top * row_top)
    product = packs.times(inverse_t, middle, 1)
    for step in range(NEWTON):
        second = packs.times(product, product)
        pair = packs.times(cat([product, second], 0), second)
        third, fourth = pair[:count], pair[count:]
        for i, value in enumerate((product, second, third, inverse_t)):
            chain[step, i] = value
        blend = 0.25 * (13.0 * packs.unit - 15.0 * product + 7.0 * second - third)
        product = 0.25 * (13.0 * product - 15.0 * second + 7.0 * third - fourth)
        inverse_t = packs.times(blend, inverse_t)
    marks[3] = inverse_t
    def tall_scores(values, wide):
        high, low = halves(values * scale)
        both = mm(cat([packs.block(high), packs.block(low)], 0), wide, 1, 0)
        return both[:head_width] + both[head_width:]

    def per_head(value):
        return value.reshape(nh, count, slot)

    scores = per_head(tall_scores(k_marks, queries))
    powers = jnp.exp(scores - jnp.max(scores, axis=1, keepdims=True))
    first = (powers * (1.0 / jnp.sum(powers, axis=1, keepdims=True))).reshape(head_width, slot)
    a1[...] = first
    scores = jnp.where(live, tall_scores(q_marks, keys), -1e9)
    powers = jnp.exp(scores - jnp.max(scores, axis=1, keepdims=True))
    third = powers * (1.0 / jnp.sum(powers, axis=1, keepdims=True))
    a3[...] = third
    values = jnp.where(live, packed[2 * head_width :].astype(F32), 0.0).astype(BF16)
    t_high, t_low = halves(third)
    summary_t = packs.diagonal(mm(values, t_high, 1, 1) + mm(values, t_low, 1, 1))
    weights_t = packs.times(summary_t, inverse_t)
    marks[4] = summary_t
    marks[5] = weights_t
    w_high, w_low = halves(weights_t)
    f_high, f_low = halves(first)
    mixed = mm(cat([packs.block(w_high), packs.block(w_low)], 0), f_high, 1, 0)
    mixed = mixed[:head_width] + mixed[head_width:] + mm(packs.block(w_high), f_low, 1, 0)
    mine = pl.ds(pl.multiple_of(rows * me, rows), rows)
    own_rows = pl.ds(pl.multiple_of(head_width * me, 64), head_width)
    att_sent = []
    for h in range(nh):
        part = slice(DIM * h, DIM * (h + 1))
        conv = unwindow(mm(windows(values[part]), bands[0][h], 1, 1), DIM)
        att[part] = jnp.where(live, mixed[part] + conv, 0.0).astype(BF16)
        goal = pl.ds(pl.multiple_of(head_width * me + DIM * h, 64), DIM)
        for k in (2, 3, 1):
            lanes = pl.ds(pl.multiple_of(rows * (me ^ k), rows), rows)
            att_sent.append(send(att.at[part, lanes], heads.at[goal], (dp, me ^ k)))
    heads[own_rows] = att[:, mine]
    wout_fetch.wait()
    tok_fetch.wait()
    for copy in att_sent:
        copy.wait()
    heads_sent = send(heads, heads_x, mate)
    branch = mm(heads[...], w_out[...], 0, 0)
    normed, root_one = norm_forward(tok[...].astype(F32) + branch)
    norm1_ref[...] = normed
    first_norm = normed * gain_ref[0:1] + shift_ref[0:1]
    first_ref[...] = first_norm
    low = first_norm.astype(BF16)
    low_all[me] = low
    low_far = send(low_all.at[me], low_all.at[me], (dp, me ^ 2))
    low_near = send(low_all.at[me], low_all.at[me], mate)
    wup_fetch.wait()
    wdown_fetch.wait()
    second_sum = None
    act_sent = []
    for i in range(quarters):
        cols = slice(block * i, block * (i + 1))
        active, slope_part = gelu_pair(mm(low, w_up[:, cols], 1, 0))
        active = active.astype(BF16)
        act[:rows, cols] = active
        act_sent.append(send(act.at[:rows, cols], act.at[rows:, cols], mate))
        slope[:, cols] = slope_part
        part = mm(active, w_down[cols, :], 1, 0)
        second_sum = part if second_sum is None else second_sum + part
    normed_two, root_two = norm_forward(first_ref[...] + second_sum)
    grad_fetch.wait()
    spot = me * rows + lax.broadcasted_iota(jnp.int32, (rows, 1), 0)
    cotangent = jnp.where(spot < length, grad_in[...].astype(F32), 0.0)
    g_two = norm_backward(cotangent, gain_ref[1:2], normed_two, root_two)
    g_low = g_two.astype(BF16)
    g2_all[me] = g_low
    g2_far = send(g2_all.at[me], g2_all.at[me], (dp, me ^ 2))
    gst[...] = g_low.T
    gst_sent = send(gst, gst_x, mate)
    g2_near = send(g2_all.at[me], g2_all.at[me], mate)
    gr1_ref[...] = g_two
    out_v[...] = (normed_two * gain_ref[1:2] + shift_ref[1:2]).astype(BF16)
    stores = [fetch(out_v, out_hbm)]
    sum_s[0] = jnp.zeros(sum_s.shape[1:], F32)
    sum_s[0, 1:2] = jnp.sum(cotangent * normed_two, axis=0, keepdims=True)
    sum_s[0, 3:4] = jnp.sum(cotangent, axis=0, keepdims=True)
    s = {}
    downs = [spread(acc_down.at[q], got_down.at[q], DOWN_ORDERS[q]) for q in range(3)]
    ups = [spread(acc_up.at[q], got_up.at[q], UP_ORDERS[q]) for q in range(3)]
    outs = spread(acc_out, got_out, OUT_ORDER)
    projs = [spread(acc_qkv.at[j], got_qkv.at[j], QKV_ORDERS[j]) for j in range(3)]
    sum_base = reserve(5)
    last = reserve(3)
    band_half = band_rows // 2
    p_sent = []

    def folded(total, d):
        top = band_rows * d
        return cat([total[top : top + band_half], total[top + band_half : top + band_rows]], 1)

    def places(x, d):
        return {"x": x, "y": d % 2, "l": d // 2 % 2, "h": d // 4}

    def down_gradient():
        for copy in act_sent:
            copy.wait()
        gst_sent.wait()
        tops = [pl.ds(pl.multiple_of(head_width * (2 * x + core), 64), head_width) for x in (0, 1)]
        lead = cat([cat([gst[top, :], gst_x[top, :]], 1) for top in tops], 0)
        for pair in range(4):
            total = mm(lead, act[:, 2 * down_cols * pair : 2 * down_cols * (pair + 1)], 1, 0)
            total = total.astype(BF16)
            for x in range(2):
                for inner in range(2):
                    at = places(x, 2 * pair + inner)
                    for q in range(3):
                        top = head_width * x + 64 * q
                        acc_down[q, position(DOWN_ORDERS[q], at)] = total[
                            top : top + 64, down_cols * inner : down_cols * (inner + 1)
                        ]
        for chunk in downs:
            chunk.start()

    def hidden_back(turns):
        g_first = s.get("g_first", g_two)
        for i in turns:
            cols = slice(block * i, block * (i + 1))
            part = (slope[:, cols] * mm(g_low, w_down[cols, :], 1, 1)).astype(BF16)
            gh[:, cols] = part
            g_first = g_first + mm(part, w_up[:, cols], 1, 1)
        s["g_first"] = g_first

    def branch_back():
        g_first = s["g_first"]
        normed = norm1_ref[...]
        sum_s[0, 0:1] = jnp.sum(g_first * normed, axis=0, keepdims=True)
        sum_s[0, 2:3] = jnp.sum(g_first, axis=0, keepdims=True)
        g_one = norm_backward(g_first, gain_ref[0:1], normed, root_one)
        gr1_ref[...] = g_one
        g_branch = g_one.astype(BF16)
        gb[...] = g_branch
        gatt[...] = mm(w_out[...], g_branch, 1, 1).astype(BF16)
        s["g"] = []
        for k in (2, 3, 1):
            src = gatt.at[pl.ds(pl.multiple_of(head_width * (me ^ k), 64), head_width)]
            s["g"].append(send(src, g_in.at[:, mine], (dp, me ^ k)))
        s["gb"] = send(gb, gb_x, mate)
        g_in[:, mine] = gatt[own_rows]

    own_cols = pl.ds(pl.multiple_of(block * me, 128), block)

    def low_onward():
        low_far.wait()
        s["low"] = send(low_all.at[me ^ 2], low_all.at[me ^ 2], mate)

    def g2_onward():
        g2_far.wait()
        s["g2"] = send(g2_all.at[me ^ 2], g2_all.at[me ^ 2], mate)

    def block_cols(b):
        return pl.ds(pl.multiple_of(block * b, 128), block)

    def up_slopes(turns):
        side = w_up[:, own_cols]
        for turn in turns:
            if turn == 1:
                low_near.wait()
            if turn == 3:
                s["low"].wait()
            hidden = mm(low_all[me ^ turn], side, 1, 0)
            slope[:, block_cols(me ^ turn)] = gelu_pair(hidden)[1]
        if 3 in turns:
            s["low_t"] = low_all[...].reshape(slot, width).T

    def up_hidden(turns):
        side = w_down[own_cols, :]
        for turn in turns:
            if turn == 1:
                g2_near.wait()
            if turn == 3:
                s["g2"].wait()
            cols = block_cols(me ^ turn)
            back = mm(g2_all[me ^ turn], side, 1, 1)
            gh[:, cols] = (slope[:, cols] * back).astype(BF16)

    def up_gradient(q):
        side = cat([gh[:, block * b + 256 * q : block * b + 256 * (q + 1)] for b in range(4)], 0)
        total = mm(s["low_t"], side, 1, 0).astype(BF16)
        for d in range(8):
            acc_up[q, position(UP_ORDERS[q], places(0, d))] = total[
                band_rows * d : band_rows * (d + 1)
            ]
        ups[q].start()

    def out_gradient():
        heads_sent.wait()
        s["gb"].wait()
        lead = cat([heads[...], heads_x[...]], 1)
        both = cat([gb[...], gb_x[...]], 0)
        for x in range(2):
            left_cols = both[:, 2 * head_width * x : 2 * head_width * x + head_width]
            right_cols = both[:, 2 * head_width * x + head_width : 2 * head_width * (x + 1)]
            total = mm(lead, jnp.where(core == 0, left_cols, right_cols), 1, 0).astype(BF16)
            for d in range(8):
                acc_out[position(OUT_ORDER, places(x, d))] = folded(total, d)
        outs.start()

    def share(part):
        own = gproj.at[head_width * part : head_width * (part + 1)]
        dst = pl.ds(pl.multiple_of(width * part + head_width * me, 64), head_width)
        for k in (2, 3, 1):
            lanes = pl.ds(pl.multiple_of(rows * (me ^ k), rows), rows)
            p_sent.append(send(own.at[:, lanes], gp_in.at[dst], (dp, me ^ k)))
        gp_in[dst] = own[:, mine]

    def values_back():
        s["tokens_t"] = everyone[...].reshape(slot, width).T
        for copy in s["g"]:
            copy.wait()
        grad = jnp.where(live, g_in[...].astype(F32), 0.0).astype(BF16)
        values = jnp.where(live, packed[2 * head_width :].astype(F32), 0.0).astype(BF16)
        f_high, f_low = halves(a1[...])
        t_high, t_low = halves(a3[...])
        g_weights = packs.diagonal(mm(f_high, grad, 1, 1) + mm(f_low, grad, 1, 1))
        s_high, s_low = halves(packs.times(marks[3], g_weights))
        g_values = mm(packs.block(s_high), t_high, 0, 0) + mm(packs.block(s_low), t_high, 0, 0)
        g_values = g_values + mm(packs.block(s_high), t_low, 0, 0)
        flip_rows = lax.broadcasted_iota(jnp.int32, (128, 128), 0)
        flip_cols = lax.broadcasted_iota(jnp.int32, (128, 128), 1)
        flip = (flip_rows + flip_cols == 127).astype(F32).astype(BF16)
        for h in range(nh):
            part = slice(DIM * h, DIM * (h + 1))
            g_wide = windows(grad[part])
            total = g_values[part] + unwindow(mm(g_wide, bands[1][h], 1, 1), DIM)
            gproj[2 * head_width + DIM * h : 2 * head_width + DIM * (h + 1)] = jnp.where(
                live, total, 0.0
            ).astype(BF16)
            turned = mm(g_wide[:, 128:256], flip, 1, 0).astype(BF16)
            gram = mm(turned, windows(values[part]), 0, 0)
            gram = pltpu.roll(gram, 384 - 127, 1, stride=1, stride_axis=0)
            found = pltpu.roll(jnp.sum(gram, axis=0, keepdims=True), 384 - 112, 1)
            at = lax.broadcasted_iota(jnp.int32, (1, 128), 1)
            lanes = pl.ds(pl.multiple_of(128 * me, 128), 128)
            sum_s[0, 4 + h : 5 + h, lanes] = jnp.where(at < TAPS, found[:, :128], 0.0)
        s.update(grad=grad, values=values, s_high=s_high, s_low=s_low)
        s["outer"] = packs.times(g_weights, marks[4])
        s["hold"] = jnp.zeros_like(s["outer"])
        share(2)

    def qkv_gradient(part):
        total = mm(s["tokens_t"], gproj[head_width * part : head_width * (part + 1)], 1, 1)
        total = total.astype(BF16)
        for d in range(8):
            acc_qkv[part, position(QKV_ORDERS[part], places(0, d))] = folded(total, d)
        projs[part].start()

    sums = [mate if name == "c" else bits[name][1] for name in SUM_ORDER]

    def sum_step(k):
        if k:
            s["sum"].wait()
            total = sum_s[k - 1] + sum_r[k - 1]
            if k == 5:
                ggain_v[...] = total[0:2]
                gshift_v[...] = total[2:4]
                for n in range(gtaps_v.shape[0]):
                    at = 128 * (n // nh)
                    row = 4 + n % nh
                    gtaps_v[n : n + 1] = total[row : row + 1, at : at + TAPS]
                stores.append(fetch(ggain_v, ggain_hbm))
                stores.append(fetch(gshift_v, gshift_hbm))
                stores.append(fetch(gtaps_v, gtaps_hbm))
                return
            sum_s[k] = total
        s["sum"] = copy_to(sum_s.at[k], sum_r.at[k], sems, sum_base + k, sums[k])
        s["sum"].start()

    def newton_back(steps):
        outer, hold = s["outer"], s["hold"]
        for step in steps:
            product, second, cube, inverse_t = [chain[step, i] for i in range(4)]
            blend = 0.25 * (13.0 * packs.unit - 15.0 * product + 7.0 * second - cube)
            inner = packs.times(inverse_t, outer)
            by_inner = packs.times(cat([product, second], 0), inner)
            zero_th, once, twice = inner, by_inner[:count], by_inner[count:]
            if step < NEWTON - 1:
                by_hold = packs.times(cat([product, second, cube], 0), hold)
                zero_th = zero_th + by_hold[:count]
                once = once + by_hold[count : 2 * count]
                twice = twice + by_hold[2 * count :]
            rest = packs.times(zero_th, 7.0 * product - second - 15.0 * packs.unit)
            rest = rest + packs.times(once, 7.0 * packs.unit - product) - twice
            pair = packs.times(cat([outer, hold], 0), blend)
            outer, hold = pair[:count], pair[count:] + 0.25 * rest
        s["outer"], s["hold"] = outer, hold

    def tall_marks(high, low, wide):
        both = mm(cat([high, low], 0), wide, 1, 1)
        return packs.diagonal(both[:head_width] + both[head_width:]) * scale

    def softmax_back():
        first = a1[...]
        w_high, w_low = halves(marks[5])
        g_tall = mm(packs.block(w_high), s["grad"], 0, 0) + mm(packs.block(w_low), s["grad"], 0, 0)
        along = jnp.sum(per_head(g_tall * first), axis=1, keepdims=True)
        g_one = first * (per_head(g_tall) - along).reshape(head_width, slot)
        s["one"], one_low = halves(g_one)
        s["g_k"] = tall_marks(s["one"], one_low, packed[:head_width])

    def places_back():
        third = a3[...]
        g_tall = mm(cat([packs.block(s["s_high"]), packs.block(s["s_low"])], 0), s["values"], 1, 0)
        g_tall = g_tall[:head_width] + g_tall[head_width:]
        g_three = third * (g_tall - jnp.sum(g_tall * third, axis=1, keepdims=True))
        s["three"], three_low = halves(g_three)
        s["g_q"] = tall_marks(s["three"], three_low, packed[head_width : 2 * head_width])

    def middle_back():
        q_marks, k_marks, middle = marks[0], marks[1], marks[2]
        outer, hold = s["outer"], s["hold"]
        inverse_t = chain[0, 3]
        col_sums = jnp.sum(middle, axis=0, keepdims=True)
        row_sums = packs.row_sum(middle)
        col_top = packs.row_max(col_sums)
        row_top = jnp.max(row_sums, axis=0, keepdims=True)
        norm = 1.0 / (col_top * row_top)
        g_start_t = packs.turn(outer) + packs.times(packs.turn(hold), middle)
        g_norm = -packs.row_sum(jnp.sum(g_start_t * inverse_t, axis=0, keepdims=True)) * norm
        col_hit = (col_sums == col_top).astype(F32)
        row_hit = (row_sums == row_top).astype(F32)
        col_hit = col_hit / packs.row_sum(col_hit)
        row_hit = row_hit / jnp.sum(row_hit, axis=0, keepdims=True)
        g_middle = packs.times(hold, inverse_t) + g_start_t * norm
        g_middle = g_middle + g_norm * (row_top * col_hit + col_top * row_hit)
        g_two_s = middle * (g_middle - packs.row_sum(g_middle * middle))
        g_q_marks = s["g_q"] + packs.times(g_two_s, k_marks)
        g_k_marks = s["g_k"] + packs.times(packs.turn(g_two_s), q_marks)
        for part, other, g_own, high in (
            (0, k_marks, g_q_marks, s["one"]),
            (1, q_marks, g_k_marks, s["three"]),
        ):
            m_high, m_low = halves(other)
            l_high, l_low = halves(g_own * share_of)
            total = mm(packs.block(m_high), high, 0, 0) + mm(packs.block(m_low), high, 0, 0)
            total = total + mm(cat([l_high, l_low], 0), cat([member, member], 0), 0, 0)
            gproj[head_width * part : head_width * (part + 1)] = (total * scale).astype(BF16)
            share(part)

    def input_gradient():
        wqkv = w_qkv[...]
        for copy in p_sent:
            copy.wait()
        in_v[...] = (gr1_ref[...] + mm(gp_in[...], wqkv, 0, 1)).astype(BF16)
        stores.append(fetch(in_v, in_hbm))

    def finish_down(q):
        gdown_v[64 * q : 64 * (q + 1)] = downs[q].finish()
        s["downs"] = s.get("downs", 0) + 1
        if s["downs"] == 3:
            stores.append(fetch(gdown_v, gdown_hbm))

    def finish_up(q):
        gup_v[:, 256 * q : 256 * (q + 1)] = ups[q].finish()
        s["ups"] = s.get("ups", 0) + 1
        if s["ups"] == 3:
            stores.append(fetch(gup_v, gup_hbm))

    def finish_out():
        total = outs.finish()
        gout_v[:band_half] = total[:, :head_width]
        gout_v[band_half:] = total[:, head_width:]
        stores.append(fetch(gout_v, gout_hbm))

    def finish_proj(part):
        total = projs[part].finish()
        goal = quarters * part + me
        dest, where = lax.div(goal, 3), lax.rem(goal, 3)

        @pl.when(dest == me)
        def _():
            slots[where] = total

        @pl.when(dest != me)
        def _():
            fin[part] = total
            pltpu.make_async_remote_copy(
                src_ref=fin.at[part], dst_ref=slots.at[where],
                send_sem=sems.at[0, last + part], recv_sem=sems.at[1, last + where],
                device_id=(dp, dest), device_id_type=MESH,
            ).start()

    def collect():
        for index in range(3):
            goal = quarters * index + me
            source = lax.rem(3 * me + index, quarters)

            @pl.when(lax.div(goal, 3) != me)
            def _():
                copy_to(fin.at[index], slots.at[0], sems, last + index, mate).wait_send()

            @pl.when(source != me)
            def _():
                copy_to(fin.at[0], slots.at[index], sems, last + index, mate).wait_recv()

        for index in range(3):
            got = slots[index]
            cols = slice(head_width * index, head_width * (index + 1))
            gqkv_v[:band_half, cols] = got[:, :head_width]
            gqkv_v[band_half:, cols] = got[:, head_width:]
        stores.append(fetch(gqkv_v, gqkv_hbm))

    table = {
        "DG": down_gradient, "FB": branch_back,
        "HB0": lambda: hidden_back((0,)), "HB1": lambda: hidden_back((1, 2, 3)),
        "HB2": lambda: hidden_back((0, 1)), "HB3": lambda: hidden_back((2, 3)),
        "OG": out_gradient, "AV": values_back,
        "SM": softmax_back, "MM": middle_back, "IN": input_gradient, "GQ": collect,
        "LF": low_onward, "GF": g2_onward,
        "UH0": lambda: up_slopes((1,)), "UH1": lambda: up_slopes((2, 3)),
        "UGA": lambda: up_hidden((1,)), "UGB": lambda: up_hidden((2, 3)),
        "SN": places_back,
        "NB1": lambda: newton_back((5, 4, 3)), "NB2": lambda: newton_back((2, 1, 0)),
    }
    for q in range(3):
        table["UG%d" % q] = lambda q=q: up_gradient(q)
        table["QG%d" % q] = lambda q=q: qkv_gradient(q)
    for k in range(6):
        table["S%d" % k] = lambda k=k: sum_step(k)
    names = {"O": (outs, finish_out)}
    for q in range(3):
        names["D%d" % q] = (downs[q], lambda q=q: finish_down(q))
        names["U%d" % q] = (ups[q], lambda q=q: finish_up(q))
        names["P%d" % q] = (projs[q], lambda q=q: finish_proj(q))
    for item in SCHEDULE:
        if item in table:
            table[item]()
        else:
            chunk, finish = names[item]
            if chunk.stage == len(chunk.bits) - 1:
                finish()
            else:
                chunk.step()
    for copy in stores:
        copy.wait()


def final_kernel(*refs):
    sem = refs[-1]
    count = (len(refs) - 1) // 3
    inward = [
        pltpu.make_async_copy(refs[i], refs[2 * count + i], sem.at[0, i]) for i in range(count)
    ]
    outward = [
        pltpu.make_async_copy(refs[2 * count + i], refs[count + i], sem.at[1, i])
        for i in range(count)
    ]
    for copy in inward:
        copy.start()
    for got, put in zip(inward, outward):
        got.wait()
        put.start()
    for copy in outward:
        copy.wait()


def per_device_fast(
    tokens, w_qkv, w_out, w_up, w_down, norm_gains, norm_shifts, conv_kernels, seq_lengths,
    seg_bounds, out_grad,
):
    rows, width = tokens.shape
    ff = w_up.shape[1]
    head_width = width // 4
    slot = 4 * rows
    band, down_cols = width // 8, ff // 8
    whole = pl.BlockSpec(memory_space=VMEM)
    anywhere = pl.BlockSpec(memory_space=pl.ANY)
    shape = jax.ShapeDtypeStruct
    outs = (
        shape((rows, width), BF16),
        shape((rows, width), BF16),
        shape((band, w_qkv.shape[1] // 4), F32),
        shape((band, width // 4), F32),
        shape((band, ff // 4), F32),
        shape((width // 4, down_cols), F32),
        shape(norm_gains.shape, F32),
        shape(norm_shifts.shape, F32),
        shape(conv_kernels.shape, F32),
    )
    found = pl.pallas_call(
        main_kernel,
        out_shape=outs,
        in_specs=[anywhere] * 6
        + [whole] * 3
        + [pl.BlockSpec(memory_space=pltpu.SMEM), whole],
        out_specs=[anywhere] * 9,
        scratch_shapes=[
            VMEM((rows, width), BF16), VMEM((rows, width), BF16),
            VMEM(w_qkv.shape, BF16), VMEM(w_out.shape, BF16),
            VMEM(w_up.shape, BF16), VMEM(w_down.shape, BF16),
            pltpu.SemaphoreType.DMA((32,)), pltpu.SemaphoreType.DMA((2, 120)),
            VMEM((4, rows, width), BF16),
            VMEM((3, 256, width), BF16),
            VMEM((2, conv_kernels.shape[0], 384), F32),
            VMEM((3 * head_width, slot), BF16),
            VMEM((head_width, slot), F32), VMEM((head_width, slot), F32),
            VMEM((NEWTON, 4, DIM, head_width), F32),
            VMEM((6, DIM, head_width), F32),
            VMEM((head_width, slot), BF16),
            VMEM((width, rows), BF16), VMEM((width, rows), BF16),
            VMEM((4, rows, width), BF16), VMEM((4, rows, width), BF16),
            VMEM((2 * rows, ff), BF16),
            VMEM((width, rows), BF16), VMEM((width, rows), BF16),
            VMEM((rows, ff), F32),
            VMEM((rows, ff), BF16),
            VMEM((rows, width), BF16), VMEM((rows, width), BF16),
            VMEM((width, rows), BF16),
            VMEM((head_width, slot), BF16),
            VMEM((3 * head_width, slot), BF16),
            VMEM((3 * width, rows), BF16),
            VMEM((rows, width), F32), VMEM((rows, width), F32), VMEM((rows, width), F32),
            VMEM((5, 8, width), F32), VMEM((5, 8, width), F32),
            VMEM((3, band // 2, 2 * head_width), F32),
            VMEM((3, band // 2, 2 * head_width), F32),
            VMEM((3, 16, 64, down_cols), BF16), VMEM((3, 15, 64, down_cols), BF16),
            VMEM((3, 8, band, 256), BF16), VMEM((3, 7, band, 256), BF16),
            VMEM((16, band // 2, 2 * head_width), BF16),
            VMEM((15, band // 2, 2 * head_width), BF16),
            VMEM((3, 8, band // 2, 2 * head_width), BF16),
            VMEM((3, 7, band // 2, 2 * head_width), BF16),
        ]
        + [VMEM(out.shape, out.dtype) for out in outs],
        compiler_params=pltpu.CompilerParams(
            collective_id=0, has_side_effects=True, vmem_limit_bytes=63 * 2**20
        ),
        name="main_kernel",
    )(
        tokens, out_grad, w_qkv, w_out, w_up, w_down, norm_gains, norm_shifts, conv_kernels,
        seq_lengths, seg_bounds,
    )
    copied = pl.pallas_call(
        final_kernel,
        out_shape=outs,
        in_specs=[anywhere] * 9,
        out_specs=[anywhere] * 9,
        scratch_shapes=[VMEM(out.shape, out.dtype) for out in outs]
        + [pltpu.SemaphoreType.DMA((2, 9))],
        name="final_kernel",
    )(*found)
    copied = tuple(copied)
    return copied[:5] + (copied[5].T,) + copied[6:]


highest = lax.Precision.HIGHEST
epsilon = 1e-05


def layer_norm(values, gain, shift):
    center = jnp.mean(values, axis=-1, keepdims=True)
    centred = values - center
    spread_sq = jnp.mean(centred * centred, axis=-1, keepdims=True)
    return centred * lax.rsqrt(spread_sq + epsilon) * gain + shift


def exact_gelu(values):
    return jax.nn.gelu(values, approximate=False)


def shifted_conv(values, kernel):
    slot_len = values.shape[0]
    taps = kernel.shape[0]
    half_width = taps // 2
    padded = jnp.pad(values, ((half_width, half_width), (0, 0)))
    total = jnp.zeros_like(values)
    for offset in range(taps):
        total = total + kernel[offset] * padded[offset : offset + slot_len]
    return total


def nystrom_head(queries, keys, values, kernel, length, bounds):
    slot_len = queries.shape[0]
    mark_count = bounds.shape[0] - 1
    head_dim = queries.shape[1]
    places = jnp.arange(slot_len, dtype=jnp.int32)
    valid = places < length
    weight_mask = valid.astype(jnp.float32)[:, None]
    scaling = head_dim ** (-0.25)
    queries = queries * weight_mask * scaling
    keys = keys * weight_mask * scaling
    values = values * weight_mask
    member = ((places[None, :] >= bounds[:-1, None]) & (places[None, :] < bounds[1:, None])).astype(
        jnp.float32
    )
    counts = (bounds[1:] - bounds[:-1]).astype(jnp.float32)[:, None]
    query_marks = jnp.dot(member, queries, precision=highest) / counts
    key_marks = jnp.dot(member, keys, precision=highest) / counts
    first = jax.nn.softmax(jnp.dot(queries, key_marks.T, precision=highest), axis=-1)
    middle = jax.nn.softmax(jnp.dot(query_marks, key_marks.T, precision=highest), axis=-1)
    third_scores = jnp.dot(query_marks, keys.T, precision=highest)
    third = jax.nn.softmax(jnp.where(valid[None, :], third_scores, -1000000000.0), axis=-1)
    inverse = middle.T / (jnp.max(jnp.sum(middle, axis=0)) * jnp.max(jnp.sum(middle, axis=1)))
    identity = jnp.eye(mark_count, dtype=jnp.float32)
    for _ in range(NEWTON):
        product = jnp.dot(middle, inverse, precision=highest)
        inner = 7.0 * identity - product
        inner = 15.0 * identity - jnp.dot(product, inner, precision=highest)
        inner = 13.0 * identity - jnp.dot(product, inner, precision=highest)
        inverse = 0.25 * jnp.dot(inverse, inner, precision=highest)
    summary = jnp.dot(third, values, precision=highest)
    mixed = jnp.dot(first, jnp.dot(inverse, summary, precision=highest), precision=highest)
    return (mixed + shifted_conv(values, kernel)) * weight_mask


def attend(packed, kernels, lengths, bounds):
    seq_count = lengths.shape[0]
    head_count = kernels.shape[0]
    head_dim = packed.shape[-1] // (3 * head_count)
    grouped = packed.reshape(seq_count, -1, 3, head_count, head_dim)
    over_heads = jax.vmap(nystrom_head, in_axes=(1, 1, 1, 0, None, None), out_axes=1)
    over_seqs = jax.vmap(over_heads, in_axes=(0, 0, 0, None, 0, 0))
    result = over_seqs(
        grouped[:, :, 0], grouped[:, :, 1], grouped[:, :, 2], kernels, lengths, bounds
    )
    return result.reshape(seq_count * grouped.shape[1], head_count * head_dim)


def row_contract(left, right):
    return lax.dot_general(
        left, right, (((0,), (0,)), ((), ())), preferred_element_type=jnp.float32
    )


def to_blocks(matrix, dp_count, quarters):
    total_rows, total_cols = matrix.shape
    shaped = matrix.reshape(dp_count, total_rows // dp_count, quarters, total_cols // quarters)
    return shaped.transpose(0, 2, 1, 3).reshape(total_rows * quarters, total_cols // quarters)


def per_device(
    tokens,
    w_qkv,
    w_out,
    w_up,
    w_down,
    norm_gains,
    norm_shifts,
    conv_kernels,
    seq_lengths,
    seg_bounds,
    out_grad,
):
    quarters = lax.axis_size("head")
    quarter = lax.axis_index("head")
    dp_count = lax.axis_size("dp")
    tok_rows, width = tokens.shape
    seq_count = seq_lengths.shape[0]
    group_rows = tok_rows * quarters
    slot_len = group_rows // seq_count
    head_count, kernel_len = conv_kernels.shape
    local_heads = head_count // quarters
    head_width = w_qkv.shape[1] // (3 * quarters)
    places = quarter * tok_rows + jnp.arange(tok_rows, dtype=jnp.int32)
    owners = places // slot_len
    within = places % slot_len
    limits = jnp.sum(
        jnp.where(
            owners[:, None] == jnp.arange(seq_count, dtype=jnp.int32)[None, :],
            seq_lengths[None, :],
            0,
        ),
        axis=1,
    )
    live = (within < limits).astype(jnp.float32)[:, None]
    local_kernels = lax.dynamic_slice_in_dim(
        conv_kernels.astype(jnp.float32), quarter * local_heads, local_heads, 0
    )
    projected = jnp.dot(tokens, w_qkv, preferred_element_type=jnp.float32).astype(jnp.bfloat16)
    packed = lax.all_to_all(
        projected.reshape(tok_rows, 3, quarters, head_width),
        "head",
        split_axis=2,
        concat_axis=0,
        tiled=True,
    )
    packed_rows = packed.reshape(group_rows, 3 * head_width)

    def attention_piece(packed_in, kernel_in):
        return attend(packed_in, kernel_in, seq_lengths, seg_bounds)

    attended, attention_back = jax.vjp(
        attention_piece, packed_rows.astype(jnp.float32), local_kernels
    )
    attended_low = attended.astype(jnp.bfloat16)
    heads_rows = lax.all_to_all(
        attended_low.reshape(group_rows, 1, head_width),
        "head",
        split_axis=0,
        concat_axis=1,
        tiled=True,
    ).reshape(tok_rows, width)
    branch = jnp.dot(heads_rows, w_out, preferred_element_type=jnp.float32)
    first_in = tokens.astype(jnp.float32) + branch
    first_norm, first_back = jax.vjp(layer_norm, first_in, norm_gains[0], norm_shifts[0])
    first_low = first_norm.astype(jnp.bfloat16)
    hidden = jnp.dot(first_low, w_up, preferred_element_type=jnp.float32)
    activated, gelu_back = jax.vjp(exact_gelu, hidden)
    act_low = activated.astype(jnp.bfloat16)
    second = jnp.dot(act_low, w_down, preferred_element_type=jnp.float32)
    output, second_back = jax.vjp(layer_norm, first_norm + second, norm_gains[1], norm_shifts[1])
    cotangent = out_grad.astype(jnp.float32) * live
    grad_second_in, grad_gain_two, grad_shift_two = second_back(cotangent)
    grad_second = grad_second_in.astype(jnp.bfloat16)
    grad_down = row_contract(act_low, grad_second)
    grad_act = jnp.dot(grad_second, w_down.T, preferred_element_type=jnp.float32)
    grad_hidden = gelu_back(grad_act)[0].astype(jnp.bfloat16)
    grad_up = row_contract(first_low, grad_hidden)
    grad_first = grad_second_in + jnp.dot(grad_hidden, w_up.T, preferred_element_type=jnp.float32)
    grad_first_in, grad_gain_one, grad_shift_one = first_back(grad_first)
    grad_branch = grad_first_in.astype(jnp.bfloat16)
    grad_wout = row_contract(heads_rows, grad_branch)
    grad_heads = jnp.dot(grad_branch, w_out.T, preferred_element_type=jnp.float32).astype(
        jnp.bfloat16
    )
    heads_grad = lax.all_to_all(
        grad_heads.reshape(tok_rows, quarters, head_width),
        "head",
        split_axis=1,
        concat_axis=0,
        tiled=True,
    ).reshape(group_rows, head_width)
    grad_packed, grad_local_kernels = attention_back(heads_grad.astype(jnp.float32))
    grad_packed_low = grad_packed.astype(jnp.bfloat16).reshape(group_rows, 3, 1, head_width)
    grad_projected = lax.all_to_all(
        grad_packed_low, "head", split_axis=0, concat_axis=2, tiled=True
    ).reshape(tok_rows, 3 * quarters * head_width)
    grad_wqkv = row_contract(tokens, grad_projected)
    input_grad = (
        grad_first_in + jnp.dot(grad_projected, w_qkv.T, preferred_element_type=jnp.float32)
    ).astype(jnp.bfloat16)
    kernel_full = lax.dynamic_update_slice_in_dim(
        jnp.zeros((head_count, kernel_len), jnp.float32),
        grad_local_kernels,
        quarter * local_heads,
        0,
    )
    small_sums = lax.psum(
        (
            jnp.stack([grad_gain_one, grad_gain_two]),
            jnp.stack([grad_shift_one, grad_shift_two]),
            kernel_full,
        ),
        ("dp", "head"),
    )
    blocked_qkv = to_blocks(grad_wqkv, dp_count, quarters)
    blocked_out = to_blocks(grad_wout, dp_count, quarters)
    blocked_up = to_blocks(grad_up, dp_count, quarters)
    blocked_down = to_blocks(grad_down, dp_count, quarters)
    weight_sums = (
        lax.psum_scatter(blocked_qkv, ("dp", "head"), scatter_dimension=0, tiled=True),
        lax.psum_scatter(blocked_out, ("dp", "head"), scatter_dimension=0, tiled=True),
        lax.psum_scatter(blocked_up, ("dp", "head"), scatter_dimension=0, tiled=True),
        lax.psum_scatter(blocked_down, ("dp", "head"), scatter_dimension=0, tiled=True),
    )
    return (
        output.astype(jnp.bfloat16),
        input_grad,
        weight_sums[0],
        weight_sums[1],
        weight_sums[2],
        weight_sums[3],
        small_sums[0],
        small_sums[1],
        small_sums[2],
    )


def solution(mesh):
    placed = (
        P(("dp", "head"), None),
        P(),
        P(),
        P(),
        P(),
        P(),
        P(),
        P(),
        P("dp"),
        P("dp", None),
        P(("dp", "head"), None),
    )
    aligned = mesh.shape["dp"] == 8 and mesh.shape["head"] == 4
    return jax.shard_map(
        per_device_fast if aligned else per_device,
        mesh=mesh,
        in_specs=placed,
        out_specs=(
            P(("dp", "head"), None),
            P(("dp", "head"), None),
            P("dp", "head"),
            P("dp", "head"),
            P("dp", "head"),
            P("dp", "head"),
            P(),
            P(),
            P(),
        ),
        check_vma=False,
    )
```
